32 devices in a mesh: items: 8 (over z, x), pipe: 4 (over y, core).
Axes of the slice: x: 2, y: 2, z: 4, core: 2. Of those that a mesh axis runs over, the one named last changes fastest.
Arguments:
- text_in: bfloat16 [32, 2, 364, 768], P(('items', 'pipe')), may hold values from -6 to 6
- memory: bfloat16 [10, 768], P(None, 'pipe'), may hold values from -6 to 6
- w_qkv: bfloat16 [1536, 2304], P('pipe'), may hold values from -0.21875 to 0.21875
- w_o: bfloat16 [1536, 768], P('pipe'), may hold values from -0.875 to 0.875
- w_in: bfloat16 [1536, 3072], P('pipe'), may hold values from -0.21875 to 0.21875
- w_out: bfloat16 [6144, 768], P('pipe'), may hold values from -0.109375 to 0.109375
- gains: bfloat16 [3072], P('pipe'), may hold values from 0.5 to 1.5
- biases: bfloat16 [15360], P('pipe'), may hold values from -1.5 to 1.5
- counts: int32 [32], P('items'), may hold values from 1 to 2, as said below
- last_lengths: int32 [32], P('items'), may hold values from 91 to 364, as said below
- text_cot: bfloat16 [32, 2, 364, 768], P(('items', 'pipe')), may hold values from -6 to 6
- memory_cot: bfloat16 [32, 10, 768], P(('items', 'pipe')), may hold values from -6 to 6
Outputs:
- final_text: float32 [32, 2, 364, 768], P(('items', 'pipe'))
- final_memory: float32 [32, 10, 768], P(('items', 'pipe'))
- text_grad: float32 [32, 2, 364, 768], P(('items', 'pipe'))
- memory_grad: float32 [10, 768], P(None, 'pipe')
- qkv_grad: float32 [1536, 2304], P('pipe')
- out_proj_grad: float32 [1536, 768], P('pipe')
- up_grad: float32 [1536, 3072], P('pipe')
- down_grad: float32 [6144, 768], P('pipe')
- gains_grad: float32 [3072], P('pipe')
- biases_grad: float32 [15360], P('pipe')
The draws below stay inside these ranges and needn't reach their ends.
Inputs may be any that keep to these rules, and one draw needn't show every extreme that they name: `counts`: some item has 2 segments and some has 1. `last_lengths`: some item reaches each end.
All inputs are finite; a program needn't handle non-finite values.
Results may differ from the reference program's by a relative error of at most 0.02.
Values may be sent and summed in bfloat16 or wider, within the bound.
A program may use at most 256 MiB of HBM per device.

```python
import jax
import jax.numpy as jnp
from jax import lax

D = 768
HEADS = 12
HEAD_DIM = 64
FF = 3072
MEM = 10
TEXT = 364
MAXSEG = 2
SEG = 384
ITEMS = 32


def draw_counts(key, part):
    key = jax.random.fold_in(key, 11)
    values = jax.random.randint(jax.random.fold_in(key, 1), (ITEMS,), 1, MAXSEG + 1)
    place = jax.random.randint(jax.random.fold_in(key, 2), (), 0, ITEMS)
    values = values.at[place].set(MAXSEG)
    values = values.at[(place + ITEMS // 2 + 1) % ITEMS].set(1)
    return values.astype(jnp.int32)


def draw_last_lengths(key, part):
    key = jax.random.fold_in(key, 23)
    values = jax.random.randint(jax.random.fold_in(key, 1), (ITEMS,), TEXT // 4, TEXT + 1)
    place = jax.random.randint(jax.random.fold_in(key, 2), (), 0, ITEMS)
    values = values.at[place].set(TEXT)
    values = values.at[(place + ITEMS // 2 + 1) % ITEMS].set(TEXT // 4)
    return values.astype(jnp.int32)


def levels(key, shape, cuts, smallest, top_value):
    loudness = 1.0
    for axis_at, shards_of in cuts:
        steps = jax.random.uniform(jax.random.fold_in(jax.random.fold_in(key, 6), axis_at), (shards_of,), jnp.float32, smallest / len(cuts), top_value / len(cuts))
        loudness = loudness * jnp.repeat(jnp.exp(steps), shape[axis_at] // shards_of).reshape((-1,) + (1,) * (len(shape) - 1 - axis_at))
    return loudness


def noise(rng, extent, deviation, bound, shards=(), held_as=jnp.bfloat16):
    entries = jax.random.normal(rng, extent, jnp.float32) * deviation
    if len(shards) > 0:
        entries = levels(rng, extent, shards, -0.22, 0.18) * entries
    return jnp.clip(entries, min=-bound, max=bound).astype(held_as)


def setup_inputs(seed: int = 0) -> dict:
    splits = jax.random.split(jax.random.key(seed), 13)
    text_in = noise(splits[0], (ITEMS, MAXSEG, TEXT, D), 1.0, 6.0, ((0, 32),))
    memory = noise(splits[1], (MEM, D), 1.0, 6.0, ((1, 4),))
    w_qkv = noise(splits[2], (2 * D, 3 * D), D ** -0.5, 0.21875, ((0, 4),))
    w_o = noise(splits[3], (2 * D, D), (D // 16) ** -0.5, 0.875, ((0, 4),))
    w_in = noise(splits[4], (2 * D, FF), D ** -0.5, 0.21875, ((0, 4),))
    w_out = noise(splits[5], (2 * FF, D), FF ** -0.5, 0.109375, ((0, 4),))
    gains = jnp.clip(1.0 + 0.1 * jax.random.normal(splits[6], (4 * D,), jnp.float32), 0.5, 1.5).astype(jnp.bfloat16)
    biases = noise(splits[7], (2 * (6 * D + FF),), 0.3, 1.5, ((0, 4),))
    counts = draw_counts(jax.random.fold_in(splits[12], 71), 0)
    last_lengths = draw_last_lengths(jax.random.fold_in(splits[12], 71), 0)
    text_cot = noise(splits[10], (ITEMS, MAXSEG, TEXT, D), 1.0, 6.0, ((0, 32),))
    memory_cot = noise(splits[11], (ITEMS, MEM, D), 1.0, 6.0, ((0, 32),))
    return {"text_in": text_in, "memory": memory, "w_qkv": w_qkv, "w_o": w_o, "w_in": w_in, "w_out": w_out, "gains": gains, "biases": biases, "counts": counts, "last_lengths": last_lengths, "text_cot": text_cot, "memory_cot": memory_cot}


@jax.custom_vjp
def low(v):
    return lax.optimization_barrier(v.astype(jnp.bfloat16)).astype(jnp.float32)

@jax.custom_vjp
def low_back(v):
    return v

def low_keep(v):
    return (low(v), None)

def low_pass(kept, grad):
    return (grad,)

def back_keep(v):
    return (v, None)

def back_low(kept, grad):
    return (low(grad),)
low.defvjp(low_keep, low_pass)
low_back.defvjp(back_keep, back_low)
highest = lax.Precision.HIGHEST
epsilon = 1e-06

def matmul(left, right):
    return jnp.dot(left, right, precision=highest)

def layer_norm(values, gain, shift):
    centre = values - lax.optimization_barrier(jnp.mean(values, axis=-1, keepdims=True))
    inverse = lax.rsqrt(lax.optimization_barrier(jnp.mean(centre * centre, axis=-1, keepdims=True)) + epsilon)
    return centre * inverse * gain + shift

def layer(weights, section, inputs, keymask):
    w_qkv, w_o, w_in, w_out, gains, biases = weights
    wide = w_qkv[section * D:(section + 1) * D]
    out_proj = w_o[section * D:(section + 1) * D]
    up_proj = w_in[section * D:(section + 1) * D]
    down_proj = w_out[section * FF:(section + 1) * FF]
    gain_one = gains[2 * section * D:(2 * section + 1) * D]
    gain_two = gains[(2 * section + 1) * D:(2 * section + 2) * D]
    base = section * (6 * D + FF)
    pieces = [biases[base + index * D:base + (index + 1) * D] for index in range(6)]
    query_bias, value_bias, out_bias, shift_one, down_bias, shift_two = pieces
    up_bias = biases[base + 6 * D:base + 6 * D + FF]
    mixed = matmul(inputs, wide)
    query = low_back(low(mixed[:, :D] + query_bias)).reshape(SEG, HEADS, HEAD_DIM)
    keyed = low_back(low(mixed[:, D:2 * D])).reshape(SEG, HEADS, HEAD_DIM)
    values = low_back(low(mixed[:, 2 * D:] + value_bias)).reshape(SEG, HEADS, HEAD_DIM)
    scores = jnp.einsum('qhd,khd->hqk', query, keyed, precision=highest) * HEAD_DIM ** (-0.5)
    scores = low_back(jnp.where(keymask[None, None, :], scores, -1000000000.0))
    probs = low(jax.nn.softmax(scores, axis=-1))
    context = jnp.einsum('hqk,khd->qhd', probs, values, precision=highest).reshape(SEG, D)
    context = low_back(low(context))
    branch = low_back(matmul(context, out_proj) + out_bias)
    hidden = layer_norm(inputs + branch, gain_one, shift_one)
    upward = low_back(matmul(low(hidden), up_proj) + up_bias)
    active = low(jax.nn.gelu(upward, approximate=False))
    down = low_back(matmul(active, down_proj) + down_bias)
    return layer_norm(hidden + down, gain_two, shift_two)

def item_run(weights, memory, text, count, last_len):
    state = memory
    rows = jnp.arange(SEG)
    columns = jnp.arange(TEXT)
    outputs = []
    for segment in range(MAXSEG):
        length = jnp.where(segment < count - 1, TEXT, last_len)
        keymask = (rows < MEM) | (rows >= MEM + TEXT) | (rows - MEM < length)
        inputs = low_back(jnp.concatenate([state, text[segment], state], axis=0))
        middle = low_back(low(layer(weights, 0, inputs, keymask)))
        top = low(layer(weights, 1, middle, keymask))
        live = segment < count
        shown = (columns < length) & live
        outputs.append(jnp.where(shown[:, None], top[MEM:MEM + TEXT], jnp.zeros_like(top[MEM:MEM + TEXT])))
        state = jnp.where(live, top[MEM + TEXT:], state)
    return (jnp.stack(outputs), state)

def reference(text_in, memory, w_qkv, w_o, w_in, w_out, gains, biases, counts, last_lengths, text_cot, memory_cot):
    weights = tuple((part.astype(jnp.float32) for part in (w_qkv, w_o, w_in, w_out, gains, biases)))
    start_memory = memory.astype(jnp.float32)

    def one_item(totals, item):
        text, count, last_len, text_cotangent, memory_cotangent = item

        def run(weight_set, memory_value, text_value):
            return item_run(weight_set, memory_value, text_value, count, last_len)
        (shown, state), pull = jax.vjp(run, weights, start_memory, text.astype(jnp.float32))
        grad_weights, grad_memory, grad_text = pull((text_cotangent.astype(jnp.float32), memory_cotangent.astype(jnp.float32)))
        summed = tuple((total + grad for total, grad in zip(totals[0], grad_weights)))
        return ((summed, totals[1] + grad_memory), (shown, state, grad_text))
    start = (tuple((jnp.zeros_like(part) for part in weights)), jnp.zeros_like(start_memory))
    (grad_weights, grad_memory), (shown, state, grad_text) = lax.scan(one_item, start, (text_in, counts, last_lengths, text_cot, memory_cot))
    return (shown, state, grad_text, grad_memory, grad_weights[0], grad_weights[1], grad_weights[2], grad_weights[3], grad_weights[4], grad_weights[5])
```

```python
import functools

import jax
import jax.numpy as jnp
from jax import lax
from jax.experimental import pallas as pl
from jax.experimental.pallas import tpu as pltpu
from jax.sharding import PartitionSpec as P

D = 768
FF = 3072
MEM = 10
TEXT = 364
SEG = 384
PAIRS = 6
LANE = 128
TAIL = 32
UNITS = 4
LOG2E = 1.4426950408889634
MASKED = -1.0e9
EPS = 1e-6
MESH = pl.DeviceIdType.MESH
BF = jnp.bfloat16
F32 = jnp.float32
G1, BQ, BV, BO, N1, BD, G2, N2, BI = 0, 1, 2, 3, 4, 5, 8, 9, 10
BLOCKS = [slice(128 * b, 128 * b + 128) for b in range(3)]


def nn(left, right):
    return jnp.dot(left, right, preferred_element_type=F32)


def nt(left, right):
    return lax.dot_general(left, right, (((1,), (1,)), ((), ())), preferred_element_type=F32)


def tn(left, right):
    return lax.dot_general(left, right, (((0,), (0,)), ((), ())), preferred_element_type=F32)


def gelu_parts(up):
    t = pl.reciprocal(1.0 + (0.3275911 * 0.7071067811865476) * jnp.abs(up), approx=True)
    poly = t * (
        0.127414796
        + t * (-0.142248368 + t * (0.7107068705 + t * (-0.7265760135 + t * 0.5307027145)))
    )
    bell = jnp.exp2(up * up * (-0.5 * LOG2E))
    half = poly * bell
    phi = jnp.where(up >= 0, 1.0 - half, half)
    return up * phi, phi + up * bell * 0.3989422804014327


def norm_parts(values):
    centre = values - jnp.mean(values, axis=-1, keepdims=True)
    inverse = lax.rsqrt(jnp.mean(centre * centre, axis=-1, keepdims=True) + EPS)
    return centre * inverse, inverse


def norm_back(grad, normed, inverse, gain):
    scaled = grad * gain
    middle = jnp.mean(scaled, axis=-1, keepdims=True)
    along = jnp.mean(scaled * normed, axis=-1, keepdims=True)
    return inverse * (scaled - middle - normed * along)


def row_sum(values):
    return jnp.sum(values, axis=0, keepdims=True)


def split_stack(dst, src):
    low = lax.broadcasted_iota(jnp.int32, (SEG, LANE), 1) < 64
    zero = jnp.zeros((SEG, LANE), BF)
    dst[:SEG, :LANE] = jnp.where(low, src, zero)
    dst[SEG:, :LANE] = jnp.where(low, zero, src)


def tail_matrix(spread):
    row = lax.broadcasted_iota(jnp.int32, (TAIL, TAIL), 0)
    col = lax.broadcasted_iota(jnp.int32, (TAIL, TAIL), 1)
    if spread:
        keep = ((row >= 22) & (col == row)) | ((row >= 12) & (row < 22) & (col == row + 10))
    else:
        keep = (row >= 22) & ((col == row) | (col == row - 10))
    return jnp.where(keep, 1.0, 0.0).astype(BF)


def relay_kernel(
    x_own,
    c_own,
    mem0,
    mc_own,
    flags,
    kmask,
    w_qkv,
    w_o,
    w_in,
    w_out,
    vec_own,
    xs,
    ctxs,
    hids,
    acts,
    tops,
    gds,
    gus,
    gbs,
    gps,
    backs,
    vecg,
    wq,
    wo,
    wi,
    wd,
    vec,
    xin,
    gsl,
    mcs,
    trx,
    packed,
    st,
    n1s,
    n2s,
    dgs,
    ctx,
    sc,
    sd,
    big,
    stk,
    stv,
    rhs,
    hid,
    outb,
    gdb,
    delta,
    w_local,
    w_send,
    w_recv,
    e_local,
    e_send,
    e_recv,
    mid_send,
    mid_recv,
    tail_send,
    tail_recv,
    grad_send,
    grad_recv,
    x_sem,
    ctx_sem,
    gu_sem,
    gp_sem,
    hid_sem,
    act_sem,
    gd_sem,
    out_sem,
):
    place = lax.axis_index("pipe")
    first = place < 2
    member = lax.rem(place, 2)
    twin = {"pipe": place + 1 - 2 * member}
    other = {"pipe": lax.rem(place + 2, 4)}

    barrier = pltpu.get_barrier_semaphore()
    pl.semaphore_signal(barrier, inc=1, device_id=twin, device_id_type=MESH)
    pl.semaphore_signal(barrier, inc=1, device_id=other, device_id_type=MESH)
    pl.semaphore_wait(barrier, 2)

    def remote(src, dst, send, recv, to):
        return pltpu.make_async_remote_copy(
            src_ref=src, dst_ref=dst, send_sem=send, recv_sem=recv, device_id=to, device_id_type=MESH
        )

    halves = (
        (vec_own, vec, 8),
        (w_qkv, wq, D // 2),
        (w_o, wo, D // 2),
        (w_in, wi, D // 2),
        (w_out, wd, FF // 2),
    )
    locals_, sends, recvs = [], [], []
    for index, (src, dst, rows) in enumerate(halves):
        mine = dst.at[pl.ds(pl.multiple_of(member * rows, rows), rows)]
        theirs = dst.at[pl.ds(pl.multiple_of((1 - member) * rows, rows), rows)]
        locals_.append(pltpu.make_async_copy(src, mine, w_local.at[index]))
        sends.append(remote(src, mine, w_send.at[index], w_recv.at[index], twin))
        recvs.append(remote(src, theirs, w_send.at[index], w_recv.at[index], twin))
    x_home = [pltpu.make_async_copy(x_own.at[k], xin.at[2 * k], e_local.at[k]) for k in range(2)]
    x_away = [
        remote(x_own.at[k], xin.at[2 * k + 1], e_send.at[k], e_recv.at[k], other) for k in range(2)
    ]
    c_home = [
        pltpu.make_async_copy(c_own.at[k], gsl.at[2 * k + 1], e_local.at[k]) for k in range(2)
    ]
    c_away = [
        remote(c_own.at[k], gsl.at[2 * k], e_send.at[k], e_recv.at[k], other) for k in range(2)
    ]
    m_home = pltpu.make_async_copy(mc_own, mcs.at[1], e_local.at[2])
    m_away = remote(mc_own, mcs.at[0], e_send.at[2], e_recv.at[2], other)

    @pl.when(first)
    def _():
        for copy in x_home:
            copy.start()

    for index in (0, 1):
        locals_[index].start()
        sends[index].start()
    for index in (2, 3, 4):
        locals_[index].start()
        sends[index].start()

    @pl.when(first)
    def _():
        for copy in c_away:
            copy.start()
        m_away.start()

    @pl.when(jnp.logical_not(first))
    def _():
        for copy in x_away:
            copy.start()
        for copy in c_home:
            copy.start()
        m_home.start()

    rhs[...] = jnp.zeros_like(rhs)
    ones_row = lax.broadcasted_iota(jnp.int32, (2 * SEG, LANE), 0)
    ones_col = lax.broadcasted_iota(jnp.int32, (2 * SEG, LANE), 1)
    ones = jnp.where(ones_col == jnp.where(ones_row < SEG, 0, 1), 1.0, 0.0).astype(BF)
    for b in range(2):
        stv[b, :, LANE:] = ones
    vecg[...] = jnp.zeros_like(vecg)
    low = lax.broadcasted_iota(jnp.int32, (SEG, LANE), 1) < 64

    def v(row):
        return vec[row : row + 1, :]

    def out_copies(u, buf, results):
        return pltpu.make_async_copy(outb.at[buf], results.at[u], out_sem.at[buf])

    def mid_copy(u, buf):
        return remote(outb.at[buf], xin.at[u], mid_send.at[buf], mid_recv.at[u], other)

    def grad_copy(u, buf):
        return remote(outb.at[buf], gsl.at[u], grad_send.at[buf], grad_recv.at[u], other)

    def tail_copy(item, buf):
        src = outb.at[buf, pl.ds(SEG - TAIL, TAIL)]
        return remote(src, trx.at[item], tail_send.at[item], tail_recv.at[item], other)

    def wait_weights(index):
        locals_[index].wait()
        sends[index].wait_send()
        recvs[index].wait_recv()

    def forward_turn(u, carry):
        item = lax.rem(u, 2)
        buf = lax.rem(u, 2)

        @pl.when(first & (u == 0))
        def _():
            for copy in x_home:
                copy.wait()

        @pl.when(first & (u == 1))
        def _():
            for copy in x_away:
                copy.wait_recv()

        @pl.when(first & (u < 2))
        def _():
            xin[u, SEG - TAIL :, :] = xin[u, SEG - TAIL :, :] + mem0[...]

        @pl.when(first & (u >= 2))
        def _():
            tail_copy(item, buf).wait_recv()
            spread = nn(tail_matrix(True), trx[item]).astype(BF)
            xin[u, SEG - TAIL :, :] = xin[u, SEG - TAIL :, :] + spread

        @pl.when(jnp.logical_not(first))
        def _():
            mid_copy(u, buf).wait_recv()

        pltpu.make_async_copy(xin.at[u], xs.at[u], x_sem.at[u]).start()

        @pl.when(u == 0)
        def _():
            wait_weights(0)
            wait_weights(1)

        mask = kmask[u]
        x = xin[u]
        packed[u, :, :D] = (nn(x, wq[:, :D]) + v(BQ)).astype(BF) * 0.125
        packed[u, :, D : 2 * D] = nn(x, wq[:, D : 2 * D]).astype(BF)
        packed[u, :, 2 * D :] = (nn(x, wq[:, 2 * D :]) + v(BV)).astype(BF)

        @pl.when(u > 0)
        def _():
            hid_copy(u).wait()
            act_copy(u).wait()

        def scores(p):
            b = p % 2
            split_stack(stk.at[b], packed[u, :, D + p * LANE : D + (p + 1) * LANE])
            split_stack(stv.at[b], packed[u, :, 2 * D + p * LANE : 2 * D + (p + 1) * LANE])
            sc[b] = nt(packed[u, :, p * LANE : (p + 1) * LANE], stk[b])

        scores(0)
        for p in range(PAIRS):
            b = p % 2
            if p + 1 < PAIRS:
                scores(p + 1)
            for rows in BLOCKS:
                for h in range(2):
                    cols = slice(h * SEG, (h + 1) * SEG)
                    scaled = sc[b, rows, cols] * LOG2E + mask
                    top = jnp.max(scaled, axis=-1, keepdims=True)
                    big[b * 2 * SEG + rows.start : b * 2 * SEG + rows.stop, cols] = jnp.exp2(
                        scaled - top
                    ).astype(BF)
                    st[u, rows, 2 * p + h : 2 * p + h + 1] = top
            mixed = nn(big[b * 2 * SEG : b * 2 * SEG + SEG, :], stv[b])
            total = mixed[:, LANE : LANE + 2]
            share = 1.0 / total
            ctx[u, :, p * LANE : (p + 1) * LANE] = (
                mixed[:, :LANE] * jnp.where(low, share[:, :1], share[:, 1:])
            ).astype(BF)
            st[u, :, 2 * p : 2 * p + 2] = st[u, :, 2 * p : 2 * p + 2] + jnp.log2(total)
        pltpu.make_async_copy(ctx.at[u], ctxs.at[u], ctx_sem.at[u]).start()

        @pl.when(u == 0)
        def _():
            wait_weights(2)

        sd[0] = nn(ctx[u], wo[...])
        for rows in BLOCKS:
            normed, inverse = norm_parts(xin[u, rows, :].astype(F32) + sd[0, rows, :] + v(BO))
            n1s[u, rows, :] = normed
            st[u, rows, 12:13] = inverse
            hid[rows, :] = (normed * v(G1) + v(N1)).astype(BF)
        hid_copy(u).start()

        @pl.when(u == 0)
        def _():
            wait_weights(3)
            wait_weights(4)

        def up(j):
            sd[j % 2] = nn(hid[...], wi[:, j * D : (j + 1) * D])

        up(0)
        for j in range(4):
            if j + 1 < 4:
                up(j + 1)
            for rows in BLOCKS:
                act, slope = gelu_parts(sd[j % 2, rows, :] + v(BI + j))
                big[j * SEG + rows.start : j * SEG + rows.stop, :] = act.astype(BF)
                dgs[u, rows, j * D : (j + 1) * D] = slope.astype(BF)
            part = nn(big[j * SEG : (j + 1) * SEG, :], wd[j * D : (j + 1) * D, :])
            sc[0] = part if j == 0 else sc[0] + part
        act_copy(u).start()

        @pl.when(u >= 2)
        def _():
            out_copies(u, buf, tops).wait()

        @pl.when((u >= 2) & first)
        def _():
            mid_copy(u, buf).wait_send()

        @pl.when((u >= 2) & jnp.logical_not(first))
        def _():
            tail_copy(item, buf).wait_send()

        for rows in BLOCKS:
            hidden = n1s[u, rows, :] * v(G1) + v(N1)
            normed, inverse = norm_parts(hidden + sc[0, rows, :] + v(BD))
            n2s[u, rows, :] = normed
            st[u, rows, 13:14] = inverse
            outb[buf, rows, :] = (normed * v(G2) + v(N2)).astype(BF)

        @pl.when(first)
        def _():
            mid_copy(u, buf).start()

        @pl.when(jnp.logical_not(first) & (u < 2))
        def _():
            tail_copy(item, buf).start()

        out_copies(u, buf, tops).start()
        return carry

    def hid_copy(u):
        return pltpu.make_async_copy(hid, hids.at[u], hid_sem)

    def act_copy(u):
        return pltpu.make_async_copy(big, acts.at[u], act_sem)

    lax.fori_loop(0, UNITS, forward_turn, 0)

    hid_copy(0).wait()
    act_copy(0).wait()
    for u in range(UNITS):
        pltpu.make_async_copy(ctx.at[u], ctxs.at[u], ctx_sem.at[u]).wait()
    for buf in range(2):
        out_copies(2 + buf, buf, tops).wait()

    @pl.when(first)
    def _():
        for buf in range(2):
            mid_copy(2 + buf, buf).wait_send()
        for copy in c_away:
            copy.wait_send()
        m_away.wait_send()

    @pl.when(jnp.logical_not(first))
    def _():
        for copy in x_away:
            copy.wait_send()
        for copy in c_home:
            copy.wait()
        for copy in c_away:
            copy.wait_recv()
        m_home.wait()
        m_away.wait_recv()

    def gd_copy(u):
        return pltpu.make_async_copy(gdb.at[0], gds.at[u], gd_sem.at[0])

    def gb_copy(u):
        return pltpu.make_async_copy(gdb.at[1], gbs.at[u], gd_sem.at[1])

    def backward_turn(turn, carry):
        u = UNITS - 1 - turn
        item = lax.rem(u, 2)
        buf = lax.rem(u, 2)

        @pl.when(first)
        def _():
            grad_copy(u, buf).wait_recv()

        sd[0] = gsl[u].astype(F32)

        @pl.when(jnp.logical_not(first) & (u >= 2))
        def _():
            sd[0, SEG - TAIL :, :] = sd[0, SEG - TAIL :, :] + mcs[item, 0]

        @pl.when(jnp.logical_not(first) & (u < 2))
        def _():
            tail_copy(item, buf).wait_recv()
            arrived = nn(tail_matrix(False), trx[item])
            sd[0, SEG - TAIL :, :] = (
                sd[0, SEG - TAIL :, :] + arrived * flags[item] + mcs[item, 1]
            )

        @pl.when(turn > 0)
        def _():
            gd_copy(u).wait()
            gb_copy(u).wait()

        for rows in BLOCKS:
            grad = sd[0, rows, :]
            normed = n2s[u, rows, :]
            second = norm_back(grad, normed, st[u, rows, 13:14], v(G2))
            sc[0, rows, :] = second
            down = second.astype(BF)
            gdb[0, rows, :] = down
            vecg[G2 : G2 + 1, :] += row_sum(grad * normed)
            vecg[N2 : N2 + 1, :] += row_sum(grad)
            vecg[BD : BD + 1, :] += row_sum(down.astype(F32))
        gd_copy(u).start()
        for j in range(4):
            sd[j % 2] = nt(gdb[0], wd[j * D : (j + 1) * D, :])
            for rows in BLOCKS:
                cols = slice(j * D, (j + 1) * D)
                lifted = (sd[j % 2, rows, :] * dgs[u, rows, cols].astype(F32)).astype(BF)
                dgs[u, rows, cols] = lifted
                vecg[BI + j : BI + j + 1, :] += row_sum(lifted.astype(F32))
        pltpu.make_async_copy(dgs.at[u], gus.at[u], gu_sem.at[u]).start()
        sd[0] = nt(dgs[u], wi[...])
        for rows in BLOCKS:
            grad = sc[0, rows, :] + sd[0, rows, :]
            normed = n1s[u, rows, :]
            first_grad = norm_back(grad, normed, st[u, rows, 12:13], v(G1))
            branch = first_grad.astype(BF)
            gdb[1, rows, :] = branch
            vecg[G1 : G1 + 1, :] += row_sum(grad * normed)
            vecg[N1 : N1 + 1, :] += row_sum(grad)
            vecg[BO : BO + 1, :] += row_sum(branch.astype(F32))
            n1s[u, rows, :] = first_grad
        gb_copy(u).start()
        head = lax.broadcasted_iota(jnp.int32, (D, LANE), 0) // 64
        heads = (head == lax.broadcasted_iota(jnp.int32, (D, LANE), 1)).astype(F32).astype(BF)
        grad_ctx = nt(gdb[1], wo[...]).astype(BF)
        product = grad_ctx.astype(F32) * ctx[u].astype(F32)
        high = product.astype(BF)
        rest = (product - high.astype(F32)).astype(BF)
        delta[...] = nn(high, heads) + nn(rest, heads)
        ctx[u] = grad_ctx
        mask = kmask[u]

        def scores(p):
            b = p % 2
            query = packed[u, :, p * LANE : (p + 1) * LANE]
            grad = ctx[u, :, p * LANE : (p + 1) * LANE]
            split_stack(stk.at[b], packed[u, :, D + p * LANE : D + (p + 1) * LANE])
            split_stack(stv.at[b], packed[u, :, 2 * D + p * LANE : 2 * D + (p + 1) * LANE])
            rhs[b, :SEG, :LANE] = grad
            rhs[b, SEG:, LANE:] = query
            sc[b] = nt(query, stk[b])
            sd[b] = nt(grad, stv[b, :, :LANE])

        scores(0)
        for p in range(PAIRS):
            b = p % 2
            base = b * 2 * SEG
            if p + 1 < PAIRS:
                scores(p + 1)
            for rows in BLOCKS:
                for h in range(2):
                    cols = slice(h * SEG, (h + 1) * SEG)
                    one = slice(2 * p + h, 2 * p + h + 1)
                    probs = jnp.exp2(sc[b, rows, cols] * LOG2E + mask - st[u, rows, one])
                    big[base + rows.start : base + rows.stop, cols] = probs.astype(BF)
                    big[base + SEG + rows.start : base + SEG + rows.stop, cols] = (
                        probs * (sd[b, rows, cols] - delta[rows, one])
                    ).astype(BF)
            packed[u, :, p * LANE : (p + 1) * LANE] = (
                nn(big[base + SEG : base + 2 * SEG, :], stk[b]) * 0.125
            ).astype(BF)
            both = tn(big[base : base + 2 * SEG, :], rhs[b])
            packed[u, :, D + p * LANE : D + (p + 1) * LANE] = jnp.where(
                low, both[:SEG, LANE:], both[SEG:, LANE:]
            ).astype(BF)
            packed[u, :, 2 * D + p * LANE : 2 * D + (p + 1) * LANE] = jnp.where(
                low, both[:SEG, :LANE], both[SEG:, :LANE]
            ).astype(BF)
        pltpu.make_async_copy(packed.at[u], gps.at[u], gp_sem.at[u]).start()
        for rows in BLOCKS:
            vecg[BQ : BQ + 1, :] += row_sum(packed[u, rows, :D].astype(F32))
            vecg[BV : BV + 1, :] += row_sum(packed[u, rows, 2 * D :].astype(F32))
        sd[0] = nt(packed[u], wq[...])

        @pl.when(turn >= 2)
        def _():
            out_copies(u, buf, backs).wait()

        @pl.when((turn >= 2) & first)
        def _():
            tail_copy(item, buf).wait_send()

        @pl.when((turn >= 2) & jnp.logical_not(first))
        def _():
            grad_copy(u, buf).wait_send()

        for rows in BLOCKS:
            outb[buf, rows, :] = (n1s[u, rows, :] + sd[0, rows, :]).astype(BF)

        @pl.when(jnp.logical_not(first))
        def _():
            grad_copy(u, buf).start()

        @pl.when(first & (u >= 2))
        def _():
            tail_copy(item, buf).start()

        out_copies(u, buf, backs).start()
        return carry

    lax.fori_loop(0, UNITS, backward_turn, 0)

    gd_copy(0).wait()
    gb_copy(0).wait()
    for u in range(UNITS):
        pltpu.make_async_copy(xin.at[u], xs.at[u], x_sem.at[u]).wait()
        pltpu.make_async_copy(dgs.at[u], gus.at[u], gu_sem.at[u]).wait()
        pltpu.make_async_copy(packed.at[u], gps.at[u], gp_sem.at[u]).wait()
    for buf in range(2):
        out_copies(buf, buf, backs).wait()

    @pl.when(jnp.logical_not(first))
    def _():
        for buf in range(2):
            grad_copy(buf, buf).wait_send()


def relay(operands):
    rows = (UNITS, SEG, D)
    shape = jax.ShapeDtypeStruct
    hbm = pl.BlockSpec(memory_space=pl.ANY)
    vmem = pl.BlockSpec(memory_space=pltpu.VMEM)
    results = (
        shape(rows, BF),
        shape(rows, BF),
        shape(rows, BF),
        shape((UNITS, 4 * SEG, D), BF),
        shape(rows, BF),
        shape(rows, BF),
        shape((UNITS, SEG, FF), BF),
        shape(rows, BF),
        shape((UNITS, SEG, 3 * D), BF),
        shape(rows, BF),
        shape((16, D), F32),
    )
    scratch = [
        pltpu.VMEM((D, 3 * D), BF),
        pltpu.VMEM((D, D), BF),
        pltpu.VMEM((D, FF), BF),
        pltpu.VMEM((FF, D), BF),
        pltpu.VMEM((16, D), F32),
        pltpu.VMEM(rows, BF),
        pltpu.VMEM(rows, BF),
        pltpu.VMEM((2, 2, TAIL, D), F32),
        pltpu.VMEM((2, TAIL, D), BF),
        pltpu.VMEM((UNITS, SEG, 3 * D), BF),
        pltpu.VMEM((UNITS, SEG, LANE), F32),
        pltpu.VMEM(rows, F32),
        pltpu.VMEM(rows, F32),
        pltpu.VMEM((UNITS, SEG, FF), BF),
        pltpu.VMEM(rows, BF),
        pltpu.VMEM((2, SEG, D), F32),
        pltpu.VMEM((2, SEG, D), F32),
        pltpu.VMEM((4 * SEG, D), BF),
        pltpu.VMEM((2, 2 * SEG, LANE), BF),
        pltpu.VMEM((2, 2 * SEG, 2 * LANE), BF),
        pltpu.VMEM((2, 2 * SEG, 2 * LANE), BF),
        pltpu.VMEM((SEG, D), BF),
        pltpu.VMEM((2, SEG, D), BF),
        pltpu.VMEM((2, SEG, D), BF),
        pltpu.VMEM((SEG, LANE), F32),
    ]
    counts = [5, 5, 5, 3, 3, 3, 2, 4, 2, 2, 2, 4, 4, 4, 4, 4, 0, 0, 2, 2]
    scratch += [pltpu.SemaphoreType.DMA((n,)) if n else pltpu.SemaphoreType.DMA for n in counts]
    in_specs = [hbm, hbm, vmem, hbm, vmem, vmem, hbm, hbm, hbm, hbm, hbm]
    return pl.pallas_call(
        relay_kernel,
        out_shape=results,
        in_specs=in_specs,
        out_specs=tuple([hbm] * 10 + [vmem]),
        scratch_shapes=scratch,
        compiler_params=pltpu.CompilerParams(
            collective_id=0, has_side_effects=True, vmem_limit_bytes=63 * 2**20
        ),
        cost_estimate=pl.CostEstimate(flops=80 * 10**9, bytes_accessed=80 * 2**20, transcendentals=0),
    )(*operands)


def from_partner(x, axis, bit):
    return lax.ppermute(x, axis, [(i, i ^ 1 << bit) for i in range(lax.axis_size(axis))])


def over_rows(left, right):
    return lax.dot_general(
        left, right, (((0, 1), (0, 1)), ((), ())), preferred_element_type=F32
    )


def per_device(
    text_in,
    memory,
    w_qkv,
    w_o,
    w_in,
    w_out,
    gains,
    biases,
    counts,
    last_lengths,
    text_cot,
    memory_cot,
):
    place = lax.axis_index("pipe")
    first = place < 2
    member = place % 2
    pad = ((0, 0), (0, SEG - TEXT), (0, 0))

    count = counts[place]
    lengths = jnp.stack([jnp.where(count > 1, TEXT, last_lengths[place]), last_lengths[place]])
    two = count > 1
    valid = jnp.stack([jnp.bool_(True), two])
    shown = (jnp.arange(TEXT)[None, :] < lengths[:, None]) & valid[:, None]
    x_own = jnp.pad(text_in[0], pad)
    c_own = jnp.pad(jnp.where(shown[:, :, None], text_cot[0], jnp.zeros_like(text_cot[0])), pad)
    memory_full = lax.all_gather(memory, "pipe", axis=1, tiled=True)
    mem0 = jnp.pad(jnp.concatenate([memory_full, memory_full], 0), ((TAIL - 2 * MEM, 0), (0, 0)))
    placed = jnp.pad(memory_cot[0].astype(F32), ((TAIL - MEM, 0), (0, 0)))
    mc_own = jnp.stack([jnp.where(two, placed, 0.0), jnp.where(two, 0.0, placed)])
    pair_counts = jnp.stack([counts[member], counts[member + 2]])
    pair_last = jnp.stack([last_lengths[member], last_lengths[member + 2]])
    flags = jnp.broadcast_to((pair_counts > 1).astype(F32)[:, None, None], (2, 1, D))
    unit_lengths = jnp.concatenate([jnp.where(pair_counts > 1, TEXT, pair_last), pair_last])
    rows = jnp.arange(SEG)
    keep = (rows[None, :] >= TEXT) | (rows[None, :] < unit_lengths[:, None])
    kmask = jnp.where(keep, 0.0, MASKED).astype(F32)[:, None, :]
    vec_own = jnp.concatenate(
        [gains[None], biases.reshape(5, D), jnp.zeros((2, D), gains.dtype)], 0
    ).astype(F32)

    xs, ctxs, hids, acts, tops, gds, gus, gbs, gps, backs, vecg = relay(
        (x_own, c_own, mem0, mc_own, flags, kmask, w_qkv, w_o, w_in, w_out, vec_own)
    )

    outgoing = jnp.where(first, backs[1::2], tops[0::2])
    returned = from_partner(outgoing, "pipe", 1)
    own_top = jnp.where(first, returned, tops[1::2])
    own_back = jnp.where(first, backs[0::2], returned)
    final_text = jnp.where(shown[:, :, None], own_top[:, :TEXT].astype(F32), 0.0)[None]
    text_grad = own_back[:, :TEXT].astype(F32)[None]
    ends = own_top[:, SEG - MEM :].astype(F32)
    final_memory = jnp.where(two, ends[1], ends[0])[None]

    starts = backs[:2, TEXT:].astype(F32)
    memory_part = jnp.where(first, jnp.sum(starts[:, :MEM] + starts[:, MEM:], axis=0), 0.0)
    memory_part = lax.psum_scatter(memory_part, "pipe", scatter_dimension=1, tiled=True)

    def halves(left, right):
        size = left.shape[-1] // 2
        mine = lax.dynamic_slice_in_dim(left, member * size, size, 2)
        theirs = lax.dynamic_slice_in_dim(left, (1 - member) * size, size, 2)
        return over_rows(mine, right), over_rows(theirs, right).astype(BF)

    parts = [halves(xs, gps), halves(ctxs, gbs), halves(hids, gus)]
    blocks = acts.reshape(UNITS, 4, SEG, D)
    mine = lax.dynamic_slice_in_dim(blocks, member * 2, 2, 1)
    theirs = lax.dynamic_slice_in_dim(blocks, (1 - member) * 2, 2, 1)
    parts.append(
        (
            jnp.concatenate([over_rows(mine[:, i], gds) for i in range(2)], 0),
            jnp.concatenate([over_rows(theirs[:, i], gds) for i in range(2)], 0).astype(BF),
        )
    )
    sums = [keep_part + from_partner(sent, "pipe", 0).astype(F32) for keep_part, sent in parts]
    vec_mine = lax.dynamic_slice_in_dim(vecg, member * 8, 8, 0)
    vec_theirs = lax.dynamic_slice_in_dim(vecg, (1 - member) * 8, 8, 0)
    vec_sum = vec_mine + from_partner(vec_theirs, "pipe", 0)
    reduced = lax.psum((*sums, vec_sum, memory_part), "items")
    return (
        final_text,
        final_memory,
        text_grad,
        reduced[5],
        reduced[0],
        reduced[1],
        reduced[2],
        reduced[3],
        reduced[4][0],
        reduced[4][1:6].reshape(5 * D),
    )


def solution(mesh):
    placed = (
        P(("items", "pipe"), None, None, None),
        P(None, "pipe"),
        P("pipe", None),
        P("pipe", None),
        P("pipe", None),
        P("pipe", None),
        P("pipe"),
        P("pipe"),
        P("items"),
        P("items"),
        P(("items", "pipe"), None, None, None),
        P(("items", "pipe"), None, None),
    )
    return jax.shard_map(
        per_device,
        mesh=mesh,
        in_specs=placed,
        out_specs=(
            P(("items", "pipe"), None, None, None),
            P(("items", "pipe"), None, None),
            P(("items", "pipe"), None, None, None),
            P(None, "pipe"),
            P("pipe", None),
            P("pipe", None),
            P("pipe", None),
            P("pipe", None),
            P("pipe"),
            P("pipe"),
        ),
        check_vma=False,
    )
```

```python
import functools

import jax
import jax.numpy as jnp
from jax import lax
from jax.experimental import pallas as pl
from jax.experimental.pallas import tpu as pltpu
from jax.sharding import PartitionSpec as P

D = 768
FF = 3072
MEM = 10
TEXT = 364
SEG = 384
PAIRS = 6
LANE = 128
TAIL = 32
UNITS = 4
LOG2E = 1.4426950408889634
MASKED = -1.0e9
EPS = 1e-6
MESH = pl.DeviceIdType.MESH
BF = jnp.bfloat16
F32 = jnp.float32
G1, BQ, BV, BO, N1, BD, G2, N2, BI = 0, 1, 2, 3, 4, 5, 8, 9, 10
BLOCKS = [slice(128 * b, 128 * b + 128) for b in range(3)]


def nn(left, right):
    return jnp.dot(left, right, preferred_element_type=F32)


def nt(left, right):
    return lax.dot_general(left, right, (((1,), (1,)), ((), ())), preferred_element_type=F32)


def tn(left, right):
    return lax.dot_general(left, right, (((0,), (0,)), ((), ())), preferred_element_type=F32)


def gelu_parts(up):
    t = pl.reciprocal(1.0 + (0.3275911 * 0.7071067811865476) * jnp.abs(up), approx=True)
    poly = t * (
        0.127414796
        + t * (-0.142248368 + t * (0.7107068705 + t * (-0.7265760135 + t * 0.5307027145)))
    )
    bell = jnp.exp2(up * up * (-0.5 * LOG2E))
    half = poly * bell
    phi = jnp.where(up >= 0, 1.0 - half, half)
    return up * phi, phi + up * bell * 0.3989422804014327


def norm_parts(values):
    centre = values - jnp.mean(values, axis=-1, keepdims=True)
    inverse = lax.rsqrt(jnp.mean(centre * centre, axis=-1, keepdims=True) + EPS)
    return centre * inverse, inverse


def norm_back(grad, normed, inverse, gain):
    scaled = grad * gain
    middle = jnp.mean(scaled, axis=-1, keepdims=True)
    along = jnp.mean(scaled * normed, axis=-1, keepdims=True)
    return inverse * (scaled - middle - normed * along)


def row_sum(values):
    return jnp.sum(values, axis=0, keepdims=True)


def split_stack(dst, src):
    low = lax.broadcasted_iota(jnp.int32, (SEG, LANE), 1) < 64
    zero = jnp.zeros((SEG, LANE), BF)
    dst[:SEG, :LANE] = jnp.where(low, src, zero)
    dst[SEG:, :LANE] = jnp.where(low, zero, src)


def tail_matrix(spread):
    row = lax.broadcasted_iota(jnp.int32, (TAIL, TAIL), 0)
    col = lax.broadcasted_iota(jnp.int32, (TAIL, TAIL), 1)
    if spread:
        keep = ((row >= 22) & (col == row)) | ((row >= 12) & (row < 22) & (col == row + 10))
    else:
        keep = (row >= 22) & ((col == row) | (col == row - 10))
    return jnp.where(keep, 1.0, 0.0).astype(BF)


def relay_kernel(
    x_own,
    c_own,
    mem0,
    mc_own,
    flags,
    kmask,
    w_qkv,
    w_o,
    w_in,
    w_out,
    vec_own,
    xs,
    ctxs,
    hids,
    acts,
    tops,
    gds,
    gus,
    gbs,
    gps,
    backs,
    vecg,
    memg,
    wq,
    wo,
    wi,
    wd,
    vec,
    xin,
    gsl,
    mcs,
    trx,
    packed,
    st,
    n1s,
    n2s,
    dgs,
    ctx,
    sc,
    sd,
    big,
    stk,
    stv,
    rhs,
    hid,
    outb,
    gdb,
    delta,
    w_local,
    w_send,
    w_recv,
    e_local,
    e_send,
    e_recv,
    mid_send,
    mid_recv,
    tail_send,
    tail_recv,
    grad_send,
    grad_recv,
    x_sem,
    ctx_sem,
    gu_sem,
    gp_sem,
    hid_sem,
    act_sem,
    gd_sem,
    out_sem,
):
    place = lax.axis_index("pipe")
    first = place < 2
    member = lax.rem(place, 2)
    twin = {"pipe": place + 1 - 2 * member}
    other = {"pipe": lax.rem(place + 2, 4)}

    barrier = pltpu.get_barrier_semaphore()
    pl.semaphore_signal(barrier, inc=1, device_id=twin, device_id_type=MESH)
    pl.semaphore_signal(barrier, inc=1, device_id=other, device_id_type=MESH)
    pl.semaphore_wait(barrier, 2)

    def remote(src, dst, send, recv, to):
        return pltpu.make_async_remote_copy(
            src_ref=src, dst_ref=dst, send_sem=send, recv_sem=recv, device_id=to, device_id_type=MESH
        )

    halves = (
        (vec_own, vec, 8),
        (w_qkv, wq, D // 2),
        (w_o, wo, D // 2),
        (w_in, wi, D // 2),
        (w_out, wd, FF // 2),
    )
    locals_, sends, recvs = [], [], []
    for index, (src, dst, rows) in enumerate(halves):
        mine = dst.at[pl.ds(pl.multiple_of(member * rows, rows), rows)]
        theirs = dst.at[pl.ds(pl.multiple_of((1 - member) * rows, rows), rows)]
        locals_.append(pltpu.make_async_copy(src, mine, w_local.at[index]))
        sends.append(remote(src, mine, w_send.at[index], w_recv.at[index], twin))
        recvs.append(remote(src, theirs, w_send.at[index], w_recv.at[index], twin))
    x_home = [pltpu.make_async_copy(x_own.at[k], xin.at[2 * k], e_local.at[k]) for k in range(2)]
    x_away = [
        remote(x_own.at[k], xin.at[2 * k + 1], e_send.at[k], e_recv.at[k], other) for k in range(2)
    ]
    c_home = [
        pltpu.make_async_copy(c_own.at[k], gsl.at[2 * k + 1], e_local.at[k]) for k in range(2)
    ]
    c_away = [
        remote(c_own.at[k], gsl.at[2 * k], e_send.at[k], e_recv.at[k], other) for k in range(2)
    ]
    m_home = pltpu.make_async_copy(mc_own, mcs.at[1], e_local.at[2])
    m_away = remote(mc_own, mcs.at[0], e_send.at[2], e_recv.at[2], other)

    @pl.when(first)
    def _():
        for copy in x_home:
            copy.start()

    for index in (0, 1):
        locals_[index].start()
        sends[index].start()
    for index in (2, 3, 4):
        locals_[index].start()
        sends[index].start()

    @pl.when(first)
    def _():
        for copy in c_away:
            copy.start()
        m_away.start()

    @pl.when(jnp.logical_not(first))
    def _():
        for copy in x_away:
            copy.start()
        for copy in c_home:
            copy.start()
        m_home.start()

    rhs[...] = jnp.zeros_like(rhs)
    ones_row = lax.broadcasted_iota(jnp.int32, (2 * SEG, LANE), 0)
    ones_col = lax.broadcasted_iota(jnp.int32, (2 * SEG, LANE), 1)
    ones = jnp.where(ones_col == jnp.where(ones_row < SEG, 0, 1), 1.0, 0.0).astype(BF)
    for b in range(2):
        stv[b, :, LANE:] = ones
    vecg[...] = jnp.zeros_like(vecg)
    memg[...] = jnp.zeros_like(memg)
    low = lax.broadcasted_iota(jnp.int32, (SEG, LANE), 1) < 64

    def v(row):
        return vec[row : row + 1, :]

    def out_copies(u, buf, results):
        return pltpu.make_async_copy(outb.at[buf], results.at[u], out_sem.at[buf])

    def mid_copy(u, buf):
        return remote(outb.at[buf], xin.at[u], mid_send.at[buf], mid_recv.at[u], other)

    def grad_copy(u, buf):
        return remote(outb.at[buf], gsl.at[u], grad_send.at[buf], grad_recv.at[u], other)

    def tail_copy(slot, buf):
        src = outb.at[buf, pl.ds(SEG - TAIL, TAIL)]
        return remote(src, trx.at[slot], tail_send.at[slot], tail_recv.at[slot], other)

    def wait_weights(index):
        locals_[index].wait()
        sends[index].wait_send()
        recvs[index].wait_recv()

    def forward_turn(u, carry):
        item = lax.rem(u, 2)
        buf = lax.rem(u, 2)

        @pl.when(first & (u == 0))
        def _():
            for copy in x_home:
                copy.wait()

        @pl.when(first & (u == 1))
        def _():
            for copy in x_away:
                copy.wait_recv()

        @pl.when(first & (u < 2))
        def _():
            xin[u, SEG - TAIL :, :] = xin[u, SEG - TAIL :, :] + mem0[...]

        @pl.when(first & (u >= 2))
        def _():
            tail_copy(item, buf).wait_recv()
            spread = nn(tail_matrix(True), trx[item]).astype(BF)
            xin[u, SEG - TAIL :, :] = xin[u, SEG - TAIL :, :] + spread

        @pl.when(jnp.logical_not(first))
        def _():
            mid_copy(u, buf).wait_recv()

        pltpu.make_async_copy(xin.at[u], xs.at[u], x_sem.at[u]).start()

        @pl.when(u == 0)
        def _():
            wait_weights(0)
            wait_weights(1)

        mask = kmask[u]
        x = xin[u]
        packed[u, :, :D] = (nn(x, wq[:, :D]) + v(BQ)).astype(BF) * 0.125
        packed[u, :, D : 2 * D] = nn(x, wq[:, D : 2 * D]).astype(BF)
        packed[u, :, 2 * D :] = (nn(x, wq[:, 2 * D :]) + v(BV)).astype(BF)

        @pl.when(u > 0)
        def _():
            hid_copy(u).wait()
            act_copy(u).wait()

        def scores(p):
            b = p % 2
            split_stack(stk.at[b], packed[u, :, D + p * LANE : D + (p + 1) * LANE])
            split_stack(stv.at[b], packed[u, :, 2 * D + p * LANE : 2 * D + (p + 1) * LANE])
            sc[b] = nt(packed[u, :, p * LANE : (p + 1) * LANE], stk[b])

        scores(0)
        for p in range(PAIRS):
            b = p % 2
            if p + 1 < PAIRS:
                scores(p + 1)
            for rows in BLOCKS:
                for h in range(2):
                    cols = slice(h * SEG, (h + 1) * SEG)
                    scaled = sc[b, rows, cols] * LOG2E + mask
                    top = jnp.max(scaled, axis=-1, keepdims=True)
                    big[b * 2 * SEG + rows.start : b * 2 * SEG + rows.stop, cols] = jnp.exp2(
                        scaled - top
                    ).astype(BF)
                    st[u, rows, 2 * p + h : 2 * p + h + 1] = top
            mixed = nn(big[b * 2 * SEG : b * 2 * SEG + SEG, :], stv[b])
            total = mixed[:, LANE : LANE + 2]
            share = 1.0 / total
            ctx[u, :, p * LANE : (p + 1) * LANE] = (
                mixed[:, :LANE] * jnp.where(low, share[:, :1], share[:, 1:])
            ).astype(BF)
            st[u, :, 2 * p : 2 * p + 2] = st[u, :, 2 * p : 2 * p + 2] + jnp.log2(total)
        pltpu.make_async_copy(ctx.at[u], ctxs.at[u], ctx_sem.at[u]).start()

        @pl.when(u == 0)
        def _():
            wait_weights(2)

        sd[0] = nn(ctx[u], wo[...])
        for rows in BLOCKS:
            normed, inverse = norm_parts(xin[u, rows, :].astype(F32) + sd[0, rows, :] + v(BO))
            n1s[u, rows, :] = normed
            st[u, rows, 12:13] = inverse
            hid[rows, :] = (normed * v(G1) + v(N1)).astype(BF)
        hid_copy(u).start()

        @pl.when(u == 0)
        def _():
            wait_weights(3)
            wait_weights(4)

        def up(j):
            sd[j % 2] = nn(hid[...], wi[:, j * D : (j + 1) * D])

        up(0)
        for j in range(4):
            if j + 1 < 4:
                up(j + 1)
            for rows in BLOCKS:
                act, slope = gelu_parts(sd[j % 2, rows, :] + v(BI + j))
                big[j * SEG + rows.start : j * SEG + rows.stop, :] = act.astype(BF)
                dgs[u, rows, j * D : (j + 1) * D] = slope.astype(BF)
            part = nn(big[j * SEG : (j + 1) * SEG, :], wd[j * D : (j + 1) * D, :])
            sc[0] = part if j == 0 else sc[0] + part
        act_copy(u).start()

        @pl.when(u >= 2)
        def _():
            out_copies(u, buf, tops).wait()

        @pl.when((u >= 2) & first)
        def _():
            mid_copy(u, buf).wait_send()

        @pl.when((u >= 2) & jnp.logical_not(first))
        def _():
            tail_copy(item, buf).wait_send()

        for rows in BLOCKS:
            hidden = n1s[u, rows, :] * v(G1) + v(N1)
            normed, inverse = norm_parts(hidden + sc[0, rows, :] + v(BD))
            n2s[u, rows, :] = normed
            st[u, rows, 13:14] = inverse
            outb[buf, rows, :] = (normed * v(G2) + v(N2)).astype(BF)

        @pl.when(first)
        def _():
            mid_copy(u, buf).start()

        @pl.when(jnp.logical_not(first) & (u < 2))
        def _():
            tail_copy(item, buf).start()

        out_copies(u, buf, tops).start()
        return carry

    def hid_copy(u):
        return pltpu.make_async_copy(hid, hids.at[u], hid_sem)

    def act_copy(u):
        return pltpu.make_async_copy(big, acts.at[u], act_sem)

    lax.fori_loop(0, UNITS, forward_turn, 0)

    hid_copy(0).wait()
    act_copy(0).wait()
    for u in range(UNITS):
        pltpu.make_async_copy(ctx.at[u], ctxs.at[u], ctx_sem.at[u]).wait()
    for buf in range(2):
        out_copies(2 + buf, buf, tops).wait()

    @pl.when(first)
    def _():
        for buf in range(2):
            mid_copy(2 + buf, buf).wait_send()
        for copy in c_away:
            copy.wait_send()
        m_away.wait_send()

    @pl.when(jnp.logical_not(first))
    def _():
        for copy in x_away:
            copy.wait_send()
        for copy in c_home:
            copy.wait()
        for copy in c_away:
            copy.wait_recv()
        m_home.wait()
        m_away.wait_recv()

    def gd_copy(u):
        return pltpu.make_async_copy(gdb.at[0], gds.at[u], gd_sem.at[0])

    def gb_copy(u):
        return pltpu.make_async_copy(gdb.at[1], gbs.at[u], gd_sem.at[1])

    def backward_turn(turn, carry):
        u = UNITS - 1 - turn
        item = lax.rem(u, 2)
        buf = lax.rem(u, 2)

        @pl.when(first)
        def _():
            grad_copy(u, buf).wait_recv()

        sd[0] = gsl[u].astype(F32)

        @pl.when(jnp.logical_not(first) & (u >= 2))
        def _():
            sd[0, SEG - TAIL :, :] = sd[0, SEG - TAIL :, :] + mcs[item, 0]

        @pl.when(jnp.logical_not(first) & (u < 2))
        def _():
            tail_copy(u + 2, buf).wait_recv()
            arrived = nn(tail_matrix(False), trx[u + 2])
            sd[0, SEG - TAIL :, :] = (
                sd[0, SEG - TAIL :, :] + arrived * flags[item] + mcs[item, 1]
            )

        @pl.when(turn > 0)
        def _():
            gd_copy(u).wait()
            gb_copy(u).wait()

        for rows in BLOCKS:
            grad = sd[0, rows, :]
            normed = n2s[u, rows, :]
            second = norm_back(grad, normed, st[u, rows, 13:14], v(G2))
            sc[0, rows, :] = second
            down = second.astype(BF)
            gdb[0, rows, :] = down
            vecg[G2 : G2 + 1, :] += row_sum(grad * normed)
            vecg[N2 : N2 + 1, :] += row_sum(grad)
            vecg[BD : BD + 1, :] += row_sum(down.astype(F32))
        gd_copy(u).start()
        for j in range(4):
            sd[j % 2] = nt(gdb[0], wd[j * D : (j + 1) * D, :])
            for rows in BLOCKS:
                cols = slice(j * D, (j + 1) * D)
                lifted = (sd[j % 2, rows, :] * dgs[u, rows, cols].astype(F32)).astype(BF)
                dgs[u, rows, cols] = lifted
                vecg[BI + j : BI + j + 1, :] += row_sum(lifted.astype(F32))
        pltpu.make_async_copy(dgs.at[u], gus.at[u], gu_sem.at[u]).start()
        sd[0] = nt(dgs[u], wi[...])
        for rows in BLOCKS:
            grad = sc[0, rows, :] + sd[0, rows, :]
            normed = n1s[u, rows, :]
            first_grad = norm_back(grad, normed, st[u, rows, 12:13], v(G1))
            branch = first_grad.astype(BF)
            gdb[1, rows, :] = branch
            vecg[G1 : G1 + 1, :] += row_sum(grad * normed)
            vecg[N1 : N1 + 1, :] += row_sum(grad)
            vecg[BO : BO + 1, :] += row_sum(branch.astype(F32))
            n1s[u, rows, :] = first_grad
        gb_copy(u).start()
        head = lax.broadcasted_iota(jnp.int32, (D, LANE), 0) // 64
        heads = (head == lax.broadcasted_iota(jnp.int32, (D, LANE), 1)).astype(F32).astype(BF)
        grad_ctx = nt(gdb[1], wo[...]).astype(BF)
        product = grad_ctx.astype(F32) * ctx[u].astype(F32)
        high = product.astype(BF)
        rest = (product - high.astype(F32)).astype(BF)
        delta[...] = nn(high, heads) + nn(rest, heads)
        ctx[u] = grad_ctx
        mask = kmask[u]

        def scores(p):
            b = p % 2
            query = packed[u, :, p * LANE : (p + 1) * LANE]
            grad = ctx[u, :, p * LANE : (p + 1) * LANE]
            split_stack(stk.at[b], packed[u, :, D + p * LANE : D + (p + 1) * LANE])
            split_stack(stv.at[b], packed[u, :, 2 * D + p * LANE : 2 * D + (p + 1) * LANE])
            rhs[b, :SEG, :LANE] = grad
            rhs[b, SEG:, LANE:] = query
            sc[b] = nt(query, stk[b])
            sd[b] = nt(grad, stv[b, :, :LANE])

        scores(0)
        for p in range(PAIRS):
            b = p % 2
            base = b * 2 * SEG
            if p + 1 < PAIRS:
                scores(p + 1)
            for rows in BLOCKS:
                for h in range(2):
                    cols = slice(h * SEG, (h + 1) * SEG)
                    one = slice(2 * p + h, 2 * p + h + 1)
                    probs = jnp.exp2(sc[b, rows, cols] * LOG2E + mask - st[u, rows, one])
                    big[base + rows.start : base + rows.stop, cols] = probs.astype(BF)
                    big[base + SEG + rows.start : base + SEG + rows.stop, cols] = (
                        probs * (sd[b, rows, cols] - delta[rows, one])
                    ).astype(BF)
            packed[u, :, p * LANE : (p + 1) * LANE] = (
                nn(big[base + SEG : base + 2 * SEG, :], stk[b]) * 0.125
            ).astype(BF)
            both = tn(big[base : base + 2 * SEG, :], rhs[b])
            packed[u, :, D + p * LANE : D + (p + 1) * LANE] = jnp.where(
                low, both[:SEG, LANE:], both[SEG:, LANE:]
            ).astype(BF)
            packed[u, :, 2 * D + p * LANE : 2 * D + (p + 1) * LANE] = jnp.where(
                low, both[:SEG, :LANE], both[SEG:, :LANE]
            ).astype(BF)
        pltpu.make_async_copy(packed.at[u], gps.at[u], gp_sem.at[u]).start()
        for rows in BLOCKS:
            vecg[BQ : BQ + 1, :] += row_sum(packed[u, rows, :D].astype(F32))
            vecg[BV : BV + 1, :] += row_sum(packed[u, rows, 2 * D :].astype(F32))
        sd[0] = nt(packed[u], wq[...])

        @pl.when(turn >= 2)
        def _():
            out_copies(u, buf, backs).wait()

        @pl.when((turn >= 2) & first)
        def _():
            tail_copy(u + 2, buf).wait_send()

        @pl.when((turn >= 2) & jnp.logical_not(first))
        def _():
            grad_copy(u, buf).wait_send()

        for rows in BLOCKS:
            outb[buf, rows, :] = (n1s[u, rows, :] + sd[0, rows, :]).astype(BF)

        @pl.when(jnp.logical_not(first))
        def _():
            grad_copy(u, buf).start()

        @pl.when(first)
        def _():
            tail_copy(u, buf).start()

        @pl.when(first & (u < 2))
        def _():
            memg[...] += nn(tail_matrix(False), outb[buf, SEG - TAIL :, :])

        out_copies(u, buf, backs).start()
        return carry

    lax.fori_loop(0, UNITS, backward_turn, 0)

    gd_copy(0).wait()
    gb_copy(0).wait()
    for u in range(UNITS):
        pltpu.make_async_copy(xin.at[u], xs.at[u], x_sem.at[u]).wait()
        pltpu.make_async_copy(dgs.at[u], gus.at[u], gu_sem.at[u]).wait()
        pltpu.make_async_copy(packed.at[u], gps.at[u], gp_sem.at[u]).wait()
    for buf in range(2):
        out_copies(buf, buf, backs).wait()

    @pl.when(first)
    def _():
        for buf in range(2):
            tail_copy(buf, buf).wait_send()

    @pl.when(jnp.logical_not(first))
    def _():
        for buf in range(2):
            grad_copy(buf, buf).wait_send()
            tail_copy(buf, buf).wait_recv()
            memg[...] += nn(tail_matrix(False), trx[buf])


def relay(operands):
    rows = (UNITS, SEG, D)
    shape = jax.ShapeDtypeStruct
    hbm = pl.BlockSpec(memory_space=pl.ANY)
    vmem = pl.BlockSpec(memory_space=pltpu.VMEM)
    results = (
        shape(rows, BF),
        shape(rows, BF),
        shape(rows, BF),
        shape((UNITS, 4 * SEG, D), BF),
        shape(rows, BF),
        shape(rows, BF),
        shape((UNITS, SEG, FF), BF),
        shape(rows, BF),
        shape((UNITS, SEG, 3 * D), BF),
        shape(rows, BF),
        shape((16, D), F32),
        shape((TAIL, D), F32),
    )
    scratch = [
        pltpu.VMEM((D, 3 * D), BF),
        pltpu.VMEM((D, D), BF),
        pltpu.VMEM((D, FF), BF),
        pltpu.VMEM((FF, D), BF),
        pltpu.VMEM((16, D), F32),
        pltpu.VMEM(rows, BF),
        pltpu.VMEM(rows, BF),
        pltpu.VMEM((2, 2, TAIL, D), F32),
        pltpu.VMEM((UNITS, TAIL, D), BF),
        pltpu.VMEM((UNITS, SEG, 3 * D), BF),
        pltpu.VMEM((UNITS, SEG, LANE), F32),
        pltpu.VMEM(rows, F32),
        pltpu.VMEM(rows, F32),
        pltpu.VMEM((UNITS, SEG, FF), BF),
        pltpu.VMEM(rows, BF),
        pltpu.VMEM((2, SEG, D), F32),
        pltpu.VMEM((2, SEG, D), F32),
        pltpu.VMEM((4 * SEG, D), BF),
        pltpu.VMEM((2, 2 * SEG, LANE), BF),
        pltpu.VMEM((2, 2 * SEG, 2 * LANE), BF),
        pltpu.VMEM((2, 2 * SEG, 2 * LANE), BF),
        pltpu.VMEM((SEG, D), BF),
        pltpu.VMEM((2, SEG, D), BF),
        pltpu.VMEM((2, SEG, D), BF),
        pltpu.VMEM((SEG, LANE), F32),
    ]
    counts = [5, 5, 5, 3, 3, 3, 2, 4, 4, 4, 2, 4, 4, 4, 4, 4, 0, 0, 2, 2]
    scratch += [pltpu.SemaphoreType.DMA((n,)) if n else pltpu.SemaphoreType.DMA for n in counts]
    in_specs = [hbm, hbm, vmem, hbm, vmem, vmem, hbm, hbm, hbm, hbm, hbm]
    return pl.pallas_call(
        relay_kernel,
        out_shape=results,
        in_specs=in_specs,
        out_specs=tuple([hbm] * 10 + [vmem, vmem]),
        scratch_shapes=scratch,
        compiler_params=pltpu.CompilerParams(
            collective_id=0, has_side_effects=True, vmem_limit_bytes=63 * 2**20
        ),
        cost_estimate=pl.CostEstimate(flops=80 * 10**9, bytes_accessed=80 * 2**20, transcendentals=0),
    )(*operands)


BLOCKS_G = 12
CHUNK = SEG // 8
STAGES = 15
SMALL = 8 + TAIL


def reduce_kernel(
    xs,
    ctxs,
    hids,
    acts,
    gps,
    gbs,
    gus,
    gds,
    vecg,
    mem_part,
    f_qkv,
    f_o,
    f_in,
    f_out,
    small,
    xt,
    xm,
    gg,
    own,
    sent,
    tw,
    ring0,
    ring,
    fin,
    sm_tw,
    sm_rx,
    sm_tx,
    load_sem,
    tw_send,
    tw_recv,
    ring_send,
    ring_recv,
    fin_sem,
    sm_send,
    sm_recv,
):
    item = lax.axis_index("items")
    place = lax.axis_index("pipe")
    member = lax.rem(place, 2)
    twin = {"pipe": place + 1 - 2 * member}
    x_at, z_at = lax.rem(item, 2), item // 2
    at = x_at * (7 - z_at) + (1 - x_at) * z_at
    turn = 1 - 2 * member
    logical = (1 - member) * at + member * (7 - at)

    def item_of(position):
        p = lax.rem(position + 8, 8)
        up = p // 4
        return up * (2 * (7 - p) + 1) + (1 - up) * 2 * p

    ahead = {"items": item_of(at + turn)}
    behind = {"items": item_of(at - turn)}
    rounds = [
        {"items": item + 1 - 2 * x_at},
        {"items": item + 2 - 4 * lax.rem(z_at, 2)},
        {"items": item + 4 - 8 * (z_at // 2)},
    ]

    barrier = pltpu.get_barrier_semaphore()
    for to in [twin, ahead, behind, *rounds]:
        pl.semaphore_signal(barrier, inc=1, device_id=to, device_id_type=MESH)
    pl.semaphore_wait(barrier, 6)

    def remote(src, dst, send, recv, to):
        return pltpu.make_async_remote_copy(
            src_ref=src, dst_ref=dst, send_sem=send, recv_sem=recv, device_id=to, device_id_type=MESH
        )

    def loads(left, right, theirs_rows, mine_rows, cols, slot):
        rows_t, col_t = theirs_rows
        rows_m, col_m = mine_rows
        return [
            pltpu.make_async_copy(left.at[:, rows_t, col_t], xt.at[slot], load_sem.at[slot, 0]),
            pltpu.make_async_copy(left.at[:, rows_m, col_m], xm.at[slot], load_sem.at[slot, 1]),
            pltpu.make_async_copy(right.at[:, :, cols], gg.at[slot], load_sem.at[slot, 2]),
        ]

    def aligned(start, size):
        return pl.ds(pl.multiple_of(start, SEG), size)

    def start_loads(b, slot):
        def go(left, right, pick, col):
            for copy in loads(left, right, pick(1 - member), pick(member), aligned(col * D, D), slot):
                copy.start()

        def flat(who):
            return aligned(0, SEG), aligned(who * SEG, SEG)

        @pl.when(b < 4)
        def _():
            def pick(who):
                return aligned((2 * who + b // 2) * SEG, SEG), aligned(lax.rem(b, 2) * SEG, SEG)

            go(acts, gds, pick, 0)

        @pl.when((b >= 4) & (b < 8))
        def _():
            go(hids, gus, flat, b - 4)

        @pl.when(b == 8)
        def _():
            go(ctxs, gbs, flat, 0)

        @pl.when(b >= 9)
        def _():
            go(xs, gps, flat, b - 9)

    def wait_loads(slot):
        zero = aligned(0, SEG)
        for copy in loads(xs, gds, (zero, zero), (zero, zero), aligned(0, D), slot):
            copy.wait()

    def twin_copy(b, slot):
        return remote(sent.at[slot], tw.at[b], tw_send.at[slot], tw_recv.at[b], twin)

    def rows_of(c):
        return pl.ds(pl.multiple_of(c * CHUNK, 16), CHUNK)

    def ring_copy(b, s, src, dst):
        return remote(src, dst, ring_send.at[b, s], ring_recv.at[b, s], ahead)

    def ring_wait(b, s):
        ring_copy(b, s, ring0.at[b], ring0.at[b]).wait_recv()

    def out_copy(b, go):
        @pl.when(b < 4)
        def _():
            go(f_out.at[aligned(b * SEG, SEG)])

        @pl.when((b >= 4) & (b < 8))
        def _():
            go(f_in.at[:, aligned((b - 4) * D, D)])

        @pl.when(b == 8)
        def _():
            go(f_o.at[...])

        @pl.when(b >= 9)
        def _():
            go(f_qkv.at[:, aligned((b - 9) * D, D)])

    def stage(b, s):
        c = lax.rem(logical - s + 16, 8)
        rows = rows_of(c)

        def part():
            return own[b, rows, :] + tw[b, rows, :].astype(F32)

        @pl.when(s == 0)
        def _():
            twin_copy(b, 0).wait_recv()
            ring0[b] = part().astype(BF)
            ring_copy(b, 0, ring0.at[b], ring.at[b, 0]).start()

        @pl.when(s > 0)
        def _():
            ring_wait(b, s - 1)

        @pl.when((s > 0) & (s < 7))
        def _():
            total = ring[b, s - 1].astype(F32) + part()
            ring[b, s - 1] = total.astype(BF)
            ring_copy(b, s, ring.at[b, s - 1], ring.at[b, s]).start()

        @pl.when(s == 7)
        def _():
            fin[b, rows, :] = (ring[b, 6].astype(F32) + part()).astype(BF)

        @pl.when((s >= 7) & (s < STAGES - 1))
        def _():
            ring_copy(b, s, fin.at[b, rows], fin.at[b, rows]).start()

        @pl.when(s == STAGES - 1)
        def _():
            out_copy(b, lambda dst: pltpu.make_async_copy(fin.at[b], dst, fin_sem.at[b]).start())

    def small_twin():
        return remote(sm_tx.at[0], sm_tw, sm_send.at[0], sm_recv.at[0], twin)

    def small_round(k):
        return remote(small, sm_rx.at[k], sm_send.at[k + 1], sm_recv.at[k + 1], rounds[k])

    start_loads(0, 0)
    eight = pl.ds(pl.multiple_of((1 - member) * 8, 8), 8)
    mine8 = pl.ds(pl.multiple_of(member * 8, 8), 8)
    sm_tx[0, :8, :] = vecg[eight, :]
    sm_tx[0, 8:, :] = mem_part[...]
    small[:8, :] = vecg[mine8, :]
    small[8:, :] = mem_part[...]
    small_twin().start()

    def step(i, carry):
        slot = lax.rem(i, 2)

        @pl.when(i < BLOCKS_G)
        def _():
            wait_loads(slot)

            @pl.when(i + 1 < BLOCKS_G)
            def _():
                start_loads(i + 1, 1 - slot)

            @pl.when(i >= 2)
            def _():
                twin_copy(i - 2, slot).wait_send()

            right = gg[slot].reshape(UNITS * SEG, D)
            sent[slot] = tn(xt[slot].reshape(UNITS * SEG, SEG), right).astype(BF)
            twin_copy(i, slot).start()
            own[i] = tn(xm[slot].reshape(UNITS * SEG, SEG), right)

        for k in range(4):

            @pl.when(i == 2 * k + 2)
            def _():
                if k == 0:
                    small_twin().wait()
                    small[...] = small[...] + sm_tw[...]
                else:
                    small_round(k - 1).wait()
                    small[...] = small[...] + sm_rx[k - 1]
                if k < 3:
                    small_round(k).start()

        first_b = jnp.maximum(i - STAGES, 0)
        last_b = jnp.minimum(i, BLOCKS_G)

        def serve(b, inner):
            stage(b, i - 1 - b)
            return inner

        lax.fori_loop(first_b, last_b, serve, 0)
        return carry

    lax.fori_loop(0, BLOCKS_G + STAGES, step, 0)

    twin_copy(0, 0).wait_send()
    twin_copy(1, 1).wait_send()

    def drain(b, carry):
        def one(s, inner):
            ring_copy(b, s, ring0.at[b], ring0.at[b]).wait_send()
            return inner

        lax.fori_loop(0, STAGES - 1, one, 0)
        out_copy(b, lambda dst: pltpu.make_async_copy(fin.at[b], dst, fin_sem.at[b]).wait())
        return carry

    lax.fori_loop(0, BLOCKS_G, drain, 0)


def reduce_grads(operands):
    shape = jax.ShapeDtypeStruct
    hbm = pl.BlockSpec(memory_space=pl.ANY)
    vmem = pl.BlockSpec(memory_space=pltpu.VMEM)
    dma = pltpu.SemaphoreType.DMA
    return pl.pallas_call(
        reduce_kernel,
        out_shape=(
            shape((SEG, 3 * D), BF),
            shape((SEG, D), BF),
            shape((SEG, FF), BF),
            shape((FF // 2, D), BF),
            shape((SMALL, D), F32),
        ),
        in_specs=[hbm] * 8 + [vmem, vmem],
        out_specs=(hbm, hbm, hbm, hbm, vmem),
        scratch_shapes=[
            pltpu.VMEM((2, UNITS, SEG, SEG), BF),
            pltpu.VMEM((2, UNITS, SEG, SEG), BF),
            pltpu.VMEM((2, UNITS, SEG, D), BF),
            pltpu.VMEM((BLOCKS_G, SEG, D), F32),
            pltpu.VMEM((2, SEG, D), BF),
            pltpu.VMEM((BLOCKS_G, SEG, D), BF),
            pltpu.VMEM((BLOCKS_G, CHUNK, D), BF),
            pltpu.VMEM((BLOCKS_G, 7, CHUNK, D), BF),
            pltpu.VMEM((BLOCKS_G, SEG, D), BF),
            pltpu.VMEM((SMALL, D), F32),
            pltpu.VMEM((3, SMALL, D), F32),
            pltpu.VMEM((1, SMALL, D), F32),
            dma((2, 3)),
            dma((2,)),
            dma((BLOCKS_G,)),
            dma((BLOCKS_G, STAGES - 1)),
            dma((BLOCKS_G, STAGES - 1)),
            dma((BLOCKS_G,)),
            dma((4,)),
            dma((4,)),
        ],
        compiler_params=pltpu.CompilerParams(
            collective_id=1, has_side_effects=True, vmem_limit_bytes=60 * 2**20
        ),
        cost_estimate=pl.CostEstimate(flops=22 * 10**9, bytes_accessed=64 * 2**20, transcendentals=0),
    )(*operands)


def from_partner(x, axis, bit):
    return lax.ppermute(x, axis, [(i, i ^ 1 << bit) for i in range(lax.axis_size(axis))])


def over_rows(left, right):
    return lax.dot_general(
        left, right, (((0, 1), (0, 1)), ((), ())), preferred_element_type=F32
    )


def sum_grads(member, xs, ctxs, hids, acts, gps, gbs, gus, gds, vecg, memg):
    def halves(left, right):
        size = left.shape[-1] // 2
        mine = lax.dynamic_slice_in_dim(left, member * size, size, 2)
        theirs = lax.dynamic_slice_in_dim(left, (1 - member) * size, size, 2)
        return over_rows(mine, right), over_rows(theirs, right).astype(BF)

    parts = [halves(xs, gps), halves(ctxs, gbs), halves(hids, gus)]
    blocks = acts.reshape(UNITS, 4, SEG, D)
    mine = lax.dynamic_slice_in_dim(blocks, member * 2, 2, 1)
    theirs = lax.dynamic_slice_in_dim(blocks, (1 - member) * 2, 2, 1)
    parts.append(
        (
            jnp.concatenate([over_rows(mine[:, i], gds) for i in range(2)], 0),
            jnp.concatenate([over_rows(theirs[:, i], gds) for i in range(2)], 0).astype(BF),
        )
    )
    sums = [kept + from_partner(sent, "pipe", 0).astype(F32) for kept, sent in parts]
    vec_mine = lax.dynamic_slice_in_dim(vecg, member * 8, 8, 0)
    vec_theirs = lax.dynamic_slice_in_dim(vecg, (1 - member) * 8, 8, 0)
    mine_small = jnp.concatenate([vec_mine, memg], 0)
    small = mine_small + from_partner(jnp.concatenate([vec_theirs, memg], 0), "pipe", 0)
    *grads, small = lax.psum((*sums, small), "items")
    return grads, small


def per_device(
    text_in,
    memory,
    w_qkv,
    w_o,
    w_in,
    w_out,
    gains,
    biases,
    counts,
    last_lengths,
    text_cot,
    memory_cot,
):
    place = lax.axis_index("pipe")
    first = place < 2
    member = place % 2
    pad = ((0, 0), (0, SEG - TEXT), (0, 0))

    count = counts[place]
    lengths = jnp.stack([jnp.where(count > 1, TEXT, last_lengths[place]), last_lengths[place]])
    two = count > 1
    valid = jnp.stack([jnp.bool_(True), two])
    shown = (jnp.arange(TEXT)[None, :] < lengths[:, None]) & valid[:, None]
    x_own = jnp.pad(text_in[0], pad)
    c_own = jnp.pad(jnp.where(shown[:, :, None], text_cot[0], jnp.zeros_like(text_cot[0])), pad)
    memory_full = lax.all_gather(memory, "pipe", axis=1, tiled=True)
    mem0 = jnp.pad(jnp.concatenate([memory_full, memory_full], 0), ((TAIL - 2 * MEM, 0), (0, 0)))
    placed = jnp.pad(memory_cot[0].astype(F32), ((TAIL - MEM, 0), (0, 0)))
    mc_own = jnp.stack([jnp.where(two, placed, 0.0), jnp.where(two, 0.0, placed)])
    pair_counts = jnp.stack([counts[member], counts[member + 2]])
    pair_last = jnp.stack([last_lengths[member], last_lengths[member + 2]])
    flags = jnp.broadcast_to((pair_counts > 1).astype(F32)[:, None, None], (2, 1, D))
    unit_lengths = jnp.concatenate([jnp.where(pair_counts > 1, TEXT, pair_last), pair_last])
    rows = jnp.arange(SEG)
    keep = (rows[None, :] >= TEXT) | (rows[None, :] < unit_lengths[:, None])
    kmask = jnp.where(keep, 0.0, MASKED).astype(F32)[:, None, :]
    vec_own = jnp.concatenate(
        [gains[None], biases.reshape(5, D), jnp.zeros((2, D), gains.dtype)], 0
    ).astype(F32)

    xs, ctxs, hids, acts, tops, gds, gus, gbs, gps, backs, vecg, memg = relay(
        (x_own, c_own, mem0, mc_own, flags, kmask, w_qkv, w_o, w_in, w_out, vec_own)
    )

    outgoing = jnp.where(first, backs[1::2], tops[0::2])
    returned = from_partner(outgoing, "pipe", 1)
    if lax.axis_size("items") == 8:
        *grads, small = reduce_grads((xs, ctxs, hids, acts, gps, gbs, gus, gds, vecg, memg))
        grads = [grad.astype(F32) for grad in grads]
    else:
        grads, small = sum_grads(member, xs, ctxs, hids, acts, gps, gbs, gus, gds, vecg, memg)
    own_top = jnp.where(first, returned, tops[1::2])
    own_back = jnp.where(first, backs[0::2], returned)
    final_text = jnp.where(shown[:, :, None], own_top[:, :TEXT].astype(F32), 0.0)[None]
    text_grad = own_back[:, :TEXT].astype(F32)[None]
    ends = own_top[:, SEG - MEM :].astype(F32)
    final_memory = jnp.where(two, ends[1], ends[0])[None]
    width = D // 4
    memory_grad = lax.dynamic_slice(small, (SMALL - MEM, place * width), (MEM, width))
    return (
        final_text,
        final_memory,
        text_grad,
        memory_grad,
        *grads,
        small[0],
        small[1:6].reshape(5 * D),
    )


def solution(mesh):
    placed = (
        P(("items", "pipe"), None, None, None),
        P(None, "pipe"),
        P("pipe", None),
        P("pipe", None),
        P("pipe", None),
        P("pipe", None),
        P("pipe"),
        P("pipe"),
        P("items"),
        P("items"),
        P(("items", "pipe"), None, None, None),
        P(("items", "pipe"), None, None),
    )
    return jax.shard_map(
        per_device,
        mesh=mesh,
        in_specs=placed,
        out_specs=(
            P(("items", "pipe"), None, None, None),
            P(("items", "pipe"), None, None),
            P(("items", "pipe"), None, None, None),
            P(None, "pipe"),
            P("pipe", None),
            P("pipe", None),
            P("pipe", None),
            P("pipe", None),
            P("pipe"),
            P("pipe"),
        ),
        check_vma=False,
    )
```

```python
import functools

import jax
import jax.numpy as jnp
from jax import lax
from jax.experimental import pallas as pl
from jax.experimental.pallas import tpu as pltpu
from jax.sharding import PartitionSpec as P

D = 768
FF = 3072
MEM = 10
TEXT = 364
SEG = 384
PAIRS = 6
LANE = 128
TAIL = 32
UNITS = 4
LOG2E = 1.4426950408889634
MASKED = -1.0e9
EPS = 1e-6
MESH = pl.DeviceIdType.MESH
BF = jnp.bfloat16
F32 = jnp.float32
G1, BQ, BV, BO, N1, BD, G2, N2, BI = 0, 1, 2, 3, 4, 5, 8, 9, 10
BLOCKS = [slice(128 * b, 128 * b + 128) for b in range(3)]


def nn(left, right):
    return jnp.dot(left, right, preferred_element_type=F32)


def nt(left, right):
    return lax.dot_general(left, right, (((1,), (1,)), ((), ())), preferred_element_type=F32)


def tn(left, right):
    return lax.dot_general(left, right, (((0,), (0,)), ((), ())), preferred_element_type=F32)


def gelu_parts(up):
    t = pl.reciprocal(1.0 + (0.3275911 * 0.7071067811865476) * jnp.abs(up), approx=True)
    poly = t * (
        0.127414796
        + t * (-0.142248368 + t * (0.7107068705 + t * (-0.7265760135 + t * 0.5307027145)))
    )
    bell = jnp.exp2(up * up * (-0.5 * LOG2E))
    half = poly * bell
    phi = jnp.where(up >= 0, 1.0 - half, half)
    return up * phi, phi + up * bell * 0.3989422804014327


def norm_parts(values):
    centre = values - jnp.mean(values, axis=-1, keepdims=True)
    inverse = lax.rsqrt(jnp.mean(centre * centre, axis=-1, keepdims=True) + EPS)
    return centre * inverse, inverse


def norm_back(grad, normed, inverse, gain):
    scaled = grad * gain
    middle = jnp.mean(scaled, axis=-1, keepdims=True)
    along = jnp.mean(scaled * normed, axis=-1, keepdims=True)
    return inverse * (scaled - middle - normed * along)


def row_sum(values):
    return jnp.sum(values, axis=0, keepdims=True)


def split_stack(dst, src):
    low = lax.broadcasted_iota(jnp.int32, (SEG, LANE), 1) < 64
    zero = jnp.zeros((SEG, LANE), BF)
    dst[:SEG, :LANE] = jnp.where(low, src, zero)
    dst[SEG:, :LANE] = jnp.where(low, zero, src)


def tail_matrix(spread):
    row = lax.broadcasted_iota(jnp.int32, (TAIL, TAIL), 0)
    col = lax.broadcasted_iota(jnp.int32, (TAIL, TAIL), 1)
    if spread:
        keep = ((row >= 22) & (col == row)) | ((row >= 12) & (row < 22) & (col == row + 10))
    else:
        keep = (row >= 22) & ((col == row) | (col == row - 10))
    return jnp.where(keep, 1.0, 0.0).astype(BF)


def relay_kernel(
    x_own,
    c_own,
    mem_own,
    mcot_own,
    counts,
    lasts,
    w_qkv,
    w_o,
    w_in,
    w_out,
    vec_own,
    xs,
    ctxs,
    hids,
    acts,
    own_top,
    gds,
    gus,
    gbs,
    gps,
    own_back,
    slopes,
    vecg,
    memg,
    wq,
    wo,
    wi,
    wd,
    vec,
    xin,
    gsl,
    mcs,
    mem_rx,
    mem0,
    trx,
    packed,
    st,
    n1s,
    n2s,
    dgf,
    gub,
    ctx,
    sc,
    sd,
    big,
    stk,
    stv,
    rhs,
    hid,
    outb,
    gdb,
    delta,
    parts,
    w_local,
    w_send,
    w_recv,
    e_local,
    e_send,
    e_recv,
    mid_send,
    mid_recv,
    tail_send,
    tail_recv,
    grad_send,
    grad_recv,
    x_sem,
    ctx_sem,
    gu_sem,
    gp_sem,
    hid_sem,
    act_sem,
    gd_sem,
    dg_sem,
    mem_send,
    mem_recv,
    top_send,
    top_recv,
    back_send,
    back_recv,
    res_sem,
    lag,
):
    place = lax.axis_index("pipe")
    first = place < 2
    member = lax.rem(place, 2)
    twin = {"pipe": place + 1 - 2 * member}
    other = {"pipe": lax.rem(place + 2, 4)}
    across = {"pipe": 3 - place}
    second = jnp.logical_not(first)

    barrier = pltpu.get_barrier_semaphore()
    for to in (twin, other, across):
        pl.semaphore_signal(barrier, inc=1, device_id=to, device_id_type=MESH)
    pl.semaphore_wait(barrier, 3)

    def remote(src, dst, send, recv, to):
        return pltpu.make_async_remote_copy(
            src_ref=src, dst_ref=dst, send_sem=send, recv_sem=recv, device_id=to, device_id_type=MESH
        )

    halves = (
        (vec_own, vec, 8),
        (w_qkv, wq, D // 2),
        (w_o, wo, D // 2),
        (w_in, wi, D // 2),
        (w_out, wd, FF // 2),
    )
    locals_, sends, recvs = [], [], []
    for index, (src, dst, rows) in enumerate(halves):
        mine = dst.at[pl.ds(pl.multiple_of(member * rows, rows), rows)]
        theirs = dst.at[pl.ds(pl.multiple_of((1 - member) * rows, rows), rows)]
        locals_.append(pltpu.make_async_copy(src, mine, w_local.at[index]))
        sends.append(remote(src, mine, w_send.at[index], w_recv.at[index], twin))
        recvs.append(remote(src, theirs, w_send.at[index], w_recv.at[index], twin))
    x_home = [pltpu.make_async_copy(x_own.at[k], xin.at[2 * k], e_local.at[k]) for k in range(2)]
    x_away = [
        remote(x_own.at[k], xin.at[2 * k + 1], e_send.at[k], e_recv.at[k], other) for k in range(2)
    ]
    c_home = [
        pltpu.make_async_copy(c_own.at[k], gsl.at[2 * k + 1], e_local.at[k]) for k in range(2)
    ]
    c_away = [
        remote(c_own.at[k], gsl.at[2 * k], e_send.at[k], e_recv.at[k], other) for k in range(2)
    ]
    m_home = pltpu.make_async_copy(mcot_own, mcs.at[1], e_local.at[2])
    m_away = remote(mcot_own, mcs.at[0], e_send.at[2], e_recv.at[2], other)
    mem_twin = remote(mem_own, mem_rx.at[place], mem_send.at[0], mem_recv.at[place], twin)
    mem_other = remote(mem_own, mem_rx.at[place], mem_send.at[0], mem_recv.at[place], other)
    mem_across = remote(mem_own, mem_rx.at[place], mem_send.at[1], mem_recv.at[place], across)

    def start_weights(index):
        locals_[index].start()
        sends[index].start()

    def wait_weights(index):
        locals_[index].wait()
        recvs[index].wait_recv()

    start_weights(0)
    start_weights(1)

    @pl.when(first)
    def _():
        for copy in x_home:
            copy.start()
        mem_twin.start()

    @pl.when(second)
    def _():
        mem_other.start()
        mem_across.start()
        x_away[0].start()
        for copy in c_home:
            copy.start()
        m_home.start()

    rhs[...] = jnp.zeros_like(rhs)
    ones = jnp.ones((2 * LANE, LANE), BF)
    vecg[...] = jnp.zeros_like(vecg)
    memg[...] = jnp.zeros_like(memg)
    low = lax.broadcasted_iota(jnp.int32, (SEG, LANE), 1) < 64

    @pl.when(first)
    def _():
        mem_twin.wait_send()
        for index in range(4):

            @pl.when(index != place)
            def _():
                remote(mem_own, mem_rx.at[index], mem_send.at[0], mem_recv.at[index], twin).wait_recv()

            @pl.when(index == place)
            def _():
                mem_rx[index] = mem_own[...]

        row = lax.broadcasted_iota(jnp.int32, (TAIL, 16), 0)
        col = lax.broadcasted_iota(jnp.int32, (TAIL, 16), 1)
        twice = ((col == row - 12) | (col == row - 22)) & (col < MEM)
        spread = jnp.where(twice, 1.0, 0.0).astype(BF)
        total = jnp.zeros((TAIL, D), F32)
        for index in range(4):
            source = lax.broadcasted_iota(jnp.int32, (2 * LANE, D), 0)
            target = lax.broadcasted_iota(jnp.int32, (2 * LANE, D), 1)
            move = (target == source + index * (D // 4)) & (source < D // 4)
            rows = nn(spread, mem_rx[index]).astype(BF)
            total = total + nn(rows, jnp.where(move, 1.0, 0.0).astype(BF))
        mem0[...] = total.astype(BF)

    def unit_scalars(u):
        item = lax.rem(u, 2)
        count = counts[member + 2 * item]
        last = lasts[member + 2 * item]
        length = jnp.where((u < 2) & (count > 1), TEXT, last)
        return count, length

    def key_mask(length):
        key = lax.broadcasted_iota(jnp.int32, (1, SEG), 1)
        return jnp.where((key >= TEXT) | (key < length), 0.0, MASKED)

    def v(row):
        return vec[row : row + 1, :]

    def top_copy(u):
        return remote(
            outb.at[0], own_top.at[u // 2], top_send.at[0], top_recv.at[u // 2], other
        )

    def top_here(u):
        return pltpu.make_async_copy(outb.at[1], own_top.at[u // 2], res_sem.at[0])

    def back_copy(u):
        return remote(
            outb.at[1], own_back.at[u // 2], back_send.at[0], back_recv.at[u // 2], other
        )

    def back_here(u):
        return pltpu.make_async_copy(outb.at[0], own_back.at[u // 2], res_sem.at[1])

    def mid_copy(u, buf):
        return remote(outb.at[buf], xin.at[u], mid_send.at[buf], mid_recv.at[u], other)

    def grad_copy(u, buf):
        return remote(outb.at[buf], gsl.at[u], grad_send.at[buf], grad_recv.at[u], other)

    def tail_copy(slot, buf):
        src = outb.at[buf, pl.ds(SEG - TAIL, TAIL)]
        return remote(src, trx.at[slot], tail_send.at[slot], tail_recv.at[slot], other)

    def forward_turn(u, carry):
        item = lax.rem(u, 2)
        buf = lax.rem(u, 2)

        @pl.when(u == 0)
        def _():
            wait_weights(0)
            wait_weights(1)
            for index in (2, 3, 4):
                start_weights(index)

        @pl.when(first & (u == 0))
        def _():
            for copy in x_home:
                copy.wait()

        @pl.when(first & (member == 1) & (u == 0))
        def _():
            pl.semaphore_wait(lag, 1)

        @pl.when(first & (u == 1))
        def _():
            x_away[0].wait_recv()

        @pl.when(first & (u == 3))
        def _():
            x_away[1].wait_recv()

        @pl.when(second & (u == 0))
        def _():
            x_away[0].wait_send()
            x_away[1].start()

        @pl.when(first & (u < 2))
        def _():
            xin[u, SEG - TAIL :, :] = xin[u, SEG - TAIL :, :] + mem0[...]

        @pl.when(first & (u >= 2))
        def _():
            tail_copy(item, buf).wait_recv()
            spread = nn(tail_matrix(True), trx[item]).astype(BF)
            xin[u, SEG - TAIL :, :] = xin[u, SEG - TAIL :, :] + spread

        @pl.when(second)
        def _():
            mid_copy(u, buf).wait_recv()

        pltpu.make_async_copy(xin.at[u], xs.at[u], x_sem.at[u]).start()

        count, length = unit_scalars(u)
        mask = key_mask(length)
        x = xin[u]
        packed[u, :, :D] = (nn(x, wq[:, :D]) + v(BQ)).astype(BF) * 0.125
        packed[u, :, D : 2 * D] = nn(x, wq[:, D : 2 * D]).astype(BF)
        packed[u, :, 2 * D :] = (nn(x, wq[:, 2 * D :]) + v(BV)).astype(BF)

        @pl.when(u > 0)
        def _():
            hid_copy(u).wait()
            act_copy(u).wait()
            slope_out(u - 1).wait()

        def scores(p):
            b = p % 2
            split_stack(stk.at[b], packed[u, :, D + p * LANE : D + (p + 1) * LANE])
            split_stack(stv.at[b], packed[u, :, 2 * D + p * LANE : 2 * D + (p + 1) * LANE])
            sc[b] = nt(packed[u, :, p * LANE : (p + 1) * LANE], stk[b])

        scores(0)
        for p in range(PAIRS):
            b = p % 2
            if p + 1 < PAIRS:
                scores(p + 1)
            for rows in BLOCKS:
                for h in range(2):
                    cols = slice(h * SEG, (h + 1) * SEG)
                    scaled = sc[b, rows, cols] * LOG2E + mask
                    top = jnp.max(scaled, axis=-1, keepdims=True)
                    raised = jnp.exp2(scaled - top)
                    total = jnp.sum(raised, axis=-1, keepdims=True)
                    big[b * 2 * SEG + rows.start : b * 2 * SEG + rows.stop, cols] = (
                        raised * (1.0 / total)
                    ).astype(BF)
                    st[u, rows, 2 * p + h : 2 * p + h + 1] = top + jnp.log2(total)
            ctx[u, :, p * LANE : (p + 1) * LANE] = nn(
                big[b * 2 * SEG : b * 2 * SEG + SEG, :], stv[b]
            ).astype(BF)
        pltpu.make_async_copy(ctx.at[u], ctxs.at[u], ctx_sem.at[u]).start()

        @pl.when(first & (member == 0) & (u == 0))
        def _():
            pl.semaphore_signal(lag, inc=1, device_id=twin, device_id_type=MESH)

        @pl.when(u == 0)
        def _():
            wait_weights(2)

        sd[0] = nn(ctx[u], wo[...])
        for rows in BLOCKS:
            normed, inverse = norm_parts(xin[u, rows, :].astype(F32) + sd[0, rows, :] + v(BO))
            n1s[u, rows, :] = normed
            st[u, rows, 12:13] = inverse
            hid[rows, :] = (normed * v(G1) + v(N1)).astype(BF)
        hid_copy(u).start()

        @pl.when(u == 0)
        def _():
            wait_weights(3)
            wait_weights(4)

        def up(j):
            sd[j % 2] = nn(hid[...], wi[:, j * D : (j + 1) * D])

        up(0)
        for j in range(4):
            if j + 1 < 4:
                up(j + 1)
            for rows in BLOCKS:
                act, slope = gelu_parts(sd[j % 2, rows, :] + v(BI + j))
                big[j * SEG + rows.start : j * SEG + rows.stop, :] = act.astype(BF)
                dgf[rows, j * D : (j + 1) * D] = slope
            part = nn(big[j * SEG : (j + 1) * SEG, :], wd[j * D : (j + 1) * D, :])
            sc[0] = part if j == 0 else sc[0] + part
        act_copy(u).start()

        @pl.when(u < UNITS - 1)
        def _():
            slope_out(u).start()

        @pl.when(second & (u == 2))
        def _():
            top_copy(u).wait_send()

        @pl.when(second & (u == 3))
        def _():
            top_here(u).wait()

        @pl.when((u >= 2) & first)
        def _():
            mid_copy(u, buf).wait_send()

        @pl.when((u >= 2) & second)
        def _():
            tail_copy(item, buf).wait_send()

        for rows in BLOCKS:
            hidden = n1s[u, rows, :] * v(G1) + v(N1)
            normed, inverse = norm_parts(hidden + sc[0, rows, :] + v(BD))
            n2s[u, rows, :] = normed
            st[u, rows, 13:14] = inverse
            outb[buf, rows, :] = (normed * v(G2) + v(N2)).astype(BF)

        @pl.when(first)
        def _():
            mid_copy(u, buf).start()

        @pl.when(second & (u < 2))
        def _():
            tail_copy(item, buf).start()

        @pl.when(second & (item == 0))
        def _():
            top_copy(u).start()

        @pl.when(second & (item == 1))
        def _():
            top_here(u).start()

        return carry

    def hid_copy(u):
        return pltpu.make_async_copy(hid, hids.at[u], hid_sem)

    def act_copy(u):
        return pltpu.make_async_copy(big, acts.at[u], act_sem)

    def slope_out(u):
        return pltpu.make_async_copy(dgf, slopes.at[u], dg_sem.at[0])

    def slope_in(u):
        return pltpu.make_async_copy(slopes.at[u], dgf, dg_sem.at[1])

    lax.fori_loop(0, UNITS, forward_turn, 0)

    hid_copy(0).wait()
    act_copy(0).wait()
    for u in range(UNITS):
        pltpu.make_async_copy(ctx.at[u], ctxs.at[u], ctx_sem.at[u]).wait()
    for index in range(5):
        sends[index].wait_send()

    @pl.when(first)
    def _():
        for buf in range(2):
            mid_copy(2 + buf, buf).wait_send()
        pl.semaphore_signal(lag, inc=1, device_id=twin, device_id_type=MESH)
        pl.semaphore_wait(lag, 1)
        c_away[1].start()
        m_away.start()
        c_away[1].wait_send()
        c_away[0].start()

    @pl.when(second)
    def _():
        top_copy(2).wait_send()
        top_here(3).wait()
        x_away[1].wait_send()
        mem_other.wait_send()
        mem_across.wait_send()
        for copy in c_home:
            copy.wait()
        m_home.wait()

    def gd_copy(u):
        return pltpu.make_async_copy(gdb.at[0], gds.at[u], gd_sem.at[0])

    def gb_copy(u):
        return pltpu.make_async_copy(gdb.at[1], gbs.at[u], gd_sem.at[1])

    def gu_copy(u):
        return pltpu.make_async_copy(gub, gus.at[u], gu_sem)

    def backward_turn(turn, carry):
        u = UNITS - 1 - turn
        item = lax.rem(u, 2)
        buf = lax.rem(u, 2)

        @pl.when(first)
        def _():
            grad_copy(u, buf).wait_recv()

        @pl.when(second & (u == 2))
        def _():
            c_away[1].wait_recv()
            m_away.wait_recv()

        @pl.when(second & (u == 0))
        def _():
            c_away[0].wait_recv()

        count, length = unit_scalars(u)
        limit = jnp.where(first, SEG, jnp.where((u < 2) | (count > 1), length, 0))
        row = lax.broadcasted_iota(jnp.int32, (SEG, D), 0)
        sd[0] = jnp.where(row < limit, gsl[u].astype(F32), 0.0)
        both_live = jnp.where(count > 1, 1.0, 0.0)

        @pl.when(second & (u >= 2))
        def _():
            sd[0, SEG - TAIL :, :] = sd[0, SEG - TAIL :, :] + mcs[item].astype(F32) * both_live

        @pl.when(second & (u < 2))
        def _():
            tail_copy(u + 2, buf).wait_recv()
            arrived = nn(tail_matrix(False), trx[u + 2])
            sd[0, SEG - TAIL :, :] = (
                sd[0, SEG - TAIL :, :]
                + arrived * both_live
                + mcs[item].astype(F32) * (1.0 - both_live)
            )

        @pl.when(turn > 0)
        def _():
            gd_copy(u).wait()
            gb_copy(u).wait()
            gu_copy(u).wait()
            slope_in(u).wait()

        for rows in BLOCKS:
            grad = sd[0, rows, :]
            normed = n2s[u, rows, :]
            second_grad = norm_back(grad, normed, st[u, rows, 13:14], v(G2))
            sc[0, rows, :] = second_grad
            down = second_grad.astype(BF)
            gdb[0, rows, :] = down
            vecg[G2 : G2 + 1, :] += row_sum(grad * normed)
            vecg[N2 : N2 + 1, :] += row_sum(grad)
            vecg[BD : BD + 1, :] += row_sum(down.astype(F32))
        gd_copy(u).start()
        for j in range(4):
            sd[j % 2] = nt(gdb[0], wd[j * D : (j + 1) * D, :])
            for rows in BLOCKS:
                cols = slice(j * D, (j + 1) * D)
                lifted = (sd[j % 2, rows, :] * dgf[rows, cols]).astype(BF)
                gub[rows, cols] = lifted
                vecg[BI + j : BI + j + 1, :] += row_sum(lifted.astype(F32))
        gu_copy(u).start()

        @pl.when(u > 0)
        def _():
            slope_in(u - 1).start()

        sd[0] = nt(gub[...], wi[...])
        for rows in BLOCKS:
            grad = sc[0, rows, :] + sd[0, rows, :]
            normed = n1s[u, rows, :]
            first_grad = norm_back(grad, normed, st[u, rows, 12:13], v(G1))
            branch = first_grad.astype(BF)
            gdb[1, rows, :] = branch
            vecg[G1 : G1 + 1, :] += row_sum(grad * normed)
            vecg[N1 : N1 + 1, :] += row_sum(grad)
            vecg[BO : BO + 1, :] += row_sum(branch.astype(F32))
            n1s[u, rows, :] = first_grad
        gb_copy(u).start()
        grad_ctx = nt(gdb[1], wo[...]).astype(BF)
        ctx[u] = grad_ctx
        mask = key_mask(length)

        def scores(p):
            b = p % 2
            query = packed[u, :, p * LANE : (p + 1) * LANE]
            grad = ctx[u, :, p * LANE : (p + 1) * LANE]
            split_stack(stk.at[b], packed[u, :, D + p * LANE : D + (p + 1) * LANE])
            split_stack(stv.at[b], packed[u, :, 2 * D + p * LANE : 2 * D + (p + 1) * LANE])
            rhs[b, :SEG, :LANE] = grad
            rhs[b, SEG:, LANE:] = query
            sc[b] = nt(query, stk[b])
            sd[b] = nt(grad, stv[b])

        scores(0)
        for p in range(PAIRS):
            b = p % 2
            base = b * 2 * SEG
            if p + 1 < PAIRS:
                scores(p + 1)
            for rows in BLOCKS:
                for h in range(2):
                    cols = slice(h * SEG, (h + 1) * SEG)
                    one = slice(2 * p + h, 2 * p + h + 1)
                    probs = jnp.exp2(sc[b, rows, cols] * LOG2E + mask - st[u, rows, one])
                    big[base + rows.start : base + rows.stop, cols] = probs.astype(BF)
                    sc[b, rows, cols] = probs
                    product = probs * sd[b, rows, cols]
                    third = product[:, :LANE] + product[:, LANE : 2 * LANE] + product[:, 2 * LANE :]
                    high = third.astype(BF)
                    at = 2 * h * LANE
                    parts[b, rows, at : at + LANE] = high
                    parts[b, rows, at + LANE : at + 2 * LANE] = (third - high.astype(F32)).astype(BF)
            for h in range(2):
                delta[b, h] = nn(parts[b, :, 2 * h * LANE : 2 * (h + 1) * LANE], ones)
            for rows in BLOCKS:
                for h in range(2):
                    for third in range(3):
                        cols = slice(h * SEG + third * LANE, h * SEG + (third + 1) * LANE)
                        big[base + SEG + rows.start : base + SEG + rows.stop, cols] = (
                            sc[b, rows, cols] * (sd[b, rows, cols] - delta[b, h, rows, :])
                        ).astype(BF)
            packed[u, :, p * LANE : (p + 1) * LANE] = (
                nn(big[base + SEG : base + 2 * SEG, :], stk[b]) * 0.125
            ).astype(BF)
            both = tn(big[base : base + 2 * SEG, :], rhs[b])
            packed[u, :, D + p * LANE : D + (p + 1) * LANE] = jnp.where(
                low, both[:SEG, LANE:], both[SEG:, LANE:]
            ).astype(BF)
            packed[u, :, 2 * D + p * LANE : 2 * D + (p + 1) * LANE] = jnp.where(
                low, both[:SEG, :LANE], both[SEG:, :LANE]
            ).astype(BF)
        pltpu.make_async_copy(packed.at[u], gps.at[u], gp_sem.at[u]).start()
        for rows in BLOCKS:
            vecg[BQ : BQ + 1, :] += row_sum(packed[u, rows, :D].astype(F32))
            vecg[BV : BV + 1, :] += row_sum(packed[u, rows, 2 * D :].astype(F32))
        sd[0] = nt(packed[u], wq[...])

        @pl.when((turn == 2) & first)
        def _():
            back_copy(u).wait_send()

        @pl.when((turn == 3) & first)
        def _():
            back_here(u).wait()

        @pl.when((turn >= 2) & first)
        def _():
            tail_copy(u + 2, buf).wait_send()

        @pl.when((turn >= 2) & second)
        def _():
            grad_copy(u, buf).wait_send()

        for rows in BLOCKS:
            outb[buf, rows, :] = (n1s[u, rows, :] + sd[0, rows, :]).astype(BF)

        @pl.when(second)
        def _():
            grad_copy(u, buf).start()

        @pl.when(first)
        def _():
            tail_copy(u, buf).start()

        @pl.when(first & (u < 2))
        def _():
            memg[...] += nn(tail_matrix(False), outb[buf, SEG - TAIL :, :])

        @pl.when(first & (item == 1))
        def _():
            back_copy(u).start()

        @pl.when(first & (item == 0))
        def _():
            back_here(u).start()

        return carry

    lax.fori_loop(0, UNITS, backward_turn, 0)

    gd_copy(0).wait()
    gb_copy(0).wait()
    gu_copy(0).wait()
    for u in range(UNITS):
        pltpu.make_async_copy(xin.at[u], xs.at[u], x_sem.at[u]).wait()
        pltpu.make_async_copy(packed.at[u], gps.at[u], gp_sem.at[u]).wait()

    @pl.when(first)
    def _():
        for buf in range(2):
            tail_copy(buf, buf).wait_send()
            top_copy(2 * buf).wait_recv()
        back_copy(1).wait_send()
        back_here(0).wait()
        c_away[0].wait_send()
        m_away.wait_send()

    @pl.when(second)
    def _():
        for buf in range(2):
            grad_copy(buf, buf).wait_send()
            tail_copy(buf, buf).wait_recv()
            memg[...] += nn(tail_matrix(False), trx[buf])
            back_copy(2 * buf + 1).wait_recv()


def relay(operands):
    rows = (UNITS, SEG, D)
    shape = jax.ShapeDtypeStruct
    hbm = pl.BlockSpec(memory_space=pl.ANY)
    vmem = pl.BlockSpec(memory_space=pltpu.VMEM)
    results = (
        shape(rows, BF),
        shape(rows, BF),
        shape(rows, BF),
        shape((UNITS, 4 * SEG, D), BF),
        shape((2, SEG, D), BF),
        shape(rows, BF),
        shape((UNITS, SEG, FF), BF),
        shape(rows, BF),
        shape((UNITS, SEG, 3 * D), BF),
        shape((2, SEG, D), BF),
        shape((UNITS - 1, SEG, FF), F32),
        shape((16, D), F32),
        shape((TAIL, D), F32),
    )
    scratch = [
        pltpu.VMEM((D, 3 * D), BF),
        pltpu.VMEM((D, D), BF),
        pltpu.VMEM((D, FF), BF),
        pltpu.VMEM((FF, D), BF),
        pltpu.VMEM((16, D), F32),
        pltpu.VMEM(rows, BF),
        pltpu.VMEM(rows, BF),
        pltpu.VMEM((2, TAIL, D), BF),
        pltpu.VMEM((4, 16, 2 * LANE), BF),
        pltpu.VMEM((TAIL, D), BF),
        pltpu.VMEM((UNITS, TAIL, D), BF),
        pltpu.VMEM((UNITS, SEG, 3 * D), BF),
        pltpu.VMEM((UNITS, SEG, LANE), F32),
        pltpu.VMEM(rows, F32),
        pltpu.VMEM(rows, F32),
        pltpu.VMEM((SEG, FF), F32),
        pltpu.VMEM((SEG, FF), BF),
        pltpu.VMEM(rows, BF),
        pltpu.VMEM((2, SEG, D), F32),
        pltpu.VMEM((2, SEG, D), F32),
        pltpu.VMEM((4 * SEG, D), BF),
        pltpu.VMEM((2, 2 * SEG, LANE), BF),
        pltpu.VMEM((2, 2 * SEG, LANE), BF),
        pltpu.VMEM((2, 2 * SEG, 2 * LANE), BF),
        pltpu.VMEM((SEG, D), BF),
        pltpu.VMEM((2, SEG, D), BF),
        pltpu.VMEM((2, SEG, D), BF),
        pltpu.VMEM((2, 2, SEG, LANE), F32),
        pltpu.VMEM((2, SEG, 4 * LANE), BF),
    ]
    counts = [5, 5, 5, 3, 3, 3, 2, 4, 4, 4, 2, 4, 4, 4, 0, 4, 0, 0, 2, 2, 2, 4, 1, 2, 1, 2, 2]
    scratch += [pltpu.SemaphoreType.DMA((n,)) if n else pltpu.SemaphoreType.DMA for n in counts]
    scratch += [pltpu.SemaphoreType.REGULAR]
    smem = pl.BlockSpec(memory_space=pltpu.SMEM)
    in_specs = [hbm, hbm, vmem, vmem, smem, smem, hbm, hbm, hbm, hbm, hbm]
    return pl.pallas_call(
        relay_kernel,
        out_shape=results,
        in_specs=in_specs,
        out_specs=tuple([hbm] * 11 + [vmem, vmem]),
        scratch_shapes=scratch,
        compiler_params=pltpu.CompilerParams(
            collective_id=0, has_side_effects=True, vmem_limit_bytes=63 * 2**20
        ),
        cost_estimate=pl.CostEstimate(flops=80 * 10**9, bytes_accessed=80 * 2**20, transcendentals=0),
    )(*operands)


BLOCKS_G = 12
CHUNK = SEG // 8
STAGES = 15
SMALL = 8 + TAIL


def reduce_kernel(
    xs,
    ctxs,
    hids,
    acts,
    gps,
    gbs,
    gus,
    gds,
    vecg,
    mem_part,
    f_qkv,
    f_o,
    f_in,
    f_out,
    small,
    xt,
    xm,
    gg,
    own,
    sent,
    tw,
    ring0,
    ring,
    fin,
    sm_tw,
    sm_rx,
    sm_tx,
    load_sem,
    tw_send,
    tw_recv,
    ring_send,
    ring_recv,
    fin_sem,
    sm_send,
    sm_recv,
):
    item = lax.axis_index("items")
    place = lax.axis_index("pipe")
    member = lax.rem(place, 2)
    twin = {"pipe": place + 1 - 2 * member}
    x_at, z_at = lax.rem(item, 2), item // 2
    at = x_at * (7 - z_at) + (1 - x_at) * z_at
    turn = 1 - 2 * member
    logical = (1 - member) * at + member * (7 - at)

    def item_of(position):
        p = lax.rem(position + 8, 8)
        up = p // 4
        return up * (2 * (7 - p) + 1) + (1 - up) * 2 * p

    ahead = {"items": item_of(at + turn)}
    behind = {"items": item_of(at - turn)}
    rounds = [
        {"items": item + 1 - 2 * x_at},
        {"items": item + 2 - 4 * lax.rem(z_at, 2)},
        {"items": item + 4 - 8 * (z_at // 2)},
    ]

    barrier = pltpu.get_barrier_semaphore()
    for to in [twin, ahead, behind, *rounds]:
        pl.semaphore_signal(barrier, inc=1, device_id=to, device_id_type=MESH)
    pl.semaphore_wait(barrier, 6)

    def remote(src, dst, send, recv, to):
        return pltpu.make_async_remote_copy(
            src_ref=src, dst_ref=dst, send_sem=send, recv_sem=recv, device_id=to, device_id_type=MESH
        )

    def loads(left, right, theirs_rows, mine_rows, cols, slot):
        rows_t, col_t = theirs_rows
        rows_m, col_m = mine_rows
        return [
            pltpu.make_async_copy(left.at[:, rows_t, col_t], xt.at[slot], load_sem.at[slot, 0]),
            pltpu.make_async_copy(left.at[:, rows_m, col_m], xm.at[slot], load_sem.at[slot, 1]),
            pltpu.make_async_copy(right.at[:, :, cols], gg.at[slot], load_sem.at[slot, 2]),
        ]

    def aligned(start, size):
        return pl.ds(pl.multiple_of(start, SEG), size)

    def start_loads(b, slot):
        def go(left, right, pick, col):
            for copy in loads(left, right, pick(1 - member), pick(member), aligned(col * D, D), slot):
                copy.start()

        def flat(who):
            return aligned(0, SEG), aligned(who * SEG, SEG)

        @pl.when(b < 4)
        def _():
            def pick(who):
                return aligned((2 * who + b // 2) * SEG, SEG), aligned(lax.rem(b, 2) * SEG, SEG)

            go(acts, gds, pick, 0)

        @pl.when((b >= 4) & (b < 8))
        def _():
            go(hids, gus, flat, b - 4)

        @pl.when(b == 8)
        def _():
            go(ctxs, gbs, flat, 0)

        @pl.when(b >= 9)
        def _():
            go(xs, gps, flat, b - 9)

    def wait_loads(slot):
        zero = aligned(0, SEG)
        for copy in loads(xs, gds, (zero, zero), (zero, zero), aligned(0, D), slot):
            copy.wait()

    def twin_copy(b, slot):
        return remote(sent.at[slot], tw.at[b], tw_send.at[slot], tw_recv.at[b], twin)

    def rows_of(c):
        return pl.ds(pl.multiple_of(c * CHUNK, 16), CHUNK)

    def ring_copy(b, s, src, dst):
        return remote(src, dst, ring_send.at[b, s], ring_recv.at[b, s], ahead)

    def ring_wait(b, s):
        ring_copy(b, s, ring0.at[b], ring0.at[b]).wait_recv()

    def out_copy(b, go):
        @pl.when(b < 4)
        def _():
            go(f_out.at[aligned(b * SEG, SEG)])

        @pl.when((b >= 4) & (b < 8))
        def _():
            go(f_in.at[:, aligned((b - 4) * D, D)])

        @pl.when(b == 8)
        def _():
            go(f_o.at[...])

        @pl.when(b >= 9)
        def _():
            go(f_qkv.at[:, aligned((b - 9) * D, D)])

    def stage(b, s):
        c = lax.rem(logical - s + 16, 8)
        rows = rows_of(c)

        def part():
            return own[b, rows, :] + tw[b, rows, :].astype(F32)

        @pl.when(s == 0)
        def _():
            twin_copy(b, 0).wait_recv()
            ring0[b] = part().astype(BF)
            ring_copy(b, 0, ring0.at[b], ring.at[b, 0]).start()

        @pl.when(s > 0)
        def _():
            ring_wait(b, s - 1)

        @pl.when((s > 0) & (s < 7))
        def _():
            total = ring[b, s - 1].astype(F32) + part()
            ring[b, s - 1] = total.astype(BF)
            ring_copy(b, s, ring.at[b, s - 1], ring.at[b, s]).start()

        @pl.when(s == 7)
        def _():
            fin[b, rows, :] = (ring[b, 6].astype(F32) + part()).astype(BF)

        @pl.when((s >= 7) & (s < STAGES - 1))
        def _():
            ring_copy(b, s, fin.at[b, rows], fin.at[b, rows]).start()

        @pl.when(s == STAGES - 1)
        def _():
            out_copy(b, lambda dst: pltpu.make_async_copy(fin.at[b], dst, fin_sem.at[b]).start())

    def small_twin():
        return remote(sm_tx.at[0], sm_tw, sm_send.at[0], sm_recv.at[0], twin)

    def small_round(k):
        return remote(small, sm_rx.at[k], sm_send.at[k + 1], sm_recv.at[k + 1], rounds[k])

    start_loads(0, 0)
    eight = pl.ds(pl.multiple_of((1 - member) * 8, 8), 8)
    mine8 = pl.ds(pl.multiple_of(member * 8, 8), 8)
    sm_tx[0, :8, :] = vecg[eight, :]
    sm_tx[0, 8:, :] = mem_part[...]
    small[:8, :] = vecg[mine8, :]
    small[8:, :] = mem_part[...]
    small_twin().start()

    def step(i, carry):
        slot = lax.rem(i, 2)

        @pl.when(i < BLOCKS_G)
        def _():
            wait_loads(slot)

            @pl.when(i + 1 < BLOCKS_G)
            def _():
                start_loads(i + 1, 1 - slot)

            @pl.when(i >= 2)
            def _():
                twin_copy(i - 2, slot).wait_send()

            right = gg[slot].reshape(UNITS * SEG, D)
            sent[slot] = tn(xt[slot].reshape(UNITS * SEG, SEG), right).astype(BF)
            twin_copy(i, slot).start()
            own[i] = tn(xm[slot].reshape(UNITS * SEG, SEG), right)

        for k in range(4):

            @pl.when(i == 2 * k + 2)
            def _():
                if k == 0:
                    small_twin().wait()
                    small[...] = small[...] + sm_tw[...]
                else:
                    small_round(k - 1).wait()
                    small[...] = small[...] + sm_rx[k - 1]
                if k < 3:
                    small_round(k).start()

        first_b = jnp.maximum(i - STAGES, 0)
        last_b = jnp.minimum(i, BLOCKS_G)

        def serve(b, inner):
            stage(b, i - 1 - b)
            return inner

        lax.fori_loop(first_b, last_b, serve, 0)
        return carry

    lax.fori_loop(0, BLOCKS_G + STAGES, step, 0)

    twin_copy(0, 0).wait_send()
    twin_copy(1, 1).wait_send()

    def drain(b, carry):
        def one(s, inner):
            ring_copy(b, s, ring0.at[b], ring0.at[b]).wait_send()
            return inner

        lax.fori_loop(0, STAGES - 1, one, 0)
        out_copy(b, lambda dst: pltpu.make_async_copy(fin.at[b], dst, fin_sem.at[b]).wait())
        return carry

    lax.fori_loop(0, BLOCKS_G, drain, 0)


def reduce_grads(operands):
    shape = jax.ShapeDtypeStruct
    hbm = pl.BlockSpec(memory_space=pl.ANY)
    vmem = pl.BlockSpec(memory_space=pltpu.VMEM)
    dma = pltpu.SemaphoreType.DMA
    return pl.pallas_call(
        reduce_kernel,
        out_shape=(
            shape((SEG, 3 * D), BF),
            shape((SEG, D), BF),
            shape((SEG, FF), BF),
            shape((FF // 2, D), BF),
            shape((SMALL, D), F32),
        ),
        in_specs=[hbm] * 8 + [vmem, vmem],
        out_specs=(hbm, hbm, hbm, hbm, vmem),
        scratch_shapes=[
            pltpu.VMEM((2, UNITS, SEG, SEG), BF),
            pltpu.VMEM((2, UNITS, SEG, SEG), BF),
            pltpu.VMEM((2, UNITS, SEG, D), BF),
            pltpu.VMEM((BLOCKS_G, SEG, D), F32),
            pltpu.VMEM((2, SEG, D), BF),
            pltpu.VMEM((BLOCKS_G, SEG, D), BF),
            pltpu.VMEM((BLOCKS_G, CHUNK, D), BF),
            pltpu.VMEM((BLOCKS_G, 7, CHUNK, D), BF),
            pltpu.VMEM((BLOCKS_G, SEG, D), BF),
            pltpu.VMEM((SMALL, D), F32),
            pltpu.VMEM((3, SMALL, D), F32),
            pltpu.VMEM((1, SMALL, D), F32),
            dma((2, 3)),
            dma((2,)),
            dma((BLOCKS_G,)),
            dma((BLOCKS_G, STAGES - 1)),
            dma((BLOCKS_G, STAGES - 1)),
            dma((BLOCKS_G,)),
            dma((4,)),
            dma((4,)),
        ],
        compiler_params=pltpu.CompilerParams(
            collective_id=1, has_side_effects=True, vmem_limit_bytes=60 * 2**20
        ),
        cost_estimate=pl.CostEstimate(flops=22 * 10**9, bytes_accessed=64 * 2**20, transcendentals=0),
    )(*operands)


def finish_kernel(
    counts, lasts, tops, backs, tail, f_qkv, f_o, f_in, f_out, small, text, text_g, memory, mem_g, qkv_g, o_g, in_g, out_g, gains_g, biases_g
):
    step = pl.program_id(0)
    place = lax.axis_index("pipe")
    count, last = counts[place], lasts[place]
    rows = tops.shape[1]
    row = lax.broadcasted_iota(jnp.int32, (rows, D), 0) + step * rows
    for k in range(2):
        limit = jnp.where(count > 1, TEXT if k == 0 else last, last if k == 0 else 0)
        text[:, k, :] = jnp.where(row < limit, tops[k].astype(F32), 0.0)
        text_g[:, k, :] = backs[k].astype(F32)
    qkv_g[...] = f_qkv[...].astype(F32)
    o_g[...] = f_o[...].astype(F32)
    in_g[...] = f_in[...].astype(F32)
    out_g[...] = f_out[...].astype(F32)

    @pl.when(step == 0)
    def _():
        ends = tail[...].astype(F32)
        memory[0] = jnp.where(count > 1, ends[1], ends[0])[TAIL - MEM :, :]
        width = D // 4
        for index in range(4):

            @pl.when(place == index)
            def _():
                mem_g[...] = small[SMALL - MEM :, index * width : (index + 1) * width]

        gains_g[...] = small[0:1, :]
        biases_g[...] = small[1:6, :]


def finish(operands):
    shape = jax.ShapeDtypeStruct
    smem = pl.BlockSpec(memory_space=pltpu.SMEM)
    steps = 8
    row = SEG // steps

    def split(rows, cols):
        return pl.BlockSpec((rows, cols), lambda i: (i, 0))

    def whole(*size):
        return pl.BlockSpec(size, lambda i: (0,) * len(size))

    pair = pl.BlockSpec((2, row, D), lambda i: (0, i, 0))
    pair_out = pl.BlockSpec((row, 2, D), lambda i: (i, 0, 0))
    grads = [split(row, 3 * D), split(row, D), split(row, FF), split(4 * row, D)]
    counts, lasts, tops, backs, *rest = operands
    return pl.pallas_call(
        finish_kernel,
        grid=(steps,),
        out_shape=(
            shape((TEXT, 2, D), F32),
            shape((TEXT, 2, D), F32),
            shape((1, MEM, D), F32),
            shape((MEM, D // 4), F32),
            shape((SEG, 3 * D), F32),
            shape((SEG, D), F32),
            shape((SEG, FF), F32),
            shape((FF // 2, D), F32),
            shape((1, D), F32),
            shape((5, D), F32),
        ),
        in_specs=[
            smem,
            smem,
            pair,
            pair,
            pl.BlockSpec((2, TAIL, D), lambda i: (0, SEG // TAIL - 1, 0)),
            *grads,
            whole(SMALL, D),
        ],
        out_specs=(
            pair_out,
            pair_out,
            whole(1, MEM, D),
            whole(MEM, D // 4),
            *grads,
            whole(1, D),
            whole(5, D),
        ),
        compiler_params=pltpu.CompilerParams(vmem_limit_bytes=62 * 2**20),
    )(counts, lasts, tops, backs, tops, *rest)


def from_partner(x, axis, bit):
    return lax.ppermute(x, axis, [(i, i ^ 1 << bit) for i in range(lax.axis_size(axis))])


def over_rows(left, right):
    return lax.dot_general(
        left, right, (((0, 1), (0, 1)), ((), ())), preferred_element_type=F32
    )


def sum_grads(member, operands):
    xs, ctxs, hids, acts, gps, gbs, gus, gds, vecg, memg = operands
    def halves(left, right):
        size = left.shape[-1] // 2
        mine = lax.dynamic_slice_in_dim(left, member * size, size, 2)
        theirs = lax.dynamic_slice_in_dim(left, (1 - member) * size, size, 2)
        return over_rows(mine, right), over_rows(theirs, right).astype(BF)

    parts = [halves(xs, gps), halves(ctxs, gbs), halves(hids, gus)]
    blocks = acts.reshape(UNITS, 4, SEG, D)
    mine = lax.dynamic_slice_in_dim(blocks, member * 2, 2, 1)
    theirs = lax.dynamic_slice_in_dim(blocks, (1 - member) * 2, 2, 1)
    parts.append(
        (
            jnp.concatenate([over_rows(mine[:, i], gds) for i in range(2)], 0),
            jnp.concatenate([over_rows(theirs[:, i], gds) for i in range(2)], 0).astype(BF),
        )
    )
    sums = [kept + from_partner(sent, "pipe", 0).astype(F32) for kept, sent in parts]
    vec_mine = lax.dynamic_slice_in_dim(vecg, member * 8, 8, 0)
    vec_theirs = lax.dynamic_slice_in_dim(vecg, (1 - member) * 8, 8, 0)
    mine_small = jnp.concatenate([vec_mine, memg], 0)
    small = mine_small + from_partner(jnp.concatenate([vec_theirs, memg], 0), "pipe", 0)
    *grads, small = lax.psum((*sums, small), "items")
    return (*grads, small)


def per_device(
    text_in,
    memory,
    w_qkv,
    w_o,
    w_in,
    w_out,
    gains,
    biases,
    counts,
    last_lengths,
    text_cot,
    memory_cot,
):
    member = lax.axis_index("pipe") % 2
    pad = ((0, 0), (0, SEG - TEXT), (0, 0))
    x_own = jnp.pad(text_in[0], pad)
    c_own = jnp.pad(text_cot[0], pad)
    mem_own = jnp.pad(memory, ((0, 16 - MEM), (0, 2 * LANE - memory.shape[1])))
    mcot_own = jnp.pad(memory_cot[0], ((TAIL - MEM, 0), (0, 0)))
    vec_own = jnp.concatenate(
        [gains[None], biases.reshape(5, D), jnp.zeros((2, D), gains.dtype)], 0
    ).astype(F32)
    xs, ctxs, hids, acts, own_top, gds, gus, gbs, gps, own_back, _, vecg, memg = relay(
        (x_own, c_own, mem_own, mcot_own, counts, last_lengths, w_qkv, w_o, w_in, w_out, vec_own)
    )
    sum_all = reduce_grads if lax.axis_size("items") == 8 else functools.partial(sum_grads, member)
    sums = sum_all((xs, ctxs, hids, acts, gps, gbs, gus, gds, vecg, memg))
    text, text_grad, last_memory, memory_grad, *grads, gains_grad, biases_grad = finish(
        (counts, last_lengths, own_top, own_back, *sums)
    )
    return (
        text.transpose(1, 0, 2)[None],
        last_memory,
        text_grad.transpose(1, 0, 2)[None],
        memory_grad,
        *grads,
        gains_grad.reshape(D),
        biases_grad.reshape(5 * D),
    )


def solution(mesh):
    placed = (
        P(("items", "pipe"), None, None, None),
        P(None, "pipe"),
        P("pipe", None),
        P("pipe", None),
        P("pipe", None),
        P("pipe", None),
        P("pipe"),
        P("pipe"),
        P("items"),
        P("items"),
        P(("items", "pipe"), None, None, None),
        P(("items", "pipe"), None, None),
    )
    return jax.shard_map(
        per_device,
        mesh=mesh,
        in_specs=placed,
        out_specs=(
            P(("items", "pipe"), None, None, None),
            P(("items", "pipe"), None, None),
            P(("items", "pipe"), None, None, None),
            P(None, "pipe"),
            P("pipe", None),
            P("pipe", None),
            P("pipe", None),
            P("pipe", None),
            P("pipe"),
            P("pipe"),
        ),
        check_vma=False,
    )
```

```python
import functools

import jax
import jax.numpy as jnp
from jax import lax
from jax.experimental import pallas as pl
from jax.experimental.pallas import tpu as pltpu
from jax.sharding import PartitionSpec as P

D = 768
FF = 3072
MEM = 10
TEXT = 364
SEG = 384
PAIRS = 6
LANE = 128
TAIL = 32
UNITS = 4
LOG2E = 1.4426950408889634
MASKED = -1.0e9
EPS = 1e-6
MESH = pl.DeviceIdType.MESH
BF = jnp.bfloat16
F32 = jnp.float32
G1, BQ, BV, BO, N1, BD, G2, N2, BI = 0, 1, 2, 3, 4, 5, 8, 9, 10
BLOCKS = [slice(128 * b, 128 * b + 128) for b in range(3)]


def nn(left, right):
    return jnp.dot(left, right, preferred_element_type=F32)


def nt(left, right):
    return lax.dot_general(left, right, (((1,), (1,)), ((), ())), preferred_element_type=F32)


def tn(left, right):
    return lax.dot_general(left, right, (((0,), (0,)), ((), ())), preferred_element_type=F32)


def gelu_parts(up):
    t = pl.reciprocal(1.0 + (0.3275911 * 0.7071067811865476) * jnp.abs(up), approx=True)
    poly = t * (
        0.127414796
        + t * (-0.142248368 + t * (0.7107068705 + t * (-0.7265760135 + t * 0.5307027145)))
    )
    bell = jnp.exp2(up * up * (-0.5 * LOG2E))
    half = poly * bell
    phi = jnp.where(up >= 0, 1.0 - half, half)
    return up * phi, phi + up * bell * 0.3989422804014327


def norm_parts(values):
    centre = values - jnp.mean(values, axis=-1, keepdims=True)
    inverse = lax.rsqrt(jnp.mean(centre * centre, axis=-1, keepdims=True) + EPS)
    return centre * inverse, inverse


def norm_back(grad, normed, inverse, gain):
    scaled = grad * gain
    middle = jnp.mean(scaled, axis=-1, keepdims=True)
    along = jnp.mean(scaled * normed, axis=-1, keepdims=True)
    return inverse * (scaled - middle - normed * along)


def row_sum(values):
    return jnp.sum(values, axis=0, keepdims=True)


def split_stack(dst, src):
    low = lax.broadcasted_iota(jnp.int32, (SEG, LANE), 1) < 64
    zero = jnp.zeros((SEG, LANE), BF)
    dst[:SEG, :LANE] = jnp.where(low, src, zero)
    dst[SEG:, :LANE] = jnp.where(low, zero, src)


def tail_matrix(spread):
    row = lax.broadcasted_iota(jnp.int32, (TAIL, TAIL), 0)
    col = lax.broadcasted_iota(jnp.int32, (TAIL, TAIL), 1)
    if spread:
        keep = ((row >= 22) & (col == row)) | ((row >= 12) & (row < 22) & (col == row + 10))
    else:
        keep = (row >= 22) & ((col == row) | (col == row - 10))
    return jnp.where(keep, 1.0, 0.0).astype(BF)


def relay_kernel(
    x_own,
    c_own,
    mem_own,
    mcot_own,
    counts,
    lasts,
    w_qkv,
    w_o,
    w_in,
    w_out,
    vec_own,
    xs,
    ctxs,
    hids,
    acts,
    own_top,
    gds,
    gus,
    gbs,
    gps,
    own_back,
    slopes,
    vecg,
    memg,
    wq,
    wo,
    wi,
    wd,
    vec,
    xin,
    gsl,
    mcs,
    mem_rx,
    mem0,
    trx,
    packed,
    st,
    n1s,
    n2s,
    dgf,
    gub,
    ctx,
    sc,
    sd,
    big,
    stk,
    stv,
    rhs,
    hid,
    outb,
    gdb,
    delta,
    parts,
    w_local,
    w_send,
    w_recv,
    e_local,
    e_send,
    e_recv,
    mid_send,
    mid_recv,
    tail_send,
    tail_recv,
    grad_send,
    grad_recv,
    x_sem,
    ctx_sem,
    gu_sem,
    gp_sem,
    hid_sem,
    act_sem,
    gd_sem,
    dg_sem,
    mem_send,
    mem_recv,
    top_send,
    top_recv,
    back_send,
    back_recv,
    res_sem,
    lag,
):
    place = lax.axis_index("pipe")
    first = place < 2
    member = lax.rem(place, 2)
    twin = {"pipe": place + 1 - 2 * member}
    other = {"pipe": lax.rem(place + 2, 4)}
    across = {"pipe": 3 - place}
    second = jnp.logical_not(first)

    barrier = pltpu.get_barrier_semaphore()
    for to in (twin, other, across):
        pl.semaphore_signal(barrier, inc=1, device_id=to, device_id_type=MESH)
    pl.semaphore_wait(barrier, 3)

    def remote(src, dst, send, recv, to):
        return pltpu.make_async_remote_copy(
            src_ref=src, dst_ref=dst, send_sem=send, recv_sem=recv, device_id=to, device_id_type=MESH
        )

    halves = (
        (vec_own, vec, 8),
        (w_qkv, wq, D // 2),
        (w_o, wo, D // 2),
        (w_in, wi, D // 2),
        (w_out, wd, FF // 2),
    )
    locals_, sends, recvs = [], [], []
    for index, (src, dst, rows) in enumerate(halves):
        mine = dst.at[pl.ds(pl.multiple_of(member * rows, rows), rows)]
        theirs = dst.at[pl.ds(pl.multiple_of((1 - member) * rows, rows), rows)]
        locals_.append(pltpu.make_async_copy(src, mine, w_local.at[index]))
        sends.append(remote(src, mine, w_send.at[index], w_recv.at[index], twin))
        recvs.append(remote(src, theirs, w_send.at[index], w_recv.at[index], twin))
    x_home = [pltpu.make_async_copy(x_own.at[k], xin.at[2 * k], e_local.at[k]) for k in range(2)]
    x_away = [
        remote(x_own.at[k], xin.at[2 * k + 1], e_send.at[k], e_recv.at[k], other) for k in range(2)
    ]
    c_home = [
        pltpu.make_async_copy(c_own.at[k], gsl.at[2 * k + 1], e_local.at[k]) for k in range(2)
    ]
    c_away = [
        remote(c_own.at[k], gsl.at[2 * k], e_send.at[k], e_recv.at[k], other) for k in range(2)
    ]
    m_home = pltpu.make_async_copy(mcot_own, mcs.at[1], e_local.at[2])
    m_away = remote(mcot_own, mcs.at[0], e_send.at[2], e_recv.at[2], other)
    mem_twin = remote(mem_own, mem_rx.at[place], mem_send.at[0], mem_recv.at[place], twin)
    mem_other = remote(mem_own, mem_rx.at[place], mem_send.at[0], mem_recv.at[place], other)
    mem_across = remote(mem_own, mem_rx.at[place], mem_send.at[1], mem_recv.at[place], across)

    def start_weights(index):
        locals_[index].start()
        sends[index].start()

    def wait_weights(index):
        locals_[index].wait()
        recvs[index].wait_recv()

    start_weights(0)
    start_weights(1)

    @pl.when(first)
    def _():
        for copy in x_home:
            copy.start()
        mem_twin.start()

    @pl.when(second)
    def _():
        mem_other.start()
        mem_across.start()
        x_away[0].start()
        for copy in c_home:
            copy.start()
        m_home.start()

    rhs[...] = jnp.zeros_like(rhs)
    ones = jnp.ones((2 * LANE, LANE), BF)
    vecg[...] = jnp.zeros_like(vecg)
    memg[...] = jnp.zeros_like(memg)
    low = lax.broadcasted_iota(jnp.int32, (SEG, LANE), 1) < 64

    @pl.when(first)
    def _():
        mem_twin.wait_send()
        for index in range(4):

            @pl.when(index != place)
            def _():
                remote(mem_own, mem_rx.at[index], mem_send.at[0], mem_recv.at[index], twin).wait_recv()

            @pl.when(index == place)
            def _():
                mem_rx[index] = mem_own[...]

        row = lax.broadcasted_iota(jnp.int32, (TAIL, 16), 0)
        col = lax.broadcasted_iota(jnp.int32, (TAIL, 16), 1)
        twice = ((col == row - 12) | (col == row - 22)) & (col < MEM)
        spread = jnp.where(twice, 1.0, 0.0).astype(BF)
        total = jnp.zeros((TAIL, D), F32)
        for index in range(4):
            source = lax.broadcasted_iota(jnp.int32, (2 * LANE, D), 0)
            target = lax.broadcasted_iota(jnp.int32, (2 * LANE, D), 1)
            move = (target == source + index * (D // 4)) & (source < D // 4)
            rows = nn(spread, mem_rx[index]).astype(BF)
            total = total + nn(rows, jnp.where(move, 1.0, 0.0).astype(BF))
        mem0[...] = total.astype(BF)

    def unit_scalars(u):
        item = lax.rem(u, 2)
        count = counts[member + 2 * item]
        last = lasts[member + 2 * item]
        length = jnp.where((u < 2) & (count > 1), TEXT, last)
        return count, length

    def key_mask(length):
        key = lax.broadcasted_iota(jnp.int32, (1, SEG), 1)
        return jnp.where((key >= TEXT) | (key < length), 0.0, MASKED)

    def v(row):
        return vec[row : row + 1, :]

    def top_copy(u):
        return remote(
            outb.at[0], own_top.at[u // 2], top_send.at[0], top_recv.at[u // 2], other
        )

    def top_here(u):
        return pltpu.make_async_copy(outb.at[1], own_top.at[u // 2], res_sem.at[0])

    def back_copy(u):
        return remote(
            outb.at[1], own_back.at[u // 2], back_send.at[0], back_recv.at[u // 2], other
        )

    def back_here(u):
        return pltpu.make_async_copy(outb.at[0], own_back.at[u // 2], res_sem.at[1])

    def mid_copy(u, buf):
        return remote(outb.at[buf], xin.at[u], mid_send.at[buf], mid_recv.at[u], other)

    def grad_copy(u, buf):
        return remote(outb.at[buf], gsl.at[u], grad_send.at[buf], grad_recv.at[u], other)

    def tail_copy(slot, buf):
        src = outb.at[buf, pl.ds(SEG - TAIL, TAIL)]
        return remote(src, trx.at[slot], tail_send.at[slot], tail_recv.at[slot], other)

    def forward_turn(u, carry):
        item = lax.rem(u, 2)
        buf = lax.rem(u, 2)

        @pl.when(u == 0)
        def _():
            wait_weights(0)
            wait_weights(1)
            for index in (2, 3, 4):
                start_weights(index)

        @pl.when(first & (u == 0))
        def _():
            for copy in x_home:
                copy.wait()

        @pl.when(first & (u == 1))
        def _():
            x_away[0].wait_recv()

        @pl.when(first & (u == 3))
        def _():
            x_away[1].wait_recv()

        @pl.when(second & (u == 0))
        def _():
            x_away[0].wait_send()
            x_away[1].start()

        @pl.when(first & (u < 2))
        def _():
            xin[u, SEG - TAIL :, :] = xin[u, SEG - TAIL :, :] + mem0[...]

        @pl.when(first & (u >= 2))
        def _():
            tail_copy(item, buf).wait_recv()
            spread = nn(tail_matrix(True), trx[item]).astype(BF)
            xin[u, SEG - TAIL :, :] = xin[u, SEG - TAIL :, :] + spread

        @pl.when(second)
        def _():
            mid_copy(u, buf).wait_recv()

        pltpu.make_async_copy(xin.at[u], xs.at[u], x_sem.at[u]).start()

        count, length = unit_scalars(u)
        mask = key_mask(length)
        x = xin[u]
        packed[u, :, :D] = (nn(x, wq[:, :D]) + v(BQ)).astype(BF) * 0.125
        packed[u, :, D : 2 * D] = nn(x, wq[:, D : 2 * D]).astype(BF)
        packed[u, :, 2 * D :] = (nn(x, wq[:, 2 * D :]) + v(BV)).astype(BF)

        @pl.when(u > 0)
        def _():
            hid_copy(u).wait()
            act_copy(u).wait()
            slope_out(u - 1).wait()

        def scores(p):
            b = p % 2
            split_stack(stk.at[b], packed[u, :, D + p * LANE : D + (p + 1) * LANE])
            split_stack(stv.at[b], packed[u, :, 2 * D + p * LANE : 2 * D + (p + 1) * LANE])
            sc[b] = nt(packed[u, :, p * LANE : (p + 1) * LANE], stk[b])

        scores(0)
        for p in range(PAIRS):
            b = p % 2
            if p + 1 < PAIRS:
                scores(p + 1)
            for rows in BLOCKS:
                for h in range(2):
                    cols = slice(h * SEG, (h + 1) * SEG)
                    scaled = sc[b, rows, cols] * LOG2E + mask
                    top = jnp.max(scaled, axis=-1, keepdims=True)
                    raised = jnp.exp2(scaled - top)
                    total = jnp.sum(raised, axis=-1, keepdims=True)
                    big[b * 2 * SEG + rows.start : b * 2 * SEG + rows.stop, cols] = (
                        raised * (1.0 / total)
                    ).astype(BF)
                    st[u, rows, 2 * p + h : 2 * p + h + 1] = top + jnp.log2(total)
            ctx[u, :, p * LANE : (p + 1) * LANE] = nn(
                big[b * 2 * SEG : b * 2 * SEG + SEG, :], stv[b]
            ).astype(BF)
        pltpu.make_async_copy(ctx.at[u], ctxs.at[u], ctx_sem.at[u]).start()

        @pl.when(u == 0)
        def _():
            wait_weights(2)

        sd[0] = nn(ctx[u], wo[...])
        for rows in BLOCKS:
            normed, inverse = norm_parts(xin[u, rows, :].astype(F32) + sd[0, rows, :] + v(BO))
            n1s[u, rows, :] = normed
            st[u, rows, 12:13] = inverse
            hid[rows, :] = (normed * v(G1) + v(N1)).astype(BF)
        hid_copy(u).start()

        @pl.when(u == 0)
        def _():
            wait_weights(3)
            wait_weights(4)

        def up(j):
            sd[j % 2] = nn(hid[...], wi[:, j * D : (j + 1) * D])

        up(0)
        for j in range(4):
            if j + 1 < 4:
                up(j + 1)
            for rows in BLOCKS:
                act, slope = gelu_parts(sd[j % 2, rows, :] + v(BI + j))
                big[j * SEG + rows.start : j * SEG + rows.stop, :] = act.astype(BF)
                dgf[rows, j * D : (j + 1) * D] = slope
            part = nn(big[j * SEG : (j + 1) * SEG, :], wd[j * D : (j + 1) * D, :])
            sc[0] = part if j == 0 else sc[0] + part
        act_copy(u).start()

        @pl.when(u < UNITS - 1)
        def _():
            slope_out(u).start()

        @pl.when(second & (u == 2))
        def _():
            top_copy(u).wait_send()

        @pl.when(second & (u == 3))
        def _():
            top_here(u).wait()

        @pl.when((u >= 2) & first)
        def _():
            mid_copy(u, buf).wait_send()

        @pl.when((u >= 2) & second)
        def _():
            tail_copy(item, buf).wait_send()

        for rows in BLOCKS:
            hidden = n1s[u, rows, :] * v(G1) + v(N1)
            normed, inverse = norm_parts(hidden + sc[0, rows, :] + v(BD))
            n2s[u, rows, :] = normed
            st[u, rows, 13:14] = inverse
            outb[buf, rows, :] = (normed * v(G2) + v(N2)).astype(BF)

        @pl.when(first)
        def _():
            mid_copy(u, buf).start()

        @pl.when(second & (u < 2))
        def _():
            tail_copy(item, buf).start()

        @pl.when(second & (item == 0))
        def _():
            top_copy(u).start()

        @pl.when(second & (item == 1))
        def _():
            top_here(u).start()

        return carry

    def hid_copy(u):
        return pltpu.make_async_copy(hid, hids.at[u], hid_sem)

    def act_copy(u):
        return pltpu.make_async_copy(big, acts.at[u], act_sem)

    def slope_out(u):
        return pltpu.make_async_copy(dgf, slopes.at[u], dg_sem.at[0])

    def slope_in(u):
        return pltpu.make_async_copy(slopes.at[u], dgf, dg_sem.at[1])

    lax.fori_loop(0, UNITS, forward_turn, 0)

    hid_copy(0).wait()
    act_copy(0).wait()
    for u in range(UNITS):
        pltpu.make_async_copy(ctx.at[u], ctxs.at[u], ctx_sem.at[u]).wait()
    for index in range(5):
        sends[index].wait_send()

    @pl.when(first)
    def _():
        for buf in range(2):
            mid_copy(2 + buf, buf).wait_send()
        pl.semaphore_signal(lag, inc=1, device_id=twin, device_id_type=MESH)
        pl.semaphore_wait(lag, 1)
        c_away[1].start()
        m_away.start()
        c_away[1].wait_send()
        c_away[0].start()

    @pl.when(second)
    def _():
        top_copy(2).wait_send()
        top_here(3).wait()
        x_away[1].wait_send()
        mem_other.wait_send()
        mem_across.wait_send()
        for copy in c_home:
            copy.wait()
        m_home.wait()

    def gd_copy(u):
        return pltpu.make_async_copy(gdb.at[0], gds.at[u], gd_sem.at[0])

    def gb_copy(u):
        return pltpu.make_async_copy(gdb.at[1], gbs.at[u], gd_sem.at[1])

    def gu_copy(u):
        return pltpu.make_async_copy(gub, gus.at[u], gu_sem)

    def backward_turn(turn, carry):
        u = UNITS - 1 - turn
        item = lax.rem(u, 2)
        buf = lax.rem(u, 2)

        @pl.when(first)
        def _():
            grad_copy(u, buf).wait_recv()

        @pl.when(second & (u == 2))
        def _():
            c_away[1].wait_recv()
            m_away.wait_recv()

        @pl.when(second & (u == 0))
        def _():
            c_away[0].wait_recv()

        count, length = unit_scalars(u)
        limit = jnp.where(first, SEG, jnp.where((u < 2) | (count > 1), length, 0))
        row = lax.broadcasted_iota(jnp.int32, (SEG, D), 0)
        sd[0] = jnp.where(row < limit, gsl[u].astype(F32), 0.0)
        both_live = jnp.where(count > 1, 1.0, 0.0)

        @pl.when(second & (u >= 2))
        def _():
            sd[0, SEG - TAIL :, :] = sd[0, SEG - TAIL :, :] + mcs[item].astype(F32) * both_live

        @pl.when(second & (u < 2))
        def _():
            tail_copy(u + 2, buf).wait_recv()
            arrived = nn(tail_matrix(False), trx[u + 2])
            sd[0, SEG - TAIL :, :] = (
                sd[0, SEG - TAIL :, :]
                + arrived * both_live
                + mcs[item].astype(F32) * (1.0 - both_live)
            )

        @pl.when(turn > 0)
        def _():
            gd_copy(u).wait()
            gb_copy(u).wait()
            gu_copy(u).wait()
            slope_in(u).wait()

        for rows in BLOCKS:
            grad = sd[0, rows, :]
            normed = n2s[u, rows, :]
            second_grad = norm_back(grad, normed, st[u, rows, 13:14], v(G2))
            sc[0, rows, :] = second_grad
            down = second_grad.astype(BF)
            gdb[0, rows, :] = down
            vecg[G2 : G2 + 1, :] += row_sum(grad * normed)
            vecg[N2 : N2 + 1, :] += row_sum(grad)
            vecg[BD : BD + 1, :] += row_sum(down.astype(F32))
        gd_copy(u).start()
        for j in range(4):
            sd[j % 2] = nt(gdb[0], wd[j * D : (j + 1) * D, :])
            for rows in BLOCKS:
                cols = slice(j * D, (j + 1) * D)
                lifted = (sd[j % 2, rows, :] * dgf[rows, cols]).astype(BF)
                gub[rows, cols] = lifted
                vecg[BI + j : BI + j + 1, :] += row_sum(lifted.astype(F32))
        gu_copy(u).start()

        @pl.when(u > 0)
        def _():
            slope_in(u - 1).start()

        sd[0] = nt(gub[...], wi[...])
        for rows in BLOCKS:
            grad = sc[0, rows, :] + sd[0, rows, :]
            normed = n1s[u, rows, :]
            first_grad = norm_back(grad, normed, st[u, rows, 12:13], v(G1))
            branch = first_grad.astype(BF)
            gdb[1, rows, :] = branch
            vecg[G1 : G1 + 1, :] += row_sum(grad * normed)
            vecg[N1 : N1 + 1, :] += row_sum(grad)
            vecg[BO : BO + 1, :] += row_sum(branch.astype(F32))
            n1s[u, rows, :] = first_grad
        gb_copy(u).start()
        grad_ctx = nt(gdb[1], wo[...]).astype(BF)
        ctx[u] = grad_ctx
        mask = key_mask(length)

        def scores(p):
            b = p % 2
            query = packed[u, :, p * LANE : (p + 1) * LANE]
            grad = ctx[u, :, p * LANE : (p + 1) * LANE]
            split_stack(stk.at[b], packed[u, :, D + p * LANE : D + (p + 1) * LANE])
            split_stack(stv.at[b], packed[u, :, 2 * D + p * LANE : 2 * D + (p + 1) * LANE])
            rhs[b, :SEG, :LANE] = grad
            rhs[b, SEG:, LANE:] = query
            sc[b] = nt(query, stk[b])
            sd[b] = nt(grad, stv[b])

        scores(0)
        for p in range(PAIRS):
            b = p % 2
            base = b * 2 * SEG
            if p + 1 < PAIRS:
                scores(p + 1)
            for rows in BLOCKS:
                for h in range(2):
                    cols = slice(h * SEG, (h + 1) * SEG)
                    one = slice(2 * p + h, 2 * p + h + 1)
                    probs = jnp.exp2(sc[b, rows, cols] * LOG2E + mask - st[u, rows, one])
                    big[base + rows.start : base + rows.stop, cols] = probs.astype(BF)
                    sc[b, rows, cols] = probs
                    product = probs * sd[b, rows, cols]
                    third = product[:, :LANE] + product[:, LANE : 2 * LANE] + product[:, 2 * LANE :]
                    high = third.astype(BF)
                    at = 2 * h * LANE
                    parts[b, rows, at : at + LANE] = high
                    parts[b, rows, at + LANE : at + 2 * LANE] = (third - high.astype(F32)).astype(BF)
            for h in range(2):
                delta[b, h] = nn(parts[b, :, 2 * h * LANE : 2 * (h + 1) * LANE], ones)
            for rows in BLOCKS:
                for h in range(2):
                    for third in range(3):
                        cols = slice(h * SEG + third * LANE, h * SEG + (third + 1) * LANE)
                        big[base + SEG + rows.start : base + SEG + rows.stop, cols] = (
                            sc[b, rows, cols] * (sd[b, rows, cols] - delta[b, h, rows, :])
                        ).astype(BF)
            packed[u, :, p * LANE : (p + 1) * LANE] = (
                nn(big[base + SEG : base + 2 * SEG, :], stk[b]) * 0.125
            ).astype(BF)
            both = tn(big[base : base + 2 * SEG, :], rhs[b])
            packed[u, :, D + p * LANE : D + (p + 1) * LANE] = jnp.where(
                low, both[:SEG, LANE:], both[SEG:, LANE:]
            ).astype(BF)
            packed[u, :, 2 * D + p * LANE : 2 * D + (p + 1) * LANE] = jnp.where(
                low, both[:SEG, :LANE], both[SEG:, :LANE]
            ).astype(BF)
        pltpu.make_async_copy(packed.at[u], gps.at[u], gp_sem.at[u]).start()
        for rows in BLOCKS:
            vecg[BQ : BQ + 1, :] += row_sum(packed[u, rows, :D].astype(F32))
            vecg[BV : BV + 1, :] += row_sum(packed[u, rows, 2 * D :].astype(F32))
        sd[0] = nt(packed[u], wq[...])

        @pl.when((turn == 2) & first)
        def _():
            back_copy(u).wait_send()

        @pl.when((turn == 3) & first)
        def _():
            back_here(u).wait()

        @pl.when((turn >= 2) & first)
        def _():
            tail_copy(u + 2, buf).wait_send()

        @pl.when((turn >= 2) & second)
        def _():
            grad_copy(u, buf).wait_send()

        for rows in BLOCKS:
            outb[buf, rows, :] = (n1s[u, rows, :] + sd[0, rows, :]).astype(BF)

        @pl.when(second)
        def _():
            grad_copy(u, buf).start()

        @pl.when(first)
        def _():
            tail_copy(u, buf).start()

        @pl.when(first & (u < 2))
        def _():
            memg[...] += nn(tail_matrix(False), outb[buf, SEG - TAIL :, :])

        @pl.when(first & (item == 1))
        def _():
            back_copy(u).start()

        @pl.when(first & (item == 0))
        def _():
            back_here(u).start()

        return carry

    lax.fori_loop(0, UNITS, backward_turn, 0)

    gd_copy(0).wait()
    gb_copy(0).wait()
    gu_copy(0).wait()
    for u in range(UNITS):
        pltpu.make_async_copy(xin.at[u], xs.at[u], x_sem.at[u]).wait()
        pltpu.make_async_copy(packed.at[u], gps.at[u], gp_sem.at[u]).wait()

    @pl.when(first)
    def _():
        for buf in range(2):
            tail_copy(buf, buf).wait_send()
            top_copy(2 * buf).wait_recv()
        back_copy(1).wait_send()
        back_here(0).wait()
        c_away[0].wait_send()
        m_away.wait_send()

    @pl.when(second)
    def _():
        for buf in range(2):
            grad_copy(buf, buf).wait_send()
            tail_copy(buf, buf).wait_recv()
            memg[...] += nn(tail_matrix(False), trx[buf])
            back_copy(2 * buf + 1).wait_recv()


def relay(operands):
    rows = (UNITS, SEG, D)
    shape = jax.ShapeDtypeStruct
    hbm = pl.BlockSpec(memory_space=pl.ANY)
    vmem = pl.BlockSpec(memory_space=pltpu.VMEM)
    results = (
        shape(rows, BF),
        shape(rows, BF),
        shape(rows, BF),
        shape((UNITS, 4 * SEG, D), BF),
        shape((2, SEG, D), BF),
        shape(rows, BF),
        shape((UNITS, SEG, FF), BF),
        shape(rows, BF),
        shape((UNITS, SEG, 3 * D), BF),
        shape((2, SEG, D), BF),
        shape((UNITS - 1, SEG, FF), F32),
        shape((16, D), F32),
        shape((TAIL, D), F32),
    )
    scratch = [
        pltpu.VMEM((D, 3 * D), BF),
        pltpu.VMEM((D, D), BF),
        pltpu.VMEM((D, FF), BF),
        pltpu.VMEM((FF, D), BF),
        pltpu.VMEM((16, D), F32),
        pltpu.VMEM(rows, BF),
        pltpu.VMEM(rows, BF),
        pltpu.VMEM((2, TAIL, D), BF),
        pltpu.VMEM((4, 16, 2 * LANE), BF),
        pltpu.VMEM((TAIL, D), BF),
        pltpu.VMEM((UNITS, TAIL, D), BF),
        pltpu.VMEM((UNITS, SEG, 3 * D), BF),
        pltpu.VMEM((UNITS, SEG, LANE), F32),
        pltpu.VMEM(rows, F32),
        pltpu.VMEM(rows, F32),
        pltpu.VMEM((SEG, FF), F32),
        pltpu.VMEM((SEG, FF), BF),
        pltpu.VMEM(rows, BF),
        pltpu.VMEM((2, SEG, D), F32),
        pltpu.VMEM((2, SEG, D), F32),
        pltpu.VMEM((4 * SEG, D), BF),
        pltpu.VMEM((2, 2 * SEG, LANE), BF),
        pltpu.VMEM((2, 2 * SEG, LANE), BF),
        pltpu.VMEM((2, 2 * SEG, 2 * LANE), BF),
        pltpu.VMEM((SEG, D), BF),
        pltpu.VMEM((2, SEG, D), BF),
        pltpu.VMEM((2, SEG, D), BF),
        pltpu.VMEM((2, 2, SEG, LANE), F32),
        pltpu.VMEM((2, SEG, 4 * LANE), BF),
    ]
    counts = [5, 5, 5, 3, 3, 3, 2, 4, 4, 4, 2, 4, 4, 4, 0, 4, 0, 0, 2, 2, 2, 4, 1, 2, 1, 2, 2]
    scratch += [pltpu.SemaphoreType.DMA((n,)) if n else pltpu.SemaphoreType.DMA for n in counts]
    scratch += [pltpu.SemaphoreType.REGULAR]
    smem = pl.BlockSpec(memory_space=pltpu.SMEM)
    in_specs = [hbm, hbm, vmem, vmem, smem, smem, hbm, hbm, hbm, hbm, hbm]
    return pl.pallas_call(
        relay_kernel,
        out_shape=results,
        in_specs=in_specs,
        out_specs=tuple([hbm] * 11 + [vmem, vmem]),
        scratch_shapes=scratch,
        compiler_params=pltpu.CompilerParams(
            collective_id=0, has_side_effects=True, vmem_limit_bytes=63 * 2**20
        ),
        cost_estimate=pl.CostEstimate(flops=80 * 10**9, bytes_accessed=80 * 2**20, transcendentals=0),
    )(*operands)


BLOCKS_G = 12
PARTS = 4
CHUNK = SEG // PARTS
PIECES = BLOCKS_G * PARTS
STAGES = 8
SLACK = 4
PATH_BLOCKS = (0, 3, 6, 9)
SMALL = 8 + TAIL


def reduce_kernel(
    xs,
    ctxs,
    hids,
    acts,
    gps,
    gbs,
    gus,
    gds,
    vecg,
    mem_part,
    f_qkv,
    f_o,
    f_in,
    f_out,
    small,
    xt,
    xm,
    gg,
    own,
    sent,
    tw,
    low_rx,
    high_rx,
    fin,
    acc,
    sm_tw,
    sm_rx,
    sm_tx,
    load_sem,
    tw_send,
    tw_recv,
    up_send,
    low_recv,
    high_recv,
    rung_recv,
    down_send,
    down_recv,
    fin_sem,
    sm_send,
    sm_recv,
):
    item = lax.axis_index("items")
    place = lax.axis_index("pipe")
    member = lax.rem(place, 2)
    twin = {"pipe": place + 1 - 2 * member}
    x_at, z_at = lax.rem(item, 2), item // 2
    rung = {"items": item + 1 - 2 * x_at}
    above = {"items": lax.rem(item + 2, 8)}
    below = {"items": lax.rem(item + 6, 8)}
    pair = {"items": item + 2 - 4 * lax.rem(z_at, 2)}
    far = {"items": item + 4 - 8 * (z_at // 2)}
    rounds = [rung, pair, far]
    has_above, has_below = z_at < 3, z_at > 0

    barrier = pltpu.get_barrier_semaphore()

    def greet(to):
        pl.semaphore_signal(barrier, inc=1, device_id=to, device_id_type=MESH)

    for to in (twin, rung, far):
        greet(to)

    @pl.when(has_above)
    def _():
        greet(above)

    @pl.when(has_below)
    def _():
        greet(below)

    def remote(src, dst, send, recv, to):
        return pltpu.make_async_remote_copy(
            src_ref=src, dst_ref=dst, send_sem=send, recv_sem=recv, device_id=to, device_id_type=MESH
        )

    def loads(left, right, theirs_rows, mine_rows, cols, slot):
        rows_t, col_t = theirs_rows
        rows_m, col_m = mine_rows
        return [
            pltpu.make_async_copy(left.at[:, rows_t, col_t], xt.at[slot], load_sem.at[slot, 0]),
            pltpu.make_async_copy(left.at[:, rows_m, col_m], xm.at[slot], load_sem.at[slot, 1]),
            pltpu.make_async_copy(right.at[:, :, cols], gg.at[slot], load_sem.at[slot, 2]),
        ]

    def aligned(start, size):
        return pl.ds(pl.multiple_of(start, SEG), size)

    def start_loads(b, slot):
        def go(left, right, pick, col):
            for copy in loads(left, right, pick(1 - member), pick(member), aligned(col * D, D), slot):
                copy.start()

        def flat(who):
            return aligned(0, SEG), aligned(who * SEG, SEG)

        @pl.when(b < 4)
        def _():
            def pick(who):
                return aligned((2 * who + b // 2) * SEG, SEG), aligned(lax.rem(b, 2) * SEG, SEG)

            go(acts, gds, pick, 0)

        @pl.when((b >= 4) & (b < 8))
        def _():
            go(hids, gus, flat, b - 4)

        @pl.when(b == 8)
        def _():
            go(ctxs, gbs, flat, 0)

        @pl.when(b >= 9)
        def _():
            go(xs, gps, flat, b - 9)

    def wait_loads(slot):
        zero = aligned(0, SEG)
        for copy in loads(xs, gds, (zero, zero), (zero, zero), aligned(0, D), slot):
            copy.wait()

    def twin_copy(b, slot):
        return remote(sent.at[slot], tw.at[b], tw_send.at[slot], tw_recv.at[b], twin)

    def out_copy(b, go):
        @pl.when(b < 4)
        def _():
            go(f_out.at[aligned(b * SEG, SEG)])

        @pl.when((b >= 4) & (b < 8))
        def _():
            go(f_in.at[:, aligned((b - 4) * D, D)])

        @pl.when(b == 8)
        def _():
            go(f_o.at[...])

        @pl.when(b >= 9)
        def _():
            go(f_qkv.at[:, aligned((b - 9) * D, D)])

    def piece(j):
        b, k = j // PARTS, lax.rem(j, PARTS)
        path = b == PATH_BLOCKS[0]
        for other_block in PATH_BLOCKS[1:]:
            path = path | (b == other_block)
        row = jnp.where(path, jnp.where(k < 4, k, k + 2 - PARTS // 2 - PARTS // 4), 1 + lax.rem(k // 2, 2))
        root = row + member * (3 - 2 * row)
        chain = path | (x_at == lax.rem(k + member, 2))
        away = jnp.abs(z_at - root)
        rows = pl.ds(pl.multiple_of(k * CHUNK, 16), CHUNK)
        return b, k, rows, path, root, chain, away

    def low_copy(j):
        return remote(low_rx.at[j], low_rx.at[j], up_send.at[j], low_recv.at[j], above)

    def high_copy(j):
        return remote(low_rx.at[j], high_rx.at[j], up_send.at[j], high_recv.at[j], below)

    def rung_up(j, b, rows):
        return remote(low_rx.at[j], fin.at[b, rows], up_send.at[j], rung_recv.at[j], rung)

    def rung_down(j, b, rows):
        return remote(fin.at[b, rows], fin.at[b, rows], down_send.at[2, j], rung_recv.at[j], rung)

    def below_down(j, b, rows):
        return remote(fin.at[b, rows], fin.at[b, rows], down_send.at[0, j], down_recv.at[j], below)

    def above_down(j, b, rows):
        return remote(fin.at[b, rows], fin.at[b, rows], down_send.at[1, j], down_recv.at[j], above)

    def spread(j, act):
        b, k, rows, path, root, chain, away = piece(j)

        @pl.when(chain & has_below & (z_at <= root))
        def _():
            act(below_down(j, b, rows))

        @pl.when(chain & has_above & (z_at >= root))
        def _():
            act(above_down(j, b, rows))

        @pl.when(chain & jnp.logical_not(path))
        def _():
            act(rung_down(j, b, rows))

    def gather(j):
        b, k, rows, path, root, chain, away = piece(j)
        acc[...] = own[b, rows, :] + tw[b, rows, :].astype(F32)

        @pl.when(chain & jnp.logical_not(path))
        def _():
            rung_down(j, b, rows).wait_recv()
            acc[...] += fin[b, rows, :].astype(F32)

        @pl.when(chain & has_below & (z_at <= root))
        def _():
            low_copy(j).wait_recv()
            acc[...] += low_rx[j].astype(F32)

        @pl.when(chain & has_above & (z_at >= root))
        def _():
            high_copy(j).wait_recv()
            acc[...] += high_rx[j].astype(F32)

        here = chain & (away == 0)

        @pl.when(here & jnp.logical_not(path))
        def _():
            fin[b, rows, :] = acc[...].astype(BF)
            spread(j, lambda copy: copy.start())

        @pl.when(jnp.logical_not(here & jnp.logical_not(path)))
        def _():
            low_rx[j] = acc[...].astype(BF)

        @pl.when(jnp.logical_not(chain) | (here & path))
        def _():
            rung_up(j, b, rows).start()

        @pl.when(chain & (z_at < root))
        def _():
            low_copy(j).start()

        @pl.when(chain & (z_at > root))
        def _():
            high_copy(j).start()

    def settle(j):
        b, k, rows, path, root, chain, away = piece(j)

        @pl.when(jnp.logical_not(chain) | (away == 0))
        def _():
            rung_down(j, b, rows).wait_recv()

        @pl.when(chain & (away == 0))
        def _():
            fin[b, rows, :] = (low_rx[j].astype(F32) + fin[b, rows, :].astype(F32)).astype(BF)

        @pl.when(chain & (away > 0))
        def _():
            below_down(j, b, rows).wait_recv()

        @pl.when(chain)
        def _():
            spread(j, lambda copy: copy.start())

    def stage(j, t):
        b, k, rows, path, root, chain, away = piece(j)

        @pl.when(t == jnp.where(chain, 3 - away, 0))
        def _():
            gather(j)

        later = jnp.where(path | jnp.logical_not(chain), 4 + away, 3 + away)

        @pl.when((t == later) & jnp.logical_not(chain & (away == 0) & jnp.logical_not(path)))
        def _():
            settle(j)

        @pl.when((t == STAGES - 1) & (k == PARTS - 1))
        def _():
            out_copy(b, lambda dst: pltpu.make_async_copy(fin.at[b], dst, fin_sem.at[b]).start())

    def small_twin():
        return remote(sm_tx.at[0], sm_tw, sm_send.at[0], sm_recv.at[0], twin)

    def small_round(k):
        return remote(small, sm_rx.at[k], sm_send.at[k + 1], sm_recv.at[k + 1], rounds[k])

    start_loads(0, 0)

    def product(slot, left):
        return tn(left[slot].reshape(UNITS * SEG, SEG), gg[slot].reshape(UNITS * SEG, D))

    wait_loads(0)
    start_loads(1, 1)
    sent[0] = product(0, xt).astype(BF)
    ends = z_at * (3 - z_at)
    pl.semaphore_wait(barrier, 4 + ends // 2)
    twin_copy(0, 0).start()
    eight = pl.ds(pl.multiple_of((1 - member) * 8, 8), 8)
    mine8 = pl.ds(pl.multiple_of(member * 8, 8), 8)
    sm_tx[0, :8, :] = vecg[eight, :]
    sm_tx[0, 8:, :] = mem_part[...]
    small[:8, :] = vecg[mine8, :]
    small[8:, :] = mem_part[...]
    small_twin().start()

    def step(i, carry):
        now = i // PARTS
        fresh = lax.rem(i, PARTS) == 0
        slot = lax.rem(now, 2)

        @pl.when(fresh & (now < BLOCKS_G))
        def _():
            @pl.when(now > 0)
            def _():
                wait_loads(slot)

                @pl.when(now + 1 < BLOCKS_G)
                def _():
                    start_loads(now + 1, 1 - slot)

                @pl.when(now >= 2)
                def _():
                    twin_copy(now - 2, slot).wait_send()

                sent[slot] = product(slot, xt).astype(BF)
                twin_copy(now, slot).start()

            own[now] = product(slot, xm)

        @pl.when(fresh & (now > 0) & (now <= BLOCKS_G))
        def _():
            twin_copy(now - 1, 0).wait_recv()

        for k in range(4):

            @pl.when(i == 4 * k + 4)
            def _():
                if k == 0:
                    small_twin().wait()
                    small[...] = small[...] + sm_tw[...]
                else:
                    small_round(k - 1).wait()
                    small[...] = small[...] + sm_rx[k - 1]
                if k < 3:
                    small_round(k).start()

        def serve(t, inner):
            j = i - PARTS - SLACK * t

            @pl.when((j >= 0) & (j < PIECES))
            def _():
                stage(j, t)

            return inner

        lax.fori_loop(0, STAGES, serve, 0)
        return carry

    lax.fori_loop(0, PARTS + PIECES + SLACK * (STAGES - 1), step, 0)

    twin_copy(0, 0).wait_send()
    twin_copy(1, 1).wait_send()

    def drain(j, carry):
        b, k, rows, path, root, chain, away = piece(j)

        @pl.when(jnp.logical_not(chain & (away == 0) & jnp.logical_not(path)))
        def _():
            low_copy(j).wait_send()

        spread(j, lambda copy: copy.wait_send())

        @pl.when(k == 0)
        def _():
            out_copy(b, lambda dst: pltpu.make_async_copy(fin.at[b], dst, fin_sem.at[b]).wait())

        return carry

    lax.fori_loop(0, PIECES, drain, 0)


def reduce_grads(operands):
    shape = jax.ShapeDtypeStruct
    hbm = pl.BlockSpec(memory_space=pl.ANY)
    vmem = pl.BlockSpec(memory_space=pltpu.VMEM)
    dma = pltpu.SemaphoreType.DMA
    return pl.pallas_call(
        reduce_kernel,
        out_shape=(
            shape((SEG, 3 * D), BF),
            shape((SEG, D), BF),
            shape((SEG, FF), BF),
            shape((FF // 2, D), BF),
            shape((SMALL, D), F32),
        ),
        in_specs=[hbm] * 8 + [vmem, vmem],
        out_specs=(hbm, hbm, hbm, hbm, vmem),
        scratch_shapes=[
            pltpu.VMEM((2, UNITS, SEG, SEG), BF),
            pltpu.VMEM((2, UNITS, SEG, SEG), BF),
            pltpu.VMEM((2, UNITS, SEG, D), BF),
            pltpu.VMEM((BLOCKS_G, SEG, D), F32),
            pltpu.VMEM((2, SEG, D), BF),
            pltpu.VMEM((BLOCKS_G, SEG, D), BF),
            pltpu.VMEM((PIECES, CHUNK, D), BF),
            pltpu.VMEM((PIECES, CHUNK, D), BF),
            pltpu.VMEM((BLOCKS_G, SEG, D), BF),
            pltpu.VMEM((CHUNK, D), F32),
            pltpu.VMEM((SMALL, D), F32),
            pltpu.VMEM((3, SMALL, D), F32),
            pltpu.VMEM((1, SMALL, D), F32),
            dma((2, 3)),
            dma((2,)),
            dma((BLOCKS_G,)),
            dma((PIECES,)),
            dma((PIECES,)),
            dma((PIECES,)),
            dma((PIECES,)),
            dma((3, PIECES)),
            dma((PIECES,)),
            dma((BLOCKS_G,)),
            dma((4,)),
            dma((4,)),
        ],
        compiler_params=pltpu.CompilerParams(
            collective_id=1, has_side_effects=True, vmem_limit_bytes=60 * 2**20
        ),
        cost_estimate=pl.CostEstimate(flops=22 * 10**9, bytes_accessed=64 * 2**20, transcendentals=0),
    )(*operands)


def finish_kernel(
    counts, lasts, tops, backs, tail, f_qkv, f_o, f_in, f_out, small, text, text_g, memory, mem_g, qkv_g, o_g, in_g, out_g, gains_g, biases_g
):
    step = pl.program_id(0)
    place = lax.axis_index("pipe")
    count, last = counts[place], lasts[place]
    rows = tops.shape[1]
    row = lax.broadcasted_iota(jnp.int32, (rows, D), 0) + step * rows
    for k in range(2):
        limit = jnp.where(count > 1, TEXT if k == 0 else last, last if k == 0 else 0)
        text[:, k, :] = jnp.where(row < limit, tops[k].astype(F32), 0.0)
        text_g[:, k, :] = backs[k].astype(F32)
    qkv_g[...] = f_qkv[...].astype(F32)
    o_g[...] = f_o[...].astype(F32)
    in_g[...] = f_in[...].astype(F32)
    out_g[...] = f_out[...].astype(F32)

    @pl.when(step == 0)
    def _():
        ends = tail[...].astype(F32)
        memory[0] = jnp.where(count > 1, ends[1], ends[0])[TAIL - MEM :, :]
        width = D // 4
        for index in range(4):

            @pl.when(place == index)
            def _():
                mem_g[...] = small[SMALL - MEM :, index * width : (index + 1) * width]

        gains_g[...] = small[0:1, :]
        biases_g[...] = small[1:6, :]


def finish(operands):
    shape = jax.ShapeDtypeStruct
    smem = pl.BlockSpec(memory_space=pltpu.SMEM)
    steps = 8
    row = SEG // steps

    def split(rows, cols):
        return pl.BlockSpec((rows, cols), lambda i: (i, 0))

    def whole(*size):
        return pl.BlockSpec(size, lambda i: (0,) * len(size))

    pair = pl.BlockSpec((2, row, D), lambda i: (0, i, 0))
    pair_out = pl.BlockSpec((row, 2, D), lambda i: (i, 0, 0))
    grads = [split(row, 3 * D), split(row, D), split(row, FF), split(4 * row, D)]
    counts, lasts, tops, backs, *rest = operands
    return pl.pallas_call(
        finish_kernel,
        grid=(steps,),
        out_shape=(
            shape((TEXT, 2, D), F32),
            shape((TEXT, 2, D), F32),
            shape((1, MEM, D), F32),
            shape((MEM, D // 4), F32),
            shape((SEG, 3 * D), F32),
            shape((SEG, D), F32),
            shape((SEG, FF), F32),
            shape((FF // 2, D), F32),
            shape((1, D), F32),
            shape((5, D), F32),
        ),
        in_specs=[
            smem,
            smem,
            pair,
            pair,
            pl.BlockSpec((2, TAIL, D), lambda i: (0, SEG // TAIL - 1, 0)),
            *grads,
            whole(SMALL, D),
        ],
        out_specs=(
            pair_out,
            pair_out,
            whole(1, MEM, D),
            whole(MEM, D // 4),
            *grads,
            whole(1, D),
            whole(5, D),
        ),
        compiler_params=pltpu.CompilerParams(vmem_limit_bytes=62 * 2**20),
    )(counts, lasts, tops, backs, tops, *rest)


def from_partner(x, axis, bit):
    return lax.ppermute(x, axis, [(i, i ^ 1 << bit) for i in range(lax.axis_size(axis))])


def over_rows(left, right):
    return lax.dot_general(
        left, right, (((0, 1), (0, 1)), ((), ())), preferred_element_type=F32
    )


def sum_grads(member, operands):
    xs, ctxs, hids, acts, gps, gbs, gus, gds, vecg, memg = operands
    def halves(left, right):
        size = left.shape[-1] // 2
        mine = lax.dynamic_slice_in_dim(left, member * size, size, 2)
        theirs = lax.dynamic_slice_in_dim(left, (1 - member) * size, size, 2)
        return over_rows(mine, right), over_rows(theirs, right).astype(BF)

    parts = [halves(xs, gps), halves(ctxs, gbs), halves(hids, gus)]
    blocks = acts.reshape(UNITS, 4, SEG, D)
    mine = lax.dynamic_slice_in_dim(blocks, member * 2, 2, 1)
    theirs = lax.dynamic_slice_in_dim(blocks, (1 - member) * 2, 2, 1)
    parts.append(
        (
            jnp.concatenate([over_rows(mine[:, i], gds) for i in range(2)], 0),
            jnp.concatenate([over_rows(theirs[:, i], gds) for i in range(2)], 0).astype(BF),
        )
    )
    sums = [kept + from_partner(sent, "pipe", 0).astype(F32) for kept, sent in parts]
    vec_mine = lax.dynamic_slice_in_dim(vecg, member * 8, 8, 0)
    vec_theirs = lax.dynamic_slice_in_dim(vecg, (1 - member) * 8, 8, 0)
    mine_small = jnp.concatenate([vec_mine, memg], 0)
    small = mine_small + from_partner(jnp.concatenate([vec_theirs, memg], 0), "pipe", 0)
    *grads, small = lax.psum((*sums, small), "items")
    return (*grads, small)


def per_device(
    text_in,
    memory,
    w_qkv,
    w_o,
    w_in,
    w_out,
    gains,
    biases,
    counts,
    last_lengths,
    text_cot,
    memory_cot,
):
    member = lax.axis_index("pipe") % 2
    pad = ((0, 0), (0, SEG - TEXT), (0, 0))
    x_own = jnp.pad(text_in[0], pad)
    c_own = jnp.pad(text_cot[0], pad)
    mem_own = jnp.pad(memory, ((0, 16 - MEM), (0, 2 * LANE - memory.shape[1])))
    mcot_own = jnp.pad(memory_cot[0], ((TAIL - MEM, 0), (0, 0)))
    vec_own = jnp.concatenate(
        [gains[None], biases.reshape(5, D), jnp.zeros((2, D), gains.dtype)], 0
    ).astype(F32)
    xs, ctxs, hids, acts, own_top, gds, gus, gbs, gps, own_back, _, vecg, memg = relay(
        (x_own, c_own, mem_own, mcot_own, counts, last_lengths, w_qkv, w_o, w_in, w_out, vec_own)
    )
    sum_all = reduce_grads if lax.axis_size("items") == 8 else functools.partial(sum_grads, member)
    sums = sum_all((xs, ctxs, hids, acts, gps, gbs, gus, gds, vecg, memg))
    text, text_grad, last_memory, memory_grad, *grads, gains_grad, biases_grad = finish(
        (counts, last_lengths, own_top, own_back, *sums)
    )
    return (
        text.transpose(1, 0, 2)[None],
        last_memory,
        text_grad.transpose(1, 0, 2)[None],
        memory_grad,
        *grads,
        gains_grad.reshape(D),
        biases_grad.reshape(5 * D),
    )


def solution(mesh):
    placed = (
        P(("items", "pipe"), None, None, None),
        P(None, "pipe"),
        P("pipe", None),
        P("pipe", None),
        P("pipe", None),
        P("pipe", None),
        P("pipe"),
        P("pipe"),
        P("items"),
        P("items"),
        P(("items", "pipe"), None, None, None),
        P(("items", "pipe"), None, None),
    )
    return jax.shard_map(
        per_device,
        mesh=mesh,
        in_specs=placed,
        out_specs=(
            P(("items", "pipe"), None, None, None),
            P(("items", "pipe"), None, None),
            P(("items", "pipe"), None, None, None),
            P(None, "pipe"),
            P("pipe", None),
            P("pipe", None),
            P("pipe", None),
            P("pipe", None),
            P("pipe"),
            P("pipe"),
        ),
        check_vma=False,
    )
```

```python
import functools

import jax
import jax.numpy as jnp
from jax import lax
from jax.experimental import pallas as pl
from jax.experimental.pallas import tpu as pltpu
from jax.sharding import PartitionSpec as P

D = 768
FF = 3072
MEM = 10
TEXT = 364
SEG = 384
PAIRS = 6
LANE = 128
TAIL = 32
UNITS = 4
LOG2E = 1.4426950408889634
MASKED = -1.0e9
EPS = 1e-6
MESH = pl.DeviceIdType.MESH
BF = jnp.bfloat16
F32 = jnp.float32
G1, BQ, BV, BO, N1, BD, G2, N2, BI = 0, 1, 2, 3, 4, 5, 8, 9, 10
BLOCKS = [slice(128 * b, 128 * b + 128) for b in range(3)]


def nn(left, right):
    return jnp.dot(left, right, preferred_element_type=F32)


def nt(left, right):
    return lax.dot_general(left, right, (((1,), (1,)), ((), ())), preferred_element_type=F32)


def tn(left, right):
    return lax.dot_general(left, right, (((0,), (0,)), ((), ())), preferred_element_type=F32)


def gelu_parts(up):
    t = pl.reciprocal(1.0 + (0.3275911 * 0.7071067811865476) * jnp.abs(up), approx=True)
    poly = t * (
        0.127414796
        + t * (-0.142248368 + t * (0.7107068705 + t * (-0.7265760135 + t * 0.5307027145)))
    )
    bell = jnp.exp2(up * up * (-0.5 * LOG2E))
    half = poly * bell
    phi = jnp.where(up >= 0, 1.0 - half, half)
    return up * phi, phi + up * bell * 0.3989422804014327


def norm_parts(values):
    centre = values - jnp.mean(values, axis=-1, keepdims=True)
    inverse = lax.rsqrt(jnp.mean(centre * centre, axis=-1, keepdims=True) + EPS)
    return centre * inverse, inverse


def norm_back(grad, normed, inverse, gain):
    scaled = grad * gain
    middle = jnp.mean(scaled, axis=-1, keepdims=True)
    along = jnp.mean(scaled * normed, axis=-1, keepdims=True)
    return inverse * (scaled - middle - normed * along)


def row_sum(values):
    return jnp.sum(values, axis=0, keepdims=True)


def split_stack(dst, src):
    low = lax.broadcasted_iota(jnp.int32, (SEG, LANE), 1) < 64
    zero = jnp.zeros((SEG, LANE), BF)
    dst[:SEG, :LANE] = jnp.where(low, src, zero)
    dst[SEG:, :LANE] = jnp.where(low, zero, src)


def tail_matrix(spread):
    row = lax.broadcasted_iota(jnp.int32, (TAIL, TAIL), 0)
    col = lax.broadcasted_iota(jnp.int32, (TAIL, TAIL), 1)
    if spread:
        keep = ((row >= 22) & (col == row)) | ((row >= 12) & (row < 22) & (col == row + 10))
    else:
        keep = (row >= 22) & ((col == row) | (col == row - 10))
    return jnp.where(keep, 1.0, 0.0).astype(BF)


def relay_kernel(
    x_own,
    c_own,
    mem_raw,
    mcot_raw,
    counts,
    lasts,
    w_qkv,
    w_o,
    w_in,
    w_out,
    vec_own,
    xs,
    ctxs,
    hids,
    acts,
    own_top,
    gds,
    gus,
    gbs,
    gps,
    own_back,
    slopes,
    vecg,
    memg,
    wq,
    wo,
    wi,
    wd,
    vec,
    xin,
    gsl,
    mcs,
    mem_rx,
    mem_own,
    mcot_own,
    mem0,
    trx,
    packed,
    st,
    n1s,
    n2s,
    dgf,
    gub,
    ctx,
    sc,
    sd,
    big,
    stk,
    stv,
    rhs,
    hid,
    outb,
    gdb,
    delta,
    parts,
    w_local,
    w_send,
    w_recv,
    e_local,
    e_send,
    e_recv,
    mid_send,
    mid_recv,
    tail_send,
    tail_recv,
    grad_send,
    grad_recv,
    x_sem,
    ctx_sem,
    gu_sem,
    gp_sem,
    hid_sem,
    act_sem,
    gd_sem,
    dg_sem,
    mem_send,
    mem_recv,
    top_send,
    top_recv,
    back_send,
    back_recv,
    res_sem,
    lag,
):
    place = lax.axis_index("pipe")
    first = place < 2
    member = lax.rem(place, 2)
    twin = {"pipe": place + 1 - 2 * member}
    other = {"pipe": lax.rem(place + 2, 4)}
    across = {"pipe": 3 - place}
    second = jnp.logical_not(first)

    halves = (
        (vec_own, vec, 8),
        (w_qkv, wq, D // 2),
        (w_o, wo, D // 2),
        (w_in, wi, D // 2),
        (w_out, wd, FF // 2),
    )

    def weight_rows(index, who):
        src, dst, rows = halves[index]
        return dst.at[pl.ds(pl.multiple_of(who * rows, rows), rows)]

    def local_weight(index):
        return pltpu.make_async_copy(
            halves[index][0], weight_rows(index, member), w_local.at[index]
        )

    def x_here(k):
        return pltpu.make_async_copy(x_own.at[k], xin.at[2 * k], e_local.at[k])

    barrier = pltpu.get_barrier_semaphore()
    for to in (twin, other, across):
        pl.semaphore_signal(barrier, inc=1, device_id=to, device_id_type=MESH)
    mem_own[...] = jnp.zeros_like(mem_own)
    mem_own[:MEM, : D // 4] = mem_raw[...]
    mcot_own[...] = jnp.zeros_like(mcot_own)
    mcot_own[TAIL - MEM :, :] = mcot_raw[:, 0, :].astype(BF)
    for index in (0, 1):
        local_weight(index).start()

    @pl.when(first)
    def _():
        for k in range(2):
            x_here(k).start()

    pl.semaphore_wait(barrier, 3)

    def remote(src, dst, send, recv, to):
        return pltpu.make_async_remote_copy(
            src_ref=src, dst_ref=dst, send_sem=send, recv_sem=recv, device_id=to, device_id_type=MESH
        )

    sends, recvs = [], []
    for index, (src, _, _) in enumerate(halves):
        mine, theirs = weight_rows(index, member), weight_rows(index, 1 - member)
        sends.append(remote(src, mine, w_send.at[index], w_recv.at[index], twin))
        recvs.append(remote(src, theirs, w_send.at[index], w_recv.at[index], twin))
    x_home = [x_here(k) for k in range(2)]
    x_away = [
        remote(x_own.at[k], xin.at[2 * k + 1], e_send.at[k], e_recv.at[k], other) for k in range(2)
    ]
    c_home = [
        pltpu.make_async_copy(c_own.at[k], gsl.at[2 * k + 1], e_local.at[k]) for k in range(2)
    ]
    c_away = [
        remote(c_own.at[k], gsl.at[2 * k], e_send.at[k], e_recv.at[k], other) for k in range(2)
    ]
    m_home = pltpu.make_async_copy(mcot_own, mcs.at[1], e_local.at[2])
    m_away = remote(mcot_own, mcs.at[0], e_send.at[2], e_recv.at[2], other)
    mem_twin = remote(mem_own, mem_rx.at[place], mem_send.at[0], mem_recv.at[place], twin)
    mem_other = remote(mem_own, mem_rx.at[place], mem_send.at[0], mem_recv.at[place], other)
    mem_across = remote(mem_own, mem_rx.at[place], mem_send.at[1], mem_recv.at[place], across)

    def start_weights(index):
        sends[index].start()

    def wait_weights(index):
        local_weight(index).wait()
        recvs[index].wait_recv()

    start_weights(0)
    start_weights(1)

    @pl.when(first)
    def _():
        mem_twin.start()

    @pl.when(second)
    def _():
        mem_other.start()
        mem_across.start()
        x_away[0].start()
        for copy in c_home:
            copy.start()
        m_home.start()

    rhs[...] = jnp.zeros_like(rhs)
    ones = jnp.ones((2 * LANE, LANE), BF)
    vecg[...] = jnp.zeros_like(vecg)
    memg[...] = jnp.zeros_like(memg)
    low = lax.broadcasted_iota(jnp.int32, (SEG, LANE), 1) < 64

    @pl.when(first)
    def _():
        mem_twin.wait_send()
        for index in range(4):

            @pl.when(index != place)
            def _():
                remote(mem_own, mem_rx.at[index], mem_send.at[0], mem_recv.at[index], twin).wait_recv()

            @pl.when(index == place)
            def _():
                mem_rx[index] = mem_own[...]

        row = lax.broadcasted_iota(jnp.int32, (TAIL, 16), 0)
        col = lax.broadcasted_iota(jnp.int32, (TAIL, 16), 1)
        twice = ((col == row - 12) | (col == row - 22)) & (col < MEM)
        spread = jnp.where(twice, 1.0, 0.0).astype(BF)
        total = jnp.zeros((TAIL, D), F32)
        for index in range(4):
            source = lax.broadcasted_iota(jnp.int32, (2 * LANE, D), 0)
            target = lax.broadcasted_iota(jnp.int32, (2 * LANE, D), 1)
            move = (target == source + index * (D // 4)) & (source < D // 4)
            rows = nn(spread, mem_rx[index]).astype(BF)
            total = total + nn(rows, jnp.where(move, 1.0, 0.0).astype(BF))
        mem0[...] = total.astype(BF)

    def unit_scalars(u):
        item = lax.rem(u, 2)
        count = counts[member + 2 * item]
        last = lasts[member + 2 * item]
        length = jnp.where((u < 2) & (count > 1), TEXT, last)
        return count, length

    def key_mask(length):
        key = lax.broadcasted_iota(jnp.int32, (1, SEG), 1)
        return jnp.where((key >= TEXT) | (key < length), 0.0, MASKED)

    def v(row):
        return vec[row : row + 1, :]

    def top_copy(u):
        return remote(
            outb.at[0], own_top.at[u // 2], top_send.at[0], top_recv.at[u // 2], other
        )

    def top_here(u):
        return pltpu.make_async_copy(outb.at[1], own_top.at[u // 2], res_sem.at[0])

    def back_copy(u):
        return remote(
            outb.at[1], own_back.at[u // 2], back_send.at[0], back_recv.at[u // 2], other
        )

    def back_here(u):
        return pltpu.make_async_copy(outb.at[0], own_back.at[u // 2], res_sem.at[1])

    def mid_copy(u, buf):
        return remote(outb.at[buf], xin.at[u], mid_send.at[buf], mid_recv.at[u], other)

    def grad_copy(u, buf):
        return remote(outb.at[buf], gsl.at[u], grad_send.at[buf], grad_recv.at[u], other)

    def tail_copy(slot, buf):
        src = outb.at[buf, pl.ds(SEG - TAIL, TAIL)]
        return remote(src, trx.at[slot], tail_send.at[slot], tail_recv.at[slot], other)

    def forward_turn(u, carry):
        item = lax.rem(u, 2)
        buf = lax.rem(u, 2)

        @pl.when(u == 0)
        def _():
            wait_weights(0)
            wait_weights(1)
            for index in (2, 3, 4):
                local_weight(index).start()
                start_weights(index)

        @pl.when(first & (u == 0))
        def _():
            for copy in x_home:
                copy.wait()

        @pl.when(first & (u == 1))
        def _():
            x_away[0].wait_recv()

        @pl.when(first & (u == 3))
        def _():
            x_away[1].wait_recv()

        @pl.when(second & (u == 0))
        def _():
            x_away[0].wait_send()
            x_away[1].start()

        @pl.when(first & (u < 2))
        def _():
            xin[u, SEG - TAIL :, :] = xin[u, SEG - TAIL :, :] + mem0[...]

        @pl.when(first & (u >= 2))
        def _():
            tail_copy(item, buf).wait_recv()
            spread = nn(tail_matrix(True), trx[item]).astype(BF)
            xin[u, SEG - TAIL :, :] = xin[u, SEG - TAIL :, :] + spread

        @pl.when(second)
        def _():
            mid_copy(u, buf).wait_recv()

        pltpu.make_async_copy(xin.at[u], xs.at[u], x_sem.at[u]).start()

        count, length = unit_scalars(u)
        mask = key_mask(length)
        x = xin[u]
        packed[u, :, :D] = (nn(x, wq[:, :D]) + v(BQ)).astype(BF) * 0.125
        packed[u, :, D : 2 * D] = nn(x, wq[:, D : 2 * D]).astype(BF)
        packed[u, :, 2 * D :] = (nn(x, wq[:, 2 * D :]) + v(BV)).astype(BF)

        @pl.when(u > 0)
        def _():
            hid_copy(u).wait()
            act_copy(u).wait()
            slope_out(u - 1).wait()

        def scores(p):
            b = p % 2
            split_stack(stk.at[b], packed[u, :, D + p * LANE : D + (p + 1) * LANE])
            split_stack(stv.at[b], packed[u, :, 2 * D + p * LANE : 2 * D + (p + 1) * LANE])
            sc[b] = nt(packed[u, :, p * LANE : (p + 1) * LANE], stk[b])

        scores(0)
        for p in range(PAIRS):
            b = p % 2
            if p + 1 < PAIRS:
                scores(p + 1)
            for rows in BLOCKS:
                for h in range(2):
                    cols = slice(h * SEG, (h + 1) * SEG)
                    scaled = sc[b, rows, cols] * LOG2E + mask
                    top = jnp.max(scaled, axis=-1, keepdims=True)
                    raised = jnp.exp2(scaled - top)
                    total = jnp.sum(raised, axis=-1, keepdims=True)
                    big[b * 2 * SEG + rows.start : b * 2 * SEG + rows.stop, cols] = (
                        raised * (1.0 / total)
                    ).astype(BF)
                    st[u, rows, 2 * p + h : 2 * p + h + 1] = top + jnp.log2(total)
            ctx[u, :, p * LANE : (p + 1) * LANE] = nn(
                big[b * 2 * SEG : b * 2 * SEG + SEG, :], stv[b]
            ).astype(BF)
        pltpu.make_async_copy(ctx.at[u], ctxs.at[u], ctx_sem.at[u]).start()

        @pl.when(u == 0)
        def _():
            wait_weights(2)

        sd[0] = nn(ctx[u], wo[...])
        for rows in BLOCKS:
            normed, inverse = norm_parts(xin[u, rows, :].astype(F32) + sd[0, rows, :] + v(BO))
            n1s[u, rows, :] = normed
            st[u, rows, 12:13] = inverse
            hid[rows, :] = (normed * v(G1) + v(N1)).astype(BF)
        hid_copy(u).start()

        @pl.when(u == 0)
        def _():
            wait_weights(3)
            wait_weights(4)

        def up(j):
            sd[j % 2] = nn(hid[...], wi[:, j * D : (j + 1) * D])

        up(0)
        for j in range(4):
            if j + 1 < 4:
                up(j + 1)
            for rows in BLOCKS:
                act, slope = gelu_parts(sd[j % 2, rows, :] + v(BI + j))
                big[j * SEG + rows.start : j * SEG + rows.stop, :] = act.astype(BF)
                dgf[rows, j * D : (j + 1) * D] = slope
            part = nn(big[j * SEG : (j + 1) * SEG, :], wd[j * D : (j + 1) * D, :])
            sc[0] = part if j == 0 else sc[0] + part
        act_copy(u).start()

        @pl.when(u < UNITS - 1)
        def _():
            slope_out(u).start()

        @pl.when(second & (u == 2))
        def _():
            top_copy(u).wait_send()

        @pl.when(second & (u == 3))
        def _():
            top_here(u).wait()

        @pl.when((u >= 2) & first)
        def _():
            mid_copy(u, buf).wait_send()

        @pl.when((u >= 2) & second)
        def _():
            tail_copy(item, buf).wait_send()

        for rows in BLOCKS:
            hidden = n1s[u, rows, :] * v(G1) + v(N1)
            normed, inverse = norm_parts(hidden + sc[0, rows, :] + v(BD))
            n2s[u, rows, :] = normed
            st[u, rows, 13:14] = inverse
            outb[buf, rows, :] = (normed * v(G2) + v(N2)).astype(BF)

        @pl.when(first)
        def _():
            mid_copy(u, buf).start()

        @pl.when(second & (u < 2))
        def _():
            tail_copy(item, buf).start()

        @pl.when(second & (item == 0))
        def _():
            top_copy(u).start()

        @pl.when(second & (item == 1))
        def _():
            top_here(u).start()

        return carry

    def hid_copy(u):
        return pltpu.make_async_copy(hid, hids.at[u], hid_sem)

    def act_copy(u):
        return pltpu.make_async_copy(big, acts.at[u], act_sem)

    def slope_out(u):
        return pltpu.make_async_copy(dgf, slopes.at[u], dg_sem.at[0])

    def slope_in(u):
        return pltpu.make_async_copy(slopes.at[u], dgf, dg_sem.at[1])

    lax.fori_loop(0, UNITS, forward_turn, 0)

    hid_copy(0).wait()
    act_copy(0).wait()
    for u in range(UNITS):
        pltpu.make_async_copy(ctx.at[u], ctxs.at[u], ctx_sem.at[u]).wait()
    for index in range(5):
        sends[index].wait_send()

    @pl.when(first)
    def _():
        for buf in range(2):
            mid_copy(2 + buf, buf).wait_send()
        pl.semaphore_signal(lag, inc=1, device_id=twin, device_id_type=MESH)
        pl.semaphore_wait(lag, 1)
        c_away[1].start()
        m_away.start()
        c_away[1].wait_send()
        c_away[0].start()

    @pl.when(second)
    def _():
        top_copy(2).wait_send()
        top_here(3).wait()
        x_away[1].wait_send()
        mem_other.wait_send()
        mem_across.wait_send()
        for copy in c_home:
            copy.wait()
        m_home.wait()

    def gd_copy(u):
        return pltpu.make_async_copy(hid, gds.at[u], gd_sem.at[0])

    def gb_copy(u):
        return pltpu.make_async_copy(gdb, gbs.at[u], gd_sem.at[1])

    def gu_copy(u):
        return pltpu.make_async_copy(gub, gus.at[u], gu_sem)

    def backward_turn(turn, carry):
        u = UNITS - 1 - turn
        item = lax.rem(u, 2)
        buf = lax.rem(u, 2)

        @pl.when(first)
        def _():
            grad_copy(u, buf).wait_recv()

        @pl.when(second & (u == 2))
        def _():
            c_away[1].wait_recv()
            m_away.wait_recv()

        @pl.when(second & (u == 0))
        def _():
            c_away[0].wait_recv()

        count, length = unit_scalars(u)
        limit = jnp.where(first, SEG, jnp.where((u < 2) | (count > 1), length, 0))
        row = lax.broadcasted_iota(jnp.int32, (SEG, D), 0)
        sd[0] = jnp.where(row < limit, gsl[u].astype(F32), 0.0)
        both_live = jnp.where(count > 1, 1.0, 0.0)

        @pl.when(second & (u >= 2))
        def _():
            sd[0, SEG - TAIL :, :] = sd[0, SEG - TAIL :, :] + mcs[item].astype(F32) * both_live

        @pl.when(second & (u < 2))
        def _():
            tail_copy(u + 2, buf).wait_recv()
            arrived = nn(tail_matrix(False), trx[u + 2])
            sd[0, SEG - TAIL :, :] = (
                sd[0, SEG - TAIL :, :]
                + arrived * both_live
                + mcs[item].astype(F32) * (1.0 - both_live)
            )

        @pl.when(turn > 0)
        def _():
            gd_copy(u).wait()
            gb_copy(u).wait()
            gu_copy(u).wait()
            slope_in(u).wait()

        for rows in BLOCKS:
            grad = sd[0, rows, :]
            normed = n2s[u, rows, :]
            second_grad = norm_back(grad, normed, st[u, rows, 13:14], v(G2))
            sc[0, rows, :] = second_grad
            down = second_grad.astype(BF)
            hid[rows, :] = down
            vecg[G2 : G2 + 1, :] += row_sum(grad * normed)
            vecg[N2 : N2 + 1, :] += row_sum(grad)
            vecg[BD : BD + 1, :] += row_sum(down.astype(F32))
        gd_copy(u).start()
        for j in range(4):
            sd[j % 2] = nt(hid[...], wd[j * D : (j + 1) * D, :])
            for rows in BLOCKS:
                cols = slice(j * D, (j + 1) * D)
                lifted = (sd[j % 2, rows, :] * dgf[rows, cols]).astype(BF)
                gub[rows, cols] = lifted
                vecg[BI + j : BI + j + 1, :] += row_sum(lifted.astype(F32))
        gu_copy(u).start()

        @pl.when(u > 0)
        def _():
            slope_in(u - 1).start()

        sd[0] = nt(gub[...], wi[...])
        for rows in BLOCKS:
            grad = sc[0, rows, :] + sd[0, rows, :]
            normed = n1s[u, rows, :]
            first_grad = norm_back(grad, normed, st[u, rows, 12:13], v(G1))
            branch = first_grad.astype(BF)
            gdb[rows, :] = branch
            vecg[G1 : G1 + 1, :] += row_sum(grad * normed)
            vecg[N1 : N1 + 1, :] += row_sum(grad)
            vecg[BO : BO + 1, :] += row_sum(branch.astype(F32))
            n1s[u, rows, :] = first_grad
        gb_copy(u).start()
        grad_ctx = nt(gdb[...], wo[...]).astype(BF)
        ctx[u] = grad_ctx
        mask = key_mask(length)

        def scores(p):
            b = p % 2
            query = packed[u, :, p * LANE : (p + 1) * LANE]
            grad = ctx[u, :, p * LANE : (p + 1) * LANE]
            split_stack(stk.at[b], packed[u, :, D + p * LANE : D + (p + 1) * LANE])
            split_stack(stv.at[b], packed[u, :, 2 * D + p * LANE : 2 * D + (p + 1) * LANE])
            rhs[b, :SEG, :LANE] = grad
            rhs[b, SEG:, LANE:] = query
            sc[b] = nt(query, stk[b])
            sd[b] = nt(grad, stv[b])

        scores(0)
        for p in range(PAIRS):
            b = p % 2
            base = b * 2 * SEG
            if p + 1 < PAIRS:
                scores(p + 1)
            for rows in BLOCKS:
                for h in range(2):
                    cols = slice(h * SEG, (h + 1) * SEG)
                    one = slice(2 * p + h, 2 * p + h + 1)
                    probs = jnp.exp2(sc[b, rows, cols] * LOG2E + mask - st[u, rows, one])
                    big[base + rows.start : base + rows.stop, cols] = probs.astype(BF)
                    sc[b, rows, cols] = probs
                    product = probs * sd[b, rows, cols]
                    third = product[:, :LANE] + product[:, LANE : 2 * LANE] + product[:, 2 * LANE :]
                    high = third.astype(BF)
                    at = 2 * h * LANE
                    parts[b, rows, at : at + LANE] = high
                    parts[b, rows, at + LANE : at + 2 * LANE] = (third - high.astype(F32)).astype(BF)
            for h in range(2):
                delta[b, h] = nn(parts[b, :, 2 * h * LANE : 2 * (h + 1) * LANE], ones)
            for rows in BLOCKS:
                for h in range(2):
                    for third in range(3):
                        cols = slice(h * SEG + third * LANE, h * SEG + (third + 1) * LANE)
                        big[base + SEG + rows.start : base + SEG + rows.stop, cols] = (
                            sc[b, rows, cols] * (sd[b, rows, cols] - delta[b, h, rows, :])
                        ).astype(BF)
            packed[u, :, p * LANE : (p + 1) * LANE] = (
                nn(big[base + SEG : base + 2 * SEG, :], stk[b]) * 0.125
            ).astype(BF)
            both = tn(big[base : base + 2 * SEG, :], rhs[b])
            packed[u, :, D + p * LANE : D + (p + 1) * LANE] = jnp.where(
                low, both[:SEG, LANE:], both[SEG:, LANE:]
            ).astype(BF)
            packed[u, :, 2 * D + p * LANE : 2 * D + (p + 1) * LANE] = jnp.where(
                low, both[:SEG, :LANE], both[SEG:, :LANE]
            ).astype(BF)
        pltpu.make_async_copy(packed.at[u], gps.at[u], gp_sem.at[u]).start()
        for rows in BLOCKS:
            vecg[BQ : BQ + 1, :] += row_sum(packed[u, rows, :D].astype(F32))
            vecg[BV : BV + 1, :] += row_sum(packed[u, rows, 2 * D :].astype(F32))
        sd[0] = nt(packed[u], wq[...])

        @pl.when((turn == 2) & first)
        def _():
            back_copy(u).wait_send()

        @pl.when((turn == 3) & first)
        def _():
            back_here(u).wait()

        @pl.when((turn >= 2) & first)
        def _():
            tail_copy(u + 2, buf).wait_send()

        @pl.when((turn >= 2) & second)
        def _():
            grad_copy(u, buf).wait_send()

        for rows in BLOCKS:
            outb[buf, rows, :] = (n1s[u, rows, :] + sd[0, rows, :]).astype(BF)

        @pl.when(second)
        def _():
            grad_copy(u, buf).start()

        @pl.when(first)
        def _():
            tail_copy(u, buf).start()

        @pl.when(first & (u < 2))
        def _():
            memg[...] += nn(tail_matrix(False), outb[buf, SEG - TAIL :, :])

        @pl.when(first & (item == 1))
        def _():
            back_copy(u).start()

        @pl.when(first & (item == 0))
        def _():
            back_here(u).start()

        return carry

    lax.fori_loop(0, UNITS, backward_turn, 0)

    gd_copy(0).wait()
    gb_copy(0).wait()
    gu_copy(0).wait()
    for u in range(UNITS):
        pltpu.make_async_copy(xin.at[u], xs.at[u], x_sem.at[u]).wait()
        pltpu.make_async_copy(packed.at[u], gps.at[u], gp_sem.at[u]).wait()

    @pl.when(first)
    def _():
        for buf in range(2):
            tail_copy(buf, buf).wait_send()
            top_copy(2 * buf).wait_recv()
        back_copy(1).wait_send()
        back_here(0).wait()
        c_away[0].wait_send()
        m_away.wait_send()

    @pl.when(second)
    def _():
        for buf in range(2):
            grad_copy(buf, buf).wait_send()
            tail_copy(buf, buf).wait_recv()
            memg[...] += nn(tail_matrix(False), trx[buf])
            back_copy(2 * buf + 1).wait_recv()


def relay(operands):
    rows = (UNITS, SEG, D)
    shape = jax.ShapeDtypeStruct
    hbm = pl.BlockSpec(memory_space=pl.ANY)
    vmem = pl.BlockSpec(memory_space=pltpu.VMEM)
    results = (
        shape(rows, BF),
        shape(rows, BF),
        shape(rows, BF),
        shape((UNITS, 4 * SEG, D), BF),
        shape((2, SEG, D), BF),
        shape(rows, BF),
        shape((UNITS, SEG, FF), BF),
        shape(rows, BF),
        shape((UNITS, SEG, 3 * D), BF),
        shape((2, SEG, D), BF),
        shape((UNITS - 1, SEG, FF), F32),
        shape((16, D), F32),
        shape((TAIL, D), F32),
    )
    scratch = [
        pltpu.VMEM((D, 3 * D), BF),
        pltpu.VMEM((D, D), BF),
        pltpu.VMEM((D, FF), BF),
        pltpu.VMEM((FF, D), BF),
        pltpu.VMEM((16, D), F32),
        pltpu.VMEM(rows, BF),
        pltpu.VMEM(rows, BF),
        pltpu.VMEM((2, TAIL, D), BF),
        pltpu.VMEM((4, 16, 2 * LANE), BF),
        pltpu.VMEM((16, 2 * LANE), BF),
        pltpu.VMEM((TAIL, D), BF),
        pltpu.VMEM((TAIL, D), BF),
        pltpu.VMEM((UNITS, TAIL, D), BF),
        pltpu.VMEM((UNITS, SEG, 3 * D), BF),
        pltpu.VMEM((UNITS, SEG, LANE), F32),
        pltpu.VMEM(rows, F32),
        pltpu.VMEM(rows, F32),
        pltpu.VMEM((SEG, FF), F32),
        pltpu.VMEM((SEG, FF), BF),
        pltpu.VMEM(rows, BF),
        pltpu.VMEM((2, SEG, D), F32),
        pltpu.VMEM((2, SEG, D), F32),
        pltpu.VMEM((4 * SEG, D), BF),
        pltpu.VMEM((2, 2 * SEG, LANE), BF),
        pltpu.VMEM((2, 2 * SEG, LANE), BF),
        pltpu.VMEM((2, 2 * SEG, 2 * LANE), BF),
        pltpu.VMEM((SEG, D), BF),
        pltpu.VMEM((2, SEG, D), BF),
        pltpu.VMEM((SEG, D), BF),
        pltpu.VMEM((2, 2, SEG, LANE), F32),
        pltpu.VMEM((2, SEG, 4 * LANE), BF),
    ]
    counts = [5, 5, 5, 3, 3, 3, 2, 4, 4, 4, 2, 4, 4, 4, 0, 4, 0, 0, 2, 2, 2, 4, 1, 2, 1, 2, 2]
    scratch += [pltpu.SemaphoreType.DMA((n,)) if n else pltpu.SemaphoreType.DMA for n in counts]
    scratch += [pltpu.SemaphoreType.REGULAR]
    smem = pl.BlockSpec(memory_space=pltpu.SMEM)
    in_specs = [hbm, hbm, vmem, vmem, smem, smem, hbm, hbm, hbm, hbm, hbm]
    return pl.pallas_call(
        relay_kernel,
        out_shape=results,
        in_specs=in_specs,
        out_specs=tuple([hbm] * 11 + [vmem, vmem]),
        scratch_shapes=scratch,
        compiler_params=pltpu.CompilerParams(
            collective_id=0, has_side_effects=True, vmem_limit_bytes=63 * 2**20
        ),
        cost_estimate=pl.CostEstimate(flops=80 * 10**9, bytes_accessed=80 * 2**20, transcendentals=0),
    )(*operands)


BLOCKS_G = 12
PARTS = 4
CHUNK = SEG // PARTS
PIECES = BLOCKS_G * PARTS
STAGES = 8
SLACK = 4
PATH_BLOCKS = (0, 3, 6, 9)
SMALL = 8 + TAIL
FINISH = 62


def reduce_kernel(
    xs,
    ctxs,
    hids,
    acts,
    gps,
    gbs,
    gus,
    gds,
    vecg,
    mem_part,
    sums,
    small,
    xb,
    gg,
    own,
    sent,
    tw,
    low_rx,
    high_rx,
    fin,
    acc,
    sm_tw,
    sm_rx,
    sm_tx,
    load_sem,
    tw_send,
    tw_recv,
    up_send,
    low_recv,
    high_recv,
    rung_recv,
    down_send,
    down_recv,
    fin_sem,
    sm_send,
    sm_recv,
):
    item = lax.axis_index("items")
    place = lax.axis_index("pipe")
    member = lax.rem(place, 2)
    twin = {"pipe": place + 1 - 2 * member}
    x_at, z_at = lax.rem(item, 2), item // 2
    rung = {"items": item + 1 - 2 * x_at}
    above = {"items": lax.rem(item + 2, 8)}
    below = {"items": lax.rem(item + 6, 8)}
    pair = {"items": item + 2 - 4 * lax.rem(z_at, 2)}
    far = {"items": item + 4 - 8 * (z_at // 2)}
    rounds = [rung, pair, far]
    has_above, has_below = z_at < 3, z_at > 0

    barrier = pltpu.get_barrier_semaphore()

    def greet(to):
        pl.semaphore_signal(barrier, inc=1, device_id=to, device_id_type=MESH)

    for to in (twin, rung, far):
        greet(to)

    @pl.when(has_above)
    def _():
        greet(above)

    @pl.when(has_below)
    def _():
        greet(below)

    def remote(src, dst, send, recv, to):
        return pltpu.make_async_remote_copy(
            src_ref=src, dst_ref=dst, send_sem=send, recv_sem=recv, device_id=to, device_id_type=MESH
        )

    def loads(left, right, theirs_rows, mine_rows, cols, slot):
        rows_t, col_t = theirs_rows
        rows_m, col_m = mine_rows
        return [
            pltpu.make_async_copy(
                left.at[:, rows_t, col_t], xb.at[slot, :, :, pl.ds(0, SEG)], load_sem.at[slot, 0]
            ),
            pltpu.make_async_copy(
                left.at[:, rows_m, col_m], xb.at[slot, :, :, pl.ds(SEG, SEG)], load_sem.at[slot, 1]
            ),
            pltpu.make_async_copy(right.at[:, :, cols], gg.at[slot], load_sem.at[slot, 2]),
        ]

    def aligned(start, size):
        return pl.ds(pl.multiple_of(start, SEG), size)

    def start_loads(b, slot):
        def go(left, right, pick, col):
            for copy in loads(left, right, pick(1 - member), pick(member), aligned(col * D, D), slot):
                copy.start()

        def flat(who):
            return aligned(0, SEG), aligned(who * SEG, SEG)

        @pl.when(b < 4)
        def _():
            def pick(who):
                return aligned((2 * who + b // 2) * SEG, SEG), aligned(lax.rem(b, 2) * SEG, SEG)

            go(acts, gds, pick, 0)

        @pl.when((b >= 4) & (b < 8))
        def _():
            go(hids, gus, flat, b - 4)

        @pl.when(b == 8)
        def _():
            go(ctxs, gbs, flat, 0)

        @pl.when(b >= 9)
        def _():
            go(xs, gps, flat, b - 9)

    def wait_loads(slot):
        zero = aligned(0, SEG)
        for copy in loads(xs, gds, (zero, zero), (zero, zero), aligned(0, D), slot):
            copy.wait()

    def twin_copy(b, slot):
        return remote(sent.at[slot], tw.at[b], tw_send.at[slot], tw_recv.at[b], twin)

    def piece(j):
        b, k = j // PARTS, lax.rem(j, PARTS)
        path = b == PATH_BLOCKS[0]
        for other_block in PATH_BLOCKS[1:]:
            path = path | (b == other_block)
        row = jnp.where(path, jnp.where(k < 4, k, k + 2 - PARTS // 2 - PARTS // 4), 1 + lax.rem(k // 2, 2))
        root = row + member * (3 - 2 * row)
        chain = path | (x_at == lax.rem(k + member, 2))
        away = jnp.abs(z_at - root)
        rows = pl.ds(pl.multiple_of(k * CHUNK, 16), CHUNK)
        return b, k, rows, path, root, chain, away

    def low_copy(j):
        return remote(low_rx.at[j], low_rx.at[j], up_send.at[j], low_recv.at[j], above)

    def high_copy(j):
        return remote(low_rx.at[j], high_rx.at[j], up_send.at[j], high_recv.at[j], below)

    def rung_up(j, b, rows):
        return remote(low_rx.at[j], fin.at[b, rows], up_send.at[j], rung_recv.at[j], rung)

    def rung_down(j, b, rows):
        return remote(fin.at[b, rows], fin.at[b, rows], down_send.at[2, j], rung_recv.at[j], rung)

    def below_down(j, b, rows):
        return remote(fin.at[b, rows], fin.at[b, rows], down_send.at[0, j], down_recv.at[j], below)

    def above_down(j, b, rows):
        return remote(fin.at[b, rows], fin.at[b, rows], down_send.at[1, j], down_recv.at[j], above)

    def spread(j, act):
        b, k, rows, path, root, chain, away = piece(j)

        @pl.when(chain & has_below & (z_at <= root))
        def _():
            act(below_down(j, b, rows))

        @pl.when(chain & has_above & (z_at >= root))
        def _():
            act(above_down(j, b, rows))

        @pl.when(chain & jnp.logical_not(path))
        def _():
            act(rung_down(j, b, rows))

    def gather(j):
        b, k, rows, path, root, chain, away = piece(j)
        acc[...] = own[b, rows, :] + tw[b, rows, :].astype(F32)

        @pl.when(chain & jnp.logical_not(path))
        def _():
            rung_down(j, b, rows).wait_recv()
            acc[...] += fin[b, rows, :].astype(F32)

        @pl.when(chain & has_below & (z_at <= root))
        def _():
            low_copy(j).wait_recv()
            acc[...] += low_rx[j].astype(F32)

        @pl.when(chain & has_above & (z_at >= root))
        def _():
            high_copy(j).wait_recv()
            acc[...] += high_rx[j].astype(F32)

        here = chain & (away == 0)

        @pl.when(here & jnp.logical_not(path))
        def _():
            fin[b, rows, :] = acc[...].astype(BF)
            spread(j, lambda copy: copy.start())

        @pl.when(jnp.logical_not(here & jnp.logical_not(path)))
        def _():
            low_rx[j] = acc[...].astype(BF)

        @pl.when(jnp.logical_not(chain) | (here & path))
        def _():
            rung_up(j, b, rows).start()

        @pl.when(chain & (z_at < root))
        def _():
            low_copy(j).start()

        @pl.when(chain & (z_at > root))
        def _():
            high_copy(j).start()

    def settle(j):
        b, k, rows, path, root, chain, away = piece(j)

        @pl.when(jnp.logical_not(chain) | (away == 0))
        def _():
            rung_down(j, b, rows).wait_recv()

        @pl.when(chain & (away == 0))
        def _():
            fin[b, rows, :] = (low_rx[j].astype(F32) + fin[b, rows, :].astype(F32)).astype(BF)

        @pl.when(chain & (away > 0))
        def _():
            below_down(j, b, rows).wait_recv()

        @pl.when(chain)
        def _():
            spread(j, lambda copy: copy.start())

    def stage(j, t):
        b, k, rows, path, root, chain, away = piece(j)

        @pl.when(t == jnp.where(chain, 3 - away, 0))
        def _():
            gather(j)

        later = jnp.where(path | jnp.logical_not(chain), 4 + away, 3 + away)

        @pl.when((t == later) & jnp.logical_not(chain & (away == 0) & jnp.logical_not(path)))
        def _():
            settle(j)

        @pl.when((t == STAGES - 1) & (k == PARTS - 1))
        def _():
            pltpu.make_async_copy(fin.at[b], sums.at[b], fin_sem.at[b]).start()

    def small_twin():
        return remote(sm_tx.at[0], sm_tw, sm_send.at[0], sm_recv.at[0], twin)

    def small_round(k):
        return remote(small, sm_rx.at[k], sm_send.at[k + 1], sm_recv.at[k + 1], rounds[k])

    start_loads(0, 0)

    def product(b, slot):
        both = tn(xb[slot].reshape(UNITS * SEG, D), gg[slot].reshape(UNITS * SEG, D))
        sent[slot] = both[:SEG].astype(BF)
        own[b] = both[SEG:]

    wait_loads(0)
    start_loads(1, 1)
    product(0, 0)
    ends = z_at * (3 - z_at)
    pl.semaphore_wait(barrier, 4 + ends // 2)
    twin_copy(0, 0).start()
    eight = pl.ds(pl.multiple_of((1 - member) * 8, 8), 8)
    mine8 = pl.ds(pl.multiple_of(member * 8, 8), 8)
    sm_tx[0, :8, :] = vecg[eight, :]
    sm_tx[0, 8:, :] = mem_part[...]
    small[:8, :] = vecg[mine8, :]
    small[8:, :] = mem_part[...]
    small_twin().start()

    def step(i, carry):
        now = i // PARTS
        fresh = lax.rem(i, PARTS) == 0
        slot = lax.rem(now, 2)

        @pl.when(fresh & (now < BLOCKS_G))
        def _():
            @pl.when(now > 0)
            def _():
                wait_loads(slot)

                @pl.when(now + 1 < BLOCKS_G)
                def _():
                    start_loads(now + 1, 1 - slot)

                @pl.when(now >= 2)
                def _():
                    twin_copy(now - 2, slot).wait_send()

                product(now, slot)
                twin_copy(now, slot).start()

        @pl.when(fresh & (now > 0) & (now <= BLOCKS_G))
        def _():
            twin_copy(now - 1, 0).wait_recv()

        for k in range(4):

            @pl.when(i == 4 * k + 4)
            def _():
                if k == 0:
                    small_twin().wait()
                    small[...] = small[...] + sm_tw[...]
                else:
                    small_round(k - 1).wait()
                    small[...] = small[...] + sm_rx[k - 1]
                if k < 3:
                    small_round(k).start()

        def serve(t, inner):
            j = i - PARTS - SLACK * t

            @pl.when((j >= 0) & (j < PIECES))
            def _():
                stage(j, t)

            return inner

        lax.fori_loop(0, STAGES, serve, 0)
        return carry

    lax.fori_loop(0, PARTS + PIECES + SLACK * (STAGES - 1), step, 0)

    twin_copy(0, 0).wait_send()
    twin_copy(1, 1).wait_send()

    def drain(j, carry):
        b, k, rows, path, root, chain, away = piece(j)

        @pl.when(jnp.logical_not(chain & (away == 0) & jnp.logical_not(path)))
        def _():
            low_copy(j).wait_send()

        spread(j, lambda copy: copy.wait_send())

        @pl.when(k == 0)
        def _():
            pltpu.make_async_copy(fin.at[b], sums.at[b], fin_sem.at[b]).wait()

        return carry

    lax.fori_loop(0, PIECES, drain, 0)


def reduce_grads(operands):
    shape = jax.ShapeDtypeStruct
    hbm = pl.BlockSpec(memory_space=pl.ANY)
    vmem = pl.BlockSpec(memory_space=pltpu.VMEM)
    dma = pltpu.SemaphoreType.DMA
    return pl.pallas_call(
        reduce_kernel,
        out_shape=(
            shape((BLOCKS_G, SEG, D), BF),
            shape((SMALL, D), F32),
        ),
        in_specs=[hbm] * 8 + [vmem, vmem],
        out_specs=(hbm, vmem),
        scratch_shapes=[
            pltpu.VMEM((2, UNITS, SEG, D), BF),
            pltpu.VMEM((2, UNITS, SEG, D), BF),
            pltpu.VMEM((BLOCKS_G, SEG, D), F32),
            pltpu.VMEM((2, SEG, D), BF),
            pltpu.VMEM((BLOCKS_G, SEG, D), BF),
            pltpu.VMEM((PIECES, CHUNK, D), BF),
            pltpu.VMEM((PIECES, CHUNK, D), BF),
            pltpu.VMEM((BLOCKS_G, SEG, D), BF),
            pltpu.VMEM((CHUNK, D), F32),
            pltpu.VMEM((SMALL, D), F32),
            pltpu.VMEM((3, SMALL, D), F32),
            pltpu.VMEM((1, SMALL, D), F32),
            dma((2, 3)),
            dma((2,)),
            dma((BLOCKS_G,)),
            dma((PIECES,)),
            dma((PIECES,)),
            dma((PIECES,)),
            dma((PIECES,)),
            dma((3, PIECES)),
            dma((PIECES,)),
            dma((BLOCKS_G,)),
            dma((4,)),
            dma((4,)),
        ],
        compiler_params=pltpu.CompilerParams(
            collective_id=1, has_side_effects=True, vmem_limit_bytes=62 * 2**20
        ),
        cost_estimate=pl.CostEstimate(flops=22 * 10**9, bytes_accessed=64 * 2**20, transcendentals=0),
    )(*operands)


def finish_kernel(
    counts,
    lasts,
    tops,
    backs,
    tail,
    sums,
    small,
    text,
    text_g,
    memory,
    mem_g,
    qkv_g,
    o_g,
    in_g,
    out_g,
    gains_g,
    biases_g,
):
    step = pl.program_id(0)
    place = lax.axis_index("pipe")
    count, last = counts[place], lasts[place]
    rows = tops.shape[1]
    row = lax.broadcasted_iota(jnp.int32, (rows, D), 0) + step * rows
    for k in range(2):
        limit = jnp.where(count > 1, TEXT if k == 0 else last, last if k == 0 else 0)
        text[:, k, :] = jnp.where(row < limit, tops[k].astype(F32), 0.0)
        text_g[:, k, :] = backs[k].astype(F32)
    out_g[...] = sums[:4].astype(F32)
    for j in range(4):
        in_g[:, j * D : (j + 1) * D] = sums[4 + j].astype(F32)
    o_g[...] = sums[8].astype(F32)
    for j in range(3):
        qkv_g[:, j * D : (j + 1) * D] = sums[9 + j].astype(F32)

    @pl.when(step == 0)
    def _():
        ends = tail[...].astype(F32)
        memory[:, 0, :] = jnp.where(count > 1, ends[1], ends[0])[TAIL - MEM :, :]
        width = D // 4
        for index in range(4):

            @pl.when(place == index)
            def _():
                mem_g[...] = small[SMALL - MEM :, index * width : (index + 1) * width]

        gains_g[...] = small[0]
        for index in range(5):
            biases_g[index * D : (index + 1) * D] = small[1 + index]


def finish(operands):
    shape = jax.ShapeDtypeStruct
    smem = pl.BlockSpec(memory_space=pltpu.SMEM)
    steps = 4
    row = SEG // steps

    def split(rows, cols):
        return pl.BlockSpec((rows, cols), lambda i: (i, 0))

    def whole(*size):
        return pl.BlockSpec(size, lambda i: (0,) * len(size))

    pair = pl.BlockSpec((2, row, D), lambda i: (0, i, 0))
    pair_out = pl.BlockSpec((row, 2, D), lambda i: (i, 0, 0))
    out_spec = pl.BlockSpec((4, row, D), lambda i: (0, i, 0))
    grads = [split(row, 3 * D), split(row, D), split(row, FF), out_spec]
    counts, lasts, tops, backs, *rest = operands
    return pl.pallas_call(
        finish_kernel,
        grid=(steps,),
        out_shape=(
            shape((TEXT, 2, D), F32),
            shape((TEXT, 2, D), F32),
            shape((MEM, 1, D), F32),
            shape((MEM, D // 4), F32),
            shape((SEG, 3 * D), F32),
            shape((SEG, D), F32),
            shape((SEG, FF), F32),
            shape((4, SEG, D), F32),
            shape((D,), F32),
            shape((5 * D,), F32),
        ),
        in_specs=[
            smem,
            smem,
            pair,
            pair,
            pl.BlockSpec((2, TAIL, D), lambda i: (0, SEG // TAIL - 1, 0)),
            pl.BlockSpec((BLOCKS_G, row, D), lambda i: (0, i, 0)),
            whole(SMALL, D),
        ],
        out_specs=(
            pair_out,
            pair_out,
            whole(MEM, 1, D),
            whole(MEM, D // 4),
            *grads,
            whole(D),
            whole(5 * D),
        ),
        compiler_params=pltpu.CompilerParams(vmem_limit_bytes=FINISH * 2**20),
    )(counts, lasts, tops, backs, tops, *rest)


def from_partner(x, axis, bit):
    return lax.ppermute(x, axis, [(i, i ^ 1 << bit) for i in range(lax.axis_size(axis))])


def over_rows(left, right):
    return lax.dot_general(
        left, right, (((0, 1), (0, 1)), ((), ())), preferred_element_type=F32
    )


def sum_grads(member, operands):
    xs, ctxs, hids, acts, gps, gbs, gus, gds, vecg, memg = operands
    def halves(left, right):
        size = left.shape[-1] // 2
        mine = lax.dynamic_slice_in_dim(left, member * size, size, 2)
        theirs = lax.dynamic_slice_in_dim(left, (1 - member) * size, size, 2)
        return over_rows(mine, right), over_rows(theirs, right).astype(BF)

    parts = [halves(xs, gps), halves(ctxs, gbs), halves(hids, gus)]
    blocks = acts.reshape(UNITS, 4, SEG, D)
    mine = lax.dynamic_slice_in_dim(blocks, member * 2, 2, 1)
    theirs = lax.dynamic_slice_in_dim(blocks, (1 - member) * 2, 2, 1)
    parts.append(
        (
            jnp.concatenate([over_rows(mine[:, i], gds) for i in range(2)], 0),
            jnp.concatenate([over_rows(theirs[:, i], gds) for i in range(2)], 0).astype(BF),
        )
    )
    sums = [kept + from_partner(sent, "pipe", 0).astype(F32) for kept, sent in parts]
    vec_mine = lax.dynamic_slice_in_dim(vecg, member * 8, 8, 0)
    vec_theirs = lax.dynamic_slice_in_dim(vecg, (1 - member) * 8, 8, 0)
    mine_small = jnp.concatenate([vec_mine, memg], 0)
    small = mine_small + from_partner(jnp.concatenate([vec_theirs, memg], 0), "pipe", 0)
    *grads, small = lax.psum((*sums, small), "items")
    qkv, out_proj, up, down = grads
    columns = [up[:, j * D : (j + 1) * D] for j in range(4)] + [out_proj]
    columns += [qkv[:, j * D : (j + 1) * D] for j in range(3)]
    return jnp.concatenate([down.reshape(4, SEG, D), jnp.stack(columns)], 0), small


def per_device(
    text_in,
    memory,
    w_qkv,
    w_o,
    w_in,
    w_out,
    gains,
    biases,
    counts,
    last_lengths,
    text_cot,
    memory_cot,
):
    member = lax.axis_index("pipe") % 2
    pad = ((0, 0), (0, SEG - TEXT), (0, 0))
    x_own = jnp.pad(text_in[0], pad)
    c_own = jnp.pad(text_cot[0], pad)
    mcot = memory_cot.astype(F32).transpose(1, 0, 2)
    vec_own = jnp.concatenate([gains, biases, jnp.zeros(2 * D, gains.dtype)]).reshape(8, D).astype(F32)
    xs, ctxs, hids, acts, own_top, gds, gus, gbs, gps, own_back, _, vecg, memg = relay(
        (x_own, c_own, memory, mcot, counts, last_lengths, w_qkv, w_o, w_in, w_out, vec_own)
    )
    sum_all = reduce_grads if lax.axis_size("items") == 8 else functools.partial(sum_grads, member)
    sums = sum_all((xs, ctxs, hids, acts, gps, gbs, gus, gds, vecg, memg))
    text, text_grad, last_memory, memory_grad, *grads, down, gains_grad, biases_grad = finish(
        (counts, last_lengths, own_top, own_back, *sums)
    )
    return (
        text.transpose(1, 0, 2)[None],
        last_memory.transpose(1, 0, 2),
        text_grad.transpose(1, 0, 2)[None],
        memory_grad,
        *grads,
        down.reshape(FF // 2, D),
        gains_grad,
        biases_grad,
    )


def solution(mesh):
    placed = (
        P(("items", "pipe"), None, None, None),
        P(None, "pipe"),
        P("pipe", None),
        P("pipe", None),
        P("pipe", None),
        P("pipe", None),
        P("pipe"),
        P("pipe"),
        P("items"),
        P("items"),
        P(("items", "pipe"), None, None, None),
        P(("items", "pipe"), None, None),
    )
    return jax.shard_map(
        per_device,
        mesh=mesh,
        in_specs=placed,
        out_specs=(
            P(("items", "pipe"), None, None, None),
            P(("items", "pipe"), None, None),
            P(("items", "pipe"), None, None, None),
            P(None, "pipe"),
            P("pipe", None),
            P("pipe", None),
            P("pipe", None),
            P("pipe", None),
            P("pipe"),
            P("pipe"),
        ),
        check_vma=False,
    )
```

```python
import functools

import jax
import jax.numpy as jnp
from jax import lax
from jax.experimental import pallas as pl
from jax.experimental.pallas import tpu as pltpu
from jax.sharding import PartitionSpec as P

D = 768
FF = 3072
MEM = 10
TEXT = 364
SEG = 384
PAIRS = 6
LANE = 128
TAIL = 32
UNITS = 4
LOG2E = 1.4426950408889634
MASKED = -1.0e9
EPS = 1e-6
MESH = pl.DeviceIdType.MESH
BF = jnp.bfloat16
F32 = jnp.float32
G1, BQ, BV, BO, N1, BD, G2, N2, BI = 0, 1, 2, 3, 4, 5, 8, 9, 10
BLOCKS = [slice(128 * b, 128 * b + 128) for b in range(3)]


def nn(left, right):
    return jnp.dot(left, right, preferred_element_type=F32)


def nt(left, right):
    return lax.dot_general(left, right, (((1,), (1,)), ((), ())), preferred_element_type=F32)


def tn(left, right):
    return lax.dot_general(left, right, (((0,), (0,)), ((), ())), preferred_element_type=F32)


def gelu_parts(up):
    t = pl.reciprocal(1.0 + (0.3275911 * 0.7071067811865476) * jnp.abs(up), approx=True)
    poly = t * (
        0.127414796
        + t * (-0.142248368 + t * (0.7107068705 + t * (-0.7265760135 + t * 0.5307027145)))
    )
    bell = jnp.exp2(up * up * (-0.5 * LOG2E))
    half = poly * bell
    phi = jnp.where(up >= 0, 1.0 - half, half)
    return up * phi, phi + up * bell * 0.3989422804014327


def norm_parts(values):
    centre = values - jnp.mean(values, axis=-1, keepdims=True)
    inverse = lax.rsqrt(jnp.mean(centre * centre, axis=-1, keepdims=True) + EPS)
    return centre * inverse, inverse


def norm_back(grad, normed, inverse, gain):
    scaled = grad * gain
    middle = jnp.mean(scaled, axis=-1, keepdims=True)
    along = jnp.mean(scaled * normed, axis=-1, keepdims=True)
    return inverse * (scaled - middle - normed * along)


def row_sum(values):
    return jnp.sum(values, axis=0, keepdims=True)


def split_stack(dst, src):
    low = lax.broadcasted_iota(jnp.int32, (SEG, LANE), 1) < 64
    zero = jnp.zeros((SEG, LANE), BF)
    dst[:SEG, :LANE] = jnp.where(low, src, zero)
    dst[SEG:, :LANE] = jnp.where(low, zero, src)


def tail_matrix(spread):
    row = lax.broadcasted_iota(jnp.int32, (TAIL, TAIL), 0)
    col = lax.broadcasted_iota(jnp.int32, (TAIL, TAIL), 1)
    if spread:
        keep = ((row >= 22) & (col == row)) | ((row >= 12) & (row < 22) & (col == row + 10))
    else:
        keep = (row >= 22) & ((col == row) | (col == row - 10))
    return jnp.where(keep, 1.0, 0.0).astype(BF)


def relay_kernel(
    x_own,
    c_own,
    mem_raw,
    mcot_raw,
    counts,
    lasts,
    w_qkv,
    w_o,
    w_in,
    w_out,
    vec_own,
    xs,
    ctxs,
    hids,
    acts,
    own_top,
    gds,
    gus,
    gbs,
    gps,
    own_back,
    slopes,
    vecg,
    memg,
    wq,
    wo,
    wi,
    wd,
    vec,
    xin,
    gsl,
    mcs,
    mem_rx,
    mem_own,
    mcot_own,
    mem0,
    trx,
    packed,
    st,
    n1s,
    n2s,
    dgf,
    gub,
    ctx,
    sc,
    sd,
    big,
    stk,
    stv,
    rhs,
    hid,
    outb,
    gdb,
    delta,
    rest,
    w_local,
    w_send,
    w_recv,
    e_local,
    e_send,
    e_recv,
    mid_send,
    mid_recv,
    tail_send,
    tail_recv,
    grad_send,
    grad_recv,
    x_sem,
    ctx_sem,
    gu_sem,
    gp_sem,
    hid_sem,
    act_sem,
    gd_sem,
    dg_sem,
    mem_send,
    mem_recv,
    top_send,
    top_recv,
    back_send,
    back_recv,
    res_sem,
    lag,
):
    place = lax.axis_index("pipe")
    first = place < 2
    member = lax.rem(place, 2)
    twin = {"pipe": place + 1 - 2 * member}
    other = {"pipe": lax.rem(place + 2, 4)}
    across = {"pipe": 3 - place}
    second = jnp.logical_not(first)

    halves = (
        (vec_own, vec, 8),
        (w_qkv, wq, D // 2),
        (w_o, wo, D // 2),
        (w_in, wi, D // 2),
        (w_out, wd, FF // 2),
    )

    def weight_rows(index, who):
        src, dst, rows = halves[index]
        return dst.at[pl.ds(pl.multiple_of(who * rows, rows), rows)]

    def local_weight(index):
        return pltpu.make_async_copy(
            halves[index][0], weight_rows(index, member), w_local.at[index]
        )

    def x_here(k):
        return pltpu.make_async_copy(x_own.at[k], xin.at[2 * k], e_local.at[k])

    barrier = pltpu.get_barrier_semaphore()
    for to in (twin, other, across):
        pl.semaphore_signal(barrier, inc=1, device_id=to, device_id_type=MESH)
    mem_own[...] = jnp.zeros_like(mem_own)
    mem_own[:MEM, : D // 4] = mem_raw[...]
    mcot_own[...] = jnp.zeros_like(mcot_own)
    mcot_own[TAIL - MEM :, :] = mcot_raw[:, 0, :].astype(BF)
    for index in (0, 1):
        local_weight(index).start()

    @pl.when(first)
    def _():
        for k in range(2):
            x_here(k).start()

    pl.semaphore_wait(barrier, 3)

    def remote(src, dst, send, recv, to):
        return pltpu.make_async_remote_copy(
            src_ref=src, dst_ref=dst, send_sem=send, recv_sem=recv, device_id=to, device_id_type=MESH
        )

    sends, recvs = [], []
    for index, (src, _, _) in enumerate(halves):
        mine, theirs = weight_rows(index, member), weight_rows(index, 1 - member)
        sends.append(remote(src, mine, w_send.at[index], w_recv.at[index], twin))
        recvs.append(remote(src, theirs, w_send.at[index], w_recv.at[index], twin))
    x_home = [x_here(k) for k in range(2)]
    x_away = [
        remote(x_own.at[k], xin.at[2 * k + 1], e_send.at[k], e_recv.at[k], other) for k in range(2)
    ]
    c_home = [
        pltpu.make_async_copy(c_own.at[k], gsl.at[2 * k + 1], e_local.at[k]) for k in range(2)
    ]
    c_away = [
        remote(c_own.at[k], gsl.at[2 * k], e_send.at[k], e_recv.at[k], other) for k in range(2)
    ]
    m_home = pltpu.make_async_copy(mcot_own, mcs.at[1], e_local.at[2])
    m_away = remote(mcot_own, mcs.at[0], e_send.at[2], e_recv.at[2], other)
    mem_twin = remote(mem_own, mem_rx.at[place], mem_send.at[0], mem_recv.at[place], twin)
    mem_other = remote(mem_own, mem_rx.at[place], mem_send.at[0], mem_recv.at[place], other)
    mem_across = remote(mem_own, mem_rx.at[place], mem_send.at[1], mem_recv.at[place], across)

    def start_weights(index):
        sends[index].start()

    def wait_weights(index):
        local_weight(index).wait()
        recvs[index].wait_recv()

    start_weights(0)
    start_weights(1)

    @pl.when(first)
    def _():
        mem_twin.start()

    @pl.when(second)
    def _():
        mem_other.start()
        mem_across.start()
        x_away[0].start()
        for copy in c_home:
            copy.start()
        m_home.start()

    rhs[...] = jnp.zeros_like(rhs)
    vecg[...] = jnp.zeros_like(vecg)
    memg[...] = jnp.zeros_like(memg)
    low = lax.broadcasted_iota(jnp.int32, (SEG, LANE), 1) < 64

    @pl.when(first)
    def _():
        mem_twin.wait_send()
        for index in range(4):

            @pl.when(index != place)
            def _():
                remote(mem_own, mem_rx.at[index], mem_send.at[0], mem_recv.at[index], twin).wait_recv()

            @pl.when(index == place)
            def _():
                mem_rx[index] = mem_own[...]

        row = lax.broadcasted_iota(jnp.int32, (TAIL, 16), 0)
        col = lax.broadcasted_iota(jnp.int32, (TAIL, 16), 1)
        twice = ((col == row - 12) | (col == row - 22)) & (col < MEM)
        spread = jnp.where(twice, 1.0, 0.0).astype(BF)
        total = jnp.zeros((TAIL, D), F32)
        for index in range(4):
            source = lax.broadcasted_iota(jnp.int32, (2 * LANE, D), 0)
            target = lax.broadcasted_iota(jnp.int32, (2 * LANE, D), 1)
            move = (target == source + index * (D // 4)) & (source < D // 4)
            rows = nn(spread, mem_rx[index]).astype(BF)
            total = total + nn(rows, jnp.where(move, 1.0, 0.0).astype(BF))
        mem0[...] = total.astype(BF)

    def unit_scalars(u):
        item = lax.rem(u, 2)
        count = counts[member + 2 * item]
        last = lasts[member + 2 * item]
        length = jnp.where((u < 2) & (count > 1), TEXT, last)
        return count, length

    def key_mask(length):
        key = lax.broadcasted_iota(jnp.int32, (1, SEG), 1)
        return jnp.where((key >= TEXT) | (key < length), 0.0, MASKED)

    def v(row):
        return vec[row : row + 1, :]

    def top_copy(u):
        return remote(
            outb.at[0], own_top.at[u // 2], top_send.at[0], top_recv.at[u // 2], other
        )

    def top_here(u):
        return pltpu.make_async_copy(outb.at[1], own_top.at[u // 2], res_sem.at[0])

    def back_copy(u):
        return remote(
            outb.at[1], own_back.at[u // 2], back_send.at[0], back_recv.at[u // 2], other
        )

    def back_here(u):
        return pltpu.make_async_copy(outb.at[0], own_back.at[u // 2], res_sem.at[1])

    def mid_copy(u, buf):
        return remote(outb.at[buf], xin.at[u], mid_send.at[buf], mid_recv.at[u], other)

    def grad_copy(u, buf):
        return remote(outb.at[buf], gsl.at[u], grad_send.at[buf], grad_recv.at[u], other)

    def tail_copy(slot, buf):
        src = outb.at[buf, pl.ds(SEG - TAIL, TAIL)]
        return remote(src, trx.at[slot], tail_send.at[slot], tail_recv.at[slot], other)

    def forward_turn(u, carry):
        item = lax.rem(u, 2)
        buf = lax.rem(u, 2)

        @pl.when(u == 0)
        def _():
            wait_weights(0)
            wait_weights(1)
            for index in (2, 3, 4):
                local_weight(index).start()
                start_weights(index)

        @pl.when(first & (u == 0))
        def _():
            for copy in x_home:
                copy.wait()

        @pl.when(first & (u == 1))
        def _():
            x_away[0].wait_recv()

        @pl.when(first & (u == 3))
        def _():
            x_away[1].wait_recv()

        @pl.when(second & (u == 0))
        def _():
            x_away[0].wait_send()
            x_away[1].start()

        @pl.when(first & (u < 2))
        def _():
            xin[u, SEG - TAIL :, :] = xin[u, SEG - TAIL :, :] + mem0[...]

        @pl.when(first & (u >= 2))
        def _():
            tail_copy(item, buf).wait_recv()
            spread = nn(tail_matrix(True), trx[item]).astype(BF)
            xin[u, SEG - TAIL :, :] = xin[u, SEG - TAIL :, :] + spread

        @pl.when(second)
        def _():
            mid_copy(u, buf).wait_recv()

        pltpu.make_async_copy(xin.at[u], xs.at[u], x_sem.at[u]).start()

        count, length = unit_scalars(u)
        mask = key_mask(length)
        x = xin[u]
        packed[u, :, :D] = (nn(x, wq[:, :D]) + v(BQ)).astype(BF) * 0.125
        packed[u, :, D : 2 * D] = nn(x, wq[:, D : 2 * D]).astype(BF)
        packed[u, :, 2 * D :] = (nn(x, wq[:, 2 * D :]) + v(BV)).astype(BF)

        @pl.when(u > 0)
        def _():
            hid_copy(u).wait()
            act_copy(u).wait()
            slope_out(u - 1).wait()

        def scores(p):
            b = p % 2
            split_stack(stk.at[b], packed[u, :, D + p * LANE : D + (p + 1) * LANE])
            split_stack(stv.at[b], packed[u, :, 2 * D + p * LANE : 2 * D + (p + 1) * LANE])
            sc[b] = nt(packed[u, :, p * LANE : (p + 1) * LANE], stk[b])

        scores(0)
        for p in range(PAIRS):
            b = p % 2
            if p + 1 < PAIRS:
                scores(p + 1)
            for rows in BLOCKS:
                for h in range(2):
                    cols = slice(h * SEG, (h + 1) * SEG)
                    scaled = sc[b, rows, cols] * LOG2E + mask
                    top = jnp.max(scaled, axis=-1, keepdims=True)
                    raised = jnp.exp2(scaled - top)
                    total = jnp.sum(raised, axis=-1, keepdims=True)
                    big[b * 2 * SEG + rows.start : b * 2 * SEG + rows.stop, cols] = (
                        raised * (1.0 / total)
                    ).astype(BF)
                    st[u, rows, 2 * p + h : 2 * p + h + 1] = top + jnp.log2(total)
            mixed = nn(big[b * 2 * SEG : b * 2 * SEG + SEG, :], stv[b])
            rounded = mixed.astype(BF)
            ctx[u, :, p * LANE : (p + 1) * LANE] = rounded
            rest[u, :, p * LANE : (p + 1) * LANE] = (mixed - rounded.astype(F32)).astype(BF)
        pltpu.make_async_copy(ctx.at[u], ctxs.at[u], ctx_sem.at[u]).start()

        @pl.when(u == 0)
        def _():
            wait_weights(2)

        sd[0] = nn(ctx[u], wo[...])
        for rows in BLOCKS:
            normed, inverse = norm_parts(xin[u, rows, :].astype(F32) + sd[0, rows, :] + v(BO))
            n1s[u, rows, :] = normed
            st[u, rows, 12:13] = inverse
            hid[rows, :] = (normed * v(G1) + v(N1)).astype(BF)
        hid_copy(u).start()

        @pl.when(u == 0)
        def _():
            wait_weights(3)
            wait_weights(4)

        def up(j):
            sd[j % 2] = nn(hid[...], wi[:, j * D : (j + 1) * D])

        up(0)
        for j in range(4):
            if j + 1 < 4:
                up(j + 1)
            for rows in BLOCKS:
                act, slope = gelu_parts(sd[j % 2, rows, :] + v(BI + j))
                big[j * SEG + rows.start : j * SEG + rows.stop, :] = act.astype(BF)
                dgf[rows, j * D : (j + 1) * D] = slope
            part = nn(big[j * SEG : (j + 1) * SEG, :], wd[j * D : (j + 1) * D, :])
            sc[0] = part if j == 0 else sc[0] + part
        act_copy(u).start()

        @pl.when(u < UNITS - 1)
        def _():
            slope_out(u).start()

        @pl.when(second & (u == 2))
        def _():
            top_copy(u).wait_send()

        @pl.when(second & (u == 3))
        def _():
            top_here(u).wait()

        @pl.when((u >= 2) & first)
        def _():
            mid_copy(u, buf).wait_send()

        @pl.when((u >= 2) & second)
        def _():
            tail_copy(item, buf).wait_send()

        for rows in BLOCKS:
            hidden = n1s[u, rows, :] * v(G1) + v(N1)
            normed, inverse = norm_parts(hidden + sc[0, rows, :] + v(BD))
            n2s[u, rows, :] = normed
            st[u, rows, 13:14] = inverse
            outb[buf, rows, :] = (normed * v(G2) + v(N2)).astype(BF)

        @pl.when(first)
        def _():
            mid_copy(u, buf).start()

        @pl.when(second & (u < 2))
        def _():
            tail_copy(item, buf).start()

        @pl.when(second & (item == 0))
        def _():
            top_copy(u).start()

        @pl.when(second & (item == 1))
        def _():
            top_here(u).start()

        return carry

    def hid_copy(u):
        return pltpu.make_async_copy(hid, hids.at[u], hid_sem)

    def act_copy(u):
        return pltpu.make_async_copy(big, acts.at[u], act_sem)

    def slope_out(u):
        return pltpu.make_async_copy(dgf, slopes.at[u], dg_sem.at[0])

    def slope_in(u):
        return pltpu.make_async_copy(slopes.at[u], dgf, dg_sem.at[1])

    lax.fori_loop(0, UNITS, forward_turn, 0)

    hid_copy(0).wait()
    act_copy(0).wait()
    for u in range(UNITS):
        pltpu.make_async_copy(ctx.at[u], ctxs.at[u], ctx_sem.at[u]).wait()
    for index in range(5):
        sends[index].wait_send()

    @pl.when(first)
    def _():
        for buf in range(2):
            mid_copy(2 + buf, buf).wait_send()
        pl.semaphore_signal(lag, inc=1, device_id=twin, device_id_type=MESH)
        pl.semaphore_wait(lag, 1)
        c_away[1].start()
        m_away.start()
        c_away[1].wait_send()
        c_away[0].start()

    @pl.when(second)
    def _():
        top_copy(2).wait_send()
        top_here(3).wait()
        x_away[1].wait_send()
        mem_other.wait_send()
        mem_across.wait_send()
        for copy in c_home:
            copy.wait()
        m_home.wait()

    def gd_copy(u):
        return pltpu.make_async_copy(hid, gds.at[u], gd_sem.at[0])

    def gb_copy(u):
        return pltpu.make_async_copy(gdb, gbs.at[u], gd_sem.at[1])

    def gu_copy(u):
        return pltpu.make_async_copy(gub, gus.at[u], gu_sem)

    def backward_turn(turn, carry):
        u = UNITS - 1 - turn
        item = lax.rem(u, 2)
        buf = lax.rem(u, 2)

        @pl.when(first)
        def _():
            grad_copy(u, buf).wait_recv()

        @pl.when(second & (u == 2))
        def _():
            c_away[1].wait_recv()
            m_away.wait_recv()

        @pl.when(second & (u == 0))
        def _():
            c_away[0].wait_recv()

        count, length = unit_scalars(u)
        limit = jnp.where(first, SEG, jnp.where((u < 2) | (count > 1), length, 0))
        row = lax.broadcasted_iota(jnp.int32, (SEG, D), 0)
        sd[0] = jnp.where(row < limit, gsl[u].astype(F32), 0.0)
        both_live = jnp.where(count > 1, 1.0, 0.0)

        @pl.when(second & (u >= 2))
        def _():
            sd[0, SEG - TAIL :, :] = sd[0, SEG - TAIL :, :] + mcs[item].astype(F32) * both_live

        @pl.when(second & (u < 2))
        def _():
            tail_copy(u + 2, buf).wait_recv()
            arrived = nn(tail_matrix(False), trx[u + 2])
            sd[0, SEG - TAIL :, :] = (
                sd[0, SEG - TAIL :, :]
                + arrived * both_live
                + mcs[item].astype(F32) * (1.0 - both_live)
            )

        @pl.when(turn > 0)
        def _():
            gd_copy(u).wait()
            gb_copy(u).wait()
            gu_copy(u).wait()
            slope_in(u).wait()

        for rows in BLOCKS:
            grad = sd[0, rows, :]
            normed = n2s[u, rows, :]
            second_grad = norm_back(grad, normed, st[u, rows, 13:14], v(G2))
            sc[0, rows, :] = second_grad
            down = second_grad.astype(BF)
            hid[rows, :] = down
            vecg[G2 : G2 + 1, :] += row_sum(grad * normed)
            vecg[N2 : N2 + 1, :] += row_sum(grad)
            vecg[BD : BD + 1, :] += row_sum(down.astype(F32))
        gd_copy(u).start()
        for j in range(4):
            sd[j % 2] = nt(hid[...], wd[j * D : (j + 1) * D, :])
            for rows in BLOCKS:
                cols = slice(j * D, (j + 1) * D)
                lifted = (sd[j % 2, rows, :] * dgf[rows, cols]).astype(BF)
                gub[rows, cols] = lifted
                vecg[BI + j : BI + j + 1, :] += row_sum(lifted.astype(F32))
        gu_copy(u).start()

        @pl.when(u > 0)
        def _():
            slope_in(u - 1).start()

        sd[0] = nt(gub[...], wi[...])
        for rows in BLOCKS:
            grad = sc[0, rows, :] + sd[0, rows, :]
            normed = n1s[u, rows, :]
            first_grad = norm_back(grad, normed, st[u, rows, 12:13], v(G1))
            branch = first_grad.astype(BF)
            gdb[rows, :] = branch
            vecg[G1 : G1 + 1, :] += row_sum(grad * normed)
            vecg[N1 : N1 + 1, :] += row_sum(grad)
            vecg[BO : BO + 1, :] += row_sum(branch.astype(F32))
            n1s[u, rows, :] = first_grad
        gb_copy(u).start()
        head = lax.broadcasted_iota(jnp.int32, (D, LANE), 0) // 64
        heads = (head == lax.broadcasted_iota(jnp.int32, (D, LANE), 1)).astype(F32).astype(BF)
        grad_ctx = nt(gdb[...], wo[...]).astype(BF)
        product = grad_ctx.astype(F32) * (ctx[u].astype(F32) + rest[u].astype(F32))
        high = product.astype(BF)
        delta[...] = nn(high, heads) + nn((product - high.astype(F32)).astype(BF), heads)
        ctx[u] = grad_ctx
        mask = key_mask(length)

        def scores(p):
            b = p % 2
            query = packed[u, :, p * LANE : (p + 1) * LANE]
            grad = ctx[u, :, p * LANE : (p + 1) * LANE]
            split_stack(stk.at[b], packed[u, :, D + p * LANE : D + (p + 1) * LANE])
            split_stack(stv.at[b], packed[u, :, 2 * D + p * LANE : 2 * D + (p + 1) * LANE])
            rhs[b, :SEG, :LANE] = grad
            rhs[b, SEG:, LANE:] = query
            sc[b] = nt(query, stk[b])
            sd[b] = nt(grad, stv[b])

        scores(0)
        for p in range(PAIRS):
            b = p % 2
            base = b * 2 * SEG
            if p + 1 < PAIRS:
                scores(p + 1)
            for rows in BLOCKS:
                for h in range(2):
                    cols = slice(h * SEG, (h + 1) * SEG)
                    one = slice(2 * p + h, 2 * p + h + 1)
                    probs = jnp.exp2(sc[b, rows, cols] * LOG2E + mask - st[u, rows, one])
                    big[base + rows.start : base + rows.stop, cols] = probs.astype(BF)
                    big[base + SEG + rows.start : base + SEG + rows.stop, cols] = (
                        probs * (sd[b, rows, cols] - delta[rows, one])
                    ).astype(BF)
            packed[u, :, p * LANE : (p + 1) * LANE] = (
                nn(big[base + SEG : base + 2 * SEG, :], stk[b]) * 0.125
            ).astype(BF)
            both = tn(big[base : base + 2 * SEG, :], rhs[b])
            packed[u, :, D + p * LANE : D + (p + 1) * LANE] = jnp.where(
                low, both[:SEG, LANE:], both[SEG:, LANE:]
            ).astype(BF)
            packed[u, :, 2 * D + p * LANE : 2 * D + (p + 1) * LANE] = jnp.where(
                low, both[:SEG, :LANE], both[SEG:, :LANE]
            ).astype(BF)
        pltpu.make_async_copy(packed.at[u], gps.at[u], gp_sem.at[u]).start()
        for rows in BLOCKS:
            vecg[BQ : BQ + 1, :] += row_sum(packed[u, rows, :D].astype(F32))
            vecg[BV : BV + 1, :] += row_sum(packed[u, rows, 2 * D :].astype(F32))
        sd[0] = nt(packed[u], wq[...])

        @pl.when((turn == 2) & first)
        def _():
            back_copy(u).wait_send()

        @pl.when((turn == 3) & first)
        def _():
            back_here(u).wait()

        @pl.when((turn >= 2) & first)
        def _():
            tail_copy(u + 2, buf).wait_send()

        @pl.when((turn >= 2) & second)
        def _():
            grad_copy(u, buf).wait_send()

        for rows in BLOCKS:
            outb[buf, rows, :] = (n1s[u, rows, :] + sd[0, rows, :]).astype(BF)

        @pl.when(second)
        def _():
            grad_copy(u, buf).start()

        @pl.when(first)
        def _():
            tail_copy(u, buf).start()

        @pl.when(first & (u < 2))
        def _():
            memg[...] += nn(tail_matrix(False), outb[buf, SEG - TAIL :, :])

        @pl.when(first & (item == 1))
        def _():
            back_copy(u).start()

        @pl.when(first & (item == 0))
        def _():
            back_here(u).start()

        return carry

    lax.fori_loop(0, UNITS, backward_turn, 0)

    gd_copy(0).wait()
    gb_copy(0).wait()
    gu_copy(0).wait()
    for u in range(UNITS):
        pltpu.make_async_copy(xin.at[u], xs.at[u], x_sem.at[u]).wait()
        pltpu.make_async_copy(packed.at[u], gps.at[u], gp_sem.at[u]).wait()

    @pl.when(first)
    def _():
        for buf in range(2):
            tail_copy(buf, buf).wait_send()
            top_copy(2 * buf).wait_recv()
        back_copy(1).wait_send()
        back_here(0).wait()
        c_away[0].wait_send()
        m_away.wait_send()

    @pl.when(second)
    def _():
        for buf in range(2):
            grad_copy(buf, buf).wait_send()
            tail_copy(buf, buf).wait_recv()
            memg[...] += nn(tail_matrix(False), trx[buf])
            back_copy(2 * buf + 1).wait_recv()


def relay(operands):
    rows = (UNITS, SEG, D)
    shape = jax.ShapeDtypeStruct
    hbm = pl.BlockSpec(memory_space=pl.ANY)
    vmem = pl.BlockSpec(memory_space=pltpu.VMEM)
    results = (
        shape(rows, BF),
        shape(rows, BF),
        shape(rows, BF),
        shape((UNITS, 4 * SEG, D), BF),
        shape((2, SEG, D), BF),
        shape(rows, BF),
        shape((UNITS, SEG, FF), BF),
        shape(rows, BF),
        shape((UNITS, SEG, 3 * D), BF),
        shape((2, SEG, D), BF),
        shape((UNITS - 1, SEG, FF), F32),
        shape((16, D), F32),
        shape((TAIL, D), F32),
    )
    scratch = [
        pltpu.VMEM((D, 3 * D), BF),
        pltpu.VMEM((D, D), BF),
        pltpu.VMEM((D, FF), BF),
        pltpu.VMEM((FF, D), BF),
        pltpu.VMEM((16, D), F32),
        pltpu.VMEM(rows, BF),
        pltpu.VMEM(rows, BF),
        pltpu.VMEM((2, TAIL, D), BF),
        pltpu.VMEM((4, 16, 2 * LANE), BF),
        pltpu.VMEM((16, 2 * LANE), BF),
        pltpu.VMEM((TAIL, D), BF),
        pltpu.VMEM((TAIL, D), BF),
        pltpu.VMEM((UNITS, TAIL, D), BF),
        pltpu.VMEM((UNITS, SEG, 3 * D), BF),
        pltpu.VMEM((UNITS, SEG, LANE), F32),
        pltpu.VMEM(rows, F32),
        pltpu.VMEM(rows, F32),
        pltpu.VMEM((SEG, FF), F32),
        pltpu.VMEM((SEG, FF), BF),
        pltpu.VMEM(rows, BF),
        pltpu.VMEM((2, SEG, D), F32),
        pltpu.VMEM((2, SEG, D), F32),
        pltpu.VMEM((4 * SEG, D), BF),
        pltpu.VMEM((2, 2 * SEG, LANE), BF),
        pltpu.VMEM((2, 2 * SEG, LANE), BF),
        pltpu.VMEM((2, 2 * SEG, 2 * LANE), BF),
        pltpu.VMEM((SEG, D), BF),
        pltpu.VMEM((2, SEG, D), BF),
        pltpu.VMEM((SEG, D), BF),
        pltpu.VMEM((SEG, LANE), F32),
        pltpu.VMEM(rows, BF),
    ]
    counts = [5, 5, 5, 3, 3, 3, 2, 4, 4, 4, 2, 4, 4, 4, 0, 4, 0, 0, 2, 2, 2, 4, 1, 2, 1, 2, 2]
    scratch += [pltpu.SemaphoreType.DMA((n,)) if n else pltpu.SemaphoreType.DMA for n in counts]
    scratch += [pltpu.SemaphoreType.REGULAR]
    smem = pl.BlockSpec(memory_space=pltpu.SMEM)
    in_specs = [hbm, hbm, vmem, vmem, smem, smem, hbm, hbm, hbm, hbm, hbm]
    return pl.pallas_call(
        relay_kernel,
        out_shape=results,
        in_specs=in_specs,
        out_specs=tuple([hbm] * 11 + [vmem, vmem]),
        scratch_shapes=scratch,
        compiler_params=pltpu.CompilerParams(
            collective_id=0, has_side_effects=True, vmem_limit_bytes=63 * 2**20
        ),
        cost_estimate=pl.CostEstimate(flops=80 * 10**9, bytes_accessed=80 * 2**20, transcendentals=0),
    )(*operands)


BLOCKS_G = 12
PARTS = 4
CHUNK = SEG // PARTS
PIECES = BLOCKS_G * PARTS
STAGES = 8
SLACK = 4
PATH_BLOCKS = (0, 3, 6, 9)
SMALL = 8 + TAIL
FINISH = 62


def reduce_kernel(
    xs,
    ctxs,
    hids,
    acts,
    gps,
    gbs,
    gus,
    gds,
    vecg,
    mem_part,
    sums,
    small,
    xb,
    gg,
    own,
    sent,
    tw,
    low_rx,
    high_rx,
    fin,
    acc,
    sm_tw,
    sm_rx,
    sm_tx,
    load_sem,
    tw_send,
    tw_recv,
    up_send,
    low_recv,
    high_recv,
    rung_recv,
    down_send,
    down_recv,
    fin_sem,
    sm_send,
    sm_recv,
):
    item = lax.axis_index("items")
    place = lax.axis_index("pipe")
    member = lax.rem(place, 2)
    twin = {"pipe": place + 1 - 2 * member}
    x_at, z_at = lax.rem(item, 2), item // 2
    rung = {"items": item + 1 - 2 * x_at}
    above = {"items": lax.rem(item + 2, 8)}
    below = {"items": lax.rem(item + 6, 8)}
    pair = {"items": item + 2 - 4 * lax.rem(z_at, 2)}
    far = {"items": item + 4 - 8 * (z_at // 2)}
    rounds = [rung, pair, far]
    has_above, has_below = z_at < 3, z_at > 0

    barrier = pltpu.get_barrier_semaphore()

    def greet(to):
        pl.semaphore_signal(barrier, inc=1, device_id=to, device_id_type=MESH)

    for to in (twin, rung, far):
        greet(to)

    @pl.when(has_above)
    def _():
        greet(above)

    @pl.when(has_below)
    def _():
        greet(below)

    def remote(src, dst, send, recv, to):
        return pltpu.make_async_remote_copy(
            src_ref=src, dst_ref=dst, send_sem=send, recv_sem=recv, device_id=to, device_id_type=MESH
        )

    def loads(left, right, theirs_rows, mine_rows, cols, slot):
        rows_t, col_t = theirs_rows
        rows_m, col_m = mine_rows
        return [
            pltpu.make_async_copy(
                left.at[:, rows_t, col_t], xb.at[slot, :, :, pl.ds(0, SEG)], load_sem.at[slot, 0]
            ),
            pltpu.make_async_copy(
                left.at[:, rows_m, col_m], xb.at[slot, :, :, pl.ds(SEG, SEG)], load_sem.at[slot, 1]
            ),
            pltpu.make_async_copy(right.at[:, :, cols], gg.at[slot], load_sem.at[slot, 2]),
        ]

    def aligned(start, size):
        return pl.ds(pl.multiple_of(start, SEG), size)

    def start_loads(b, slot):
        def go(left, right, pick, col):
            for copy in loads(left, right, pick(1 - member), pick(member), aligned(col * D, D), slot):
                copy.start()

        def flat(who):
            return aligned(0, SEG), aligned(who * SEG, SEG)

        @pl.when(b < 4)
        def _():
            def pick(who):
                return aligned((2 * who + b // 2) * SEG, SEG), aligned(lax.rem(b, 2) * SEG, SEG)

            go(acts, gds, pick, 0)

        @pl.when((b >= 4) & (b < 8))
        def _():
            go(hids, gus, flat, b - 4)

        @pl.when(b == 8)
        def _():
            go(ctxs, gbs, flat, 0)

        @pl.when(b >= 9)
        def _():
            go(xs, gps, flat, b - 9)

    def wait_loads(slot):
        zero = aligned(0, SEG)
        for copy in loads(xs, gds, (zero, zero), (zero, zero), aligned(0, D), slot):
            copy.wait()

    def twin_copy(b, slot):
        return remote(sent.at[slot], tw.at[b], tw_send.at[slot], tw_recv.at[b], twin)

    def piece(j):
        b, k = j // PARTS, lax.rem(j, PARTS)
        path = b == PATH_BLOCKS[0]
        for other_block in PATH_BLOCKS[1:]:
            path = path | (b == other_block)
        row = jnp.where(path, jnp.where(k < 4, k, k + 2 - PARTS // 2 - PARTS // 4), 1 + lax.rem(k // 2, 2))
        root = row + member * (3 - 2 * row)
        chain = path | (x_at == lax.rem(k + member, 2))
        away = jnp.abs(z_at - root)
        rows = pl.ds(pl.multiple_of(k * CHUNK, 16), CHUNK)
        return b, k, rows, path, root, chain, away

    def low_copy(j):
        return remote(low_rx.at[j], low_rx.at[j], up_send.at[j], low_recv.at[j], above)

    def high_copy(j):
        return remote(low_rx.at[j], high_rx.at[j], up_send.at[j], high_recv.at[j], below)

    def rung_up(j, b, rows):
        return remote(low_rx.at[j], fin.at[b, rows], up_send.at[j], rung_recv.at[j], rung)

    def rung_down(j, b, rows):
        return remote(fin.at[b, rows], fin.at[b, rows], down_send.at[2, j], rung_recv.at[j], rung)

    def below_down(j, b, rows):
        return remote(fin.at[b, rows], fin.at[b, rows], down_send.at[0, j], down_recv.at[j], below)

    def above_down(j, b, rows):
        return remote(fin.at[b, rows], fin.at[b, rows], down_send.at[1, j], down_recv.at[j], above)

    def spread(j, act):
        b, k, rows, path, root, chain, away = piece(j)

        @pl.when(chain & has_below & (z_at <= root))
        def _():
            act(below_down(j, b, rows))

        @pl.when(chain & has_above & (z_at >= root))
        def _():
            act(above_down(j, b, rows))

        @pl.when(chain & jnp.logical_not(path))
        def _():
            act(rung_down(j, b, rows))

    def gather(j):
        b, k, rows, path, root, chain, away = piece(j)
        acc[...] = own[b, rows, :] + tw[b, rows, :].astype(F32)

        @pl.when(chain & jnp.logical_not(path))
        def _():
            rung_down(j, b, rows).wait_recv()
            acc[...] += fin[b, rows, :].astype(F32)

        @pl.when(chain & has_below & (z_at <= root))
        def _():
            low_copy(j).wait_recv()
            acc[...] += low_rx[j].astype(F32)

        @pl.when(chain & has_above & (z_at >= root))
        def _():
            high_copy(j).wait_recv()
            acc[...] += high_rx[j].astype(F32)

        here = chain & (away == 0)

        @pl.when(here & jnp.logical_not(path))
        def _():
            fin[b, rows, :] = acc[...].astype(BF)
            spread(j, lambda copy: copy.start())

        @pl.when(jnp.logical_not(here & jnp.logical_not(path)))
        def _():
            low_rx[j] = acc[...].astype(BF)

        @pl.when(jnp.logical_not(chain) | (here & path))
        def _():
            rung_up(j, b, rows).start()

        @pl.when(chain & (z_at < root))
        def _():
            low_copy(j).start()

        @pl.when(chain & (z_at > root))
        def _():
            high_copy(j).start()

    def settle(j):
        b, k, rows, path, root, chain, away = piece(j)

        @pl.when(jnp.logical_not(chain) | (away == 0))
        def _():
            rung_down(j, b, rows).wait_recv()

        @pl.when(chain & (away == 0))
        def _():
            fin[b, rows, :] = (low_rx[j].astype(F32) + fin[b, rows, :].astype(F32)).astype(BF)

        @pl.when(chain & (away > 0))
        def _():
            below_down(j, b, rows).wait_recv()

        @pl.when(chain)
        def _():
            spread(j, lambda copy: copy.start())

    def stage(j, t):
        b, k, rows, path, root, chain, away = piece(j)

        @pl.when(t == jnp.where(chain, 3 - away, 0))
        def _():
            gather(j)

        later = jnp.where(path | jnp.logical_not(chain), 4 + away, 3 + away)

        @pl.when((t == later) & jnp.logical_not(chain & (away == 0) & jnp.logical_not(path)))
        def _():
            settle(j)

        @pl.when((t == STAGES - 1) & (k == PARTS - 1))
        def _():
            pltpu.make_async_copy(fin.at[b], sums.at[b], fin_sem.at[b]).start()

    def small_twin():
        return remote(sm_tx.at[0], sm_tw, sm_send.at[0], sm_recv.at[0], twin)

    def small_round(k):
        return remote(small, sm_rx.at[k], sm_send.at[k + 1], sm_recv.at[k + 1], rounds[k])

    start_loads(0, 0)

    def product(b, slot):
        both = tn(xb[slot].reshape(UNITS * SEG, D), gg[slot].reshape(UNITS * SEG, D))
        sent[slot] = both[:SEG].astype(BF)
        own[b] = both[SEG:]

    wait_loads(0)
    start_loads(1, 1)
    product(0, 0)
    ends = z_at * (3 - z_at)
    pl.semaphore_wait(barrier, 4 + ends // 2)
    twin_copy(0, 0).start()
    eight = pl.ds(pl.multiple_of((1 - member) * 8, 8), 8)
    mine8 = pl.ds(pl.multiple_of(member * 8, 8), 8)
    sm_tx[0, :8, :] = vecg[eight, :]
    sm_tx[0, 8:, :] = mem_part[...]
    small[:8, :] = vecg[mine8, :]
    small[8:, :] = mem_part[...]
    small_twin().start()

    def step(i, carry):
        now = i // PARTS
        fresh = lax.rem(i, PARTS) == 0
        slot = lax.rem(now, 2)

        @pl.when(fresh & (now < BLOCKS_G))
        def _():
            @pl.when(now > 0)
            def _():
                wait_loads(slot)

                @pl.when(now + 1 < BLOCKS_G)
                def _():
                    start_loads(now + 1, 1 - slot)

                @pl.when(now >= 2)
                def _():
                    twin_copy(now - 2, slot).wait_send()

                product(now, slot)
                twin_copy(now, slot).start()

        @pl.when(fresh & (now > 0) & (now <= BLOCKS_G))
        def _():
            twin_copy(now - 1, 0).wait_recv()

        for k in range(4):

            @pl.when(i == 4 * k + 4)
            def _():
                if k == 0:
                    small_twin().wait()
                    small[...] = small[...] + sm_tw[...]
                else:
                    small_round(k - 1).wait()
                    small[...] = small[...] + sm_rx[k - 1]
                if k < 3:
                    small_round(k).start()

        def serve(t, inner):
            j = i - PARTS - SLACK * t

            @pl.when((j >= 0) & (j < PIECES))
            def _():
                stage(j, t)

            return inner

        lax.fori_loop(0, STAGES, serve, 0)
        return carry

    lax.fori_loop(0, PARTS + PIECES + SLACK * (STAGES - 1), step, 0)

    twin_copy(0, 0).wait_send()
    twin_copy(1, 1).wait_send()

    def drain(j, carry):
        b, k, rows, path, root, chain, away = piece(j)

        @pl.when(jnp.logical_not(chain & (away == 0) & jnp.logical_not(path)))
        def _():
            low_copy(j).wait_send()

        spread(j, lambda copy: copy.wait_send())

        @pl.when(k == 0)
        def _():
            pltpu.make_async_copy(fin.at[b], sums.at[b], fin_sem.at[b]).wait()

        return carry

    lax.fori_loop(0, PIECES, drain, 0)


def reduce_grads(operands):
    shape = jax.ShapeDtypeStruct
    hbm = pl.BlockSpec(memory_space=pl.ANY)
    vmem = pl.BlockSpec(memory_space=pltpu.VMEM)
    dma = pltpu.SemaphoreType.DMA
    return pl.pallas_call(
        reduce_kernel,
        out_shape=(
            shape((BLOCKS_G, SEG, D), BF),
            shape((SMALL, D), F32),
        ),
        in_specs=[hbm] * 8 + [vmem, vmem],
        out_specs=(hbm, vmem),
        scratch_shapes=[
            pltpu.VMEM((2, UNITS, SEG, D), BF),
            pltpu.VMEM((2, UNITS, SEG, D), BF),
            pltpu.VMEM((BLOCKS_G, SEG, D), F32),
            pltpu.VMEM((2, SEG, D), BF),
            pltpu.VMEM((BLOCKS_G, SEG, D), BF),
            pltpu.VMEM((PIECES, CHUNK, D), BF),
            pltpu.VMEM((PIECES, CHUNK, D), BF),
            pltpu.VMEM((BLOCKS_G, SEG, D), BF),
            pltpu.VMEM((CHUNK, D), F32),
            pltpu.VMEM((SMALL, D), F32),
            pltpu.VMEM((3, SMALL, D), F32),
            pltpu.VMEM((1, SMALL, D), F32),
            dma((2, 3)),
            dma((2,)),
            dma((BLOCKS_G,)),
            dma((PIECES,)),
            dma((PIECES,)),
            dma((PIECES,)),
            dma((PIECES,)),
            dma((3, PIECES)),
            dma((PIECES,)),
            dma((BLOCKS_G,)),
            dma((4,)),
            dma((4,)),
        ],
        compiler_params=pltpu.CompilerParams(
            collective_id=1, has_side_effects=True, vmem_limit_bytes=62 * 2**20
        ),
        cost_estimate=pl.CostEstimate(flops=22 * 10**9, bytes_accessed=64 * 2**20, transcendentals=0),
    )(*operands)


def finish_kernel(
    counts,
    lasts,
    tops,
    backs,
    tail,
    sums,
    small,
    text,
    text_g,
    memory,
    mem_g,
    qkv_g,
    o_g,
    in_g,
    out_g,
    gains_g,
    biases_g,
):
    step = pl.program_id(0)
    place = lax.axis_index("pipe")
    count, last = counts[place], lasts[place]
    rows = tops.shape[1]
    row = lax.broadcasted_iota(jnp.int32, (rows, D), 0) + step * rows
    for k in range(2):
        limit = jnp.where(count > 1, TEXT if k == 0 else last, last if k == 0 else 0)
        text[:, k, :] = jnp.where(row < limit, tops[k].astype(F32), 0.0)
        text_g[:, k, :] = backs[k].astype(F32)
    out_g[...] = sums[:4].astype(F32)
    for j in range(4):
        in_g[:, j * D : (j + 1) * D] = sums[4 + j].astype(F32)
    o_g[...] = sums[8].astype(F32)
    for j in range(3):
        qkv_g[:, j * D : (j + 1) * D] = sums[9 + j].astype(F32)

    @pl.when(step == 0)
    def _():
        ends = tail[...].astype(F32)
        memory[:, 0, :] = jnp.where(count > 1, ends[1], ends[0])[TAIL - MEM :, :]
        width = D // 4
        for index in range(4):

            @pl.when(place == index)
            def _():
                mem_g[...] = small[SMALL - MEM :, index * width : (index + 1) * width]

        gains_g[...] = small[0]
        for index in range(5):
            biases_g[index * D : (index + 1) * D] = small[1 + index]


def finish(operands):
    shape = jax.ShapeDtypeStruct
    smem = pl.BlockSpec(memory_space=pltpu.SMEM)
    steps = 4
    row = SEG // steps

    def split(rows, cols):
        return pl.BlockSpec((rows, cols), lambda i: (i, 0))

    def whole(*size):
        return pl.BlockSpec(size, lambda i: (0,) * len(size))

    pair = pl.BlockSpec((2, row, D), lambda i: (0, i, 0))
    pair_out = pl.BlockSpec((row, 2, D), lambda i: (i, 0, 0))
    out_spec = pl.BlockSpec((4, row, D), lambda i: (0, i, 0))
    grads = [split(row, 3 * D), split(row, D), split(row, FF), out_spec]
    counts, lasts, tops, backs, *rest = operands
    return pl.pallas_call(
        finish_kernel,
        grid=(steps,),
        out_shape=(
            shape((TEXT, 2, D), F32),
            shape((TEXT, 2, D), F32),
            shape((MEM, 1, D), F32),
            shape((MEM, D // 4), F32),
            shape((SEG, 3 * D), F32),
            shape((SEG, D), F32),
            shape((SEG, FF), F32),
            shape((4, SEG, D), F32),
            shape((D,), F32),
            shape((5 * D,), F32),
        ),
        in_specs=[
            smem,
            smem,
            pair,
            pair,
            pl.BlockSpec((2, TAIL, D), lambda i: (0, SEG // TAIL - 1, 0)),
            pl.BlockSpec((BLOCKS_G, row, D), lambda i: (0, i, 0)),
            whole(SMALL, D),
        ],
        out_specs=(
            pair_out,
            pair_out,
            whole(MEM, 1, D),
            whole(MEM, D // 4),
            *grads,
            whole(D),
            whole(5 * D),
        ),
        compiler_params=pltpu.CompilerParams(vmem_limit_bytes=FINISH * 2**20),
    )(counts, lasts, tops, backs, tops, *rest)


def from_partner(x, axis, bit):
    return lax.ppermute(x, axis, [(i, i ^ 1 << bit) for i in range(lax.axis_size(axis))])


def over_rows(left, right):
    return lax.dot_general(
        left, right, (((0, 1), (0, 1)), ((), ())), preferred_element_type=F32
    )


def sum_grads(member, operands):
    xs, ctxs, hids, acts, gps, gbs, gus, gds, vecg, memg = operands
    def halves(left, right):
        size = left.shape[-1] // 2
        mine = lax.dynamic_slice_in_dim(left, member * size, size, 2)
        theirs = lax.dynamic_slice_in_dim(left, (1 - member) * size, size, 2)
        return over_rows(mine, right), over_rows(theirs, right).astype(BF)

    parts = [halves(xs, gps), halves(ctxs, gbs), halves(hids, gus)]
    blocks = acts.reshape(UNITS, 4, SEG, D)
    mine = lax.dynamic_slice_in_dim(blocks, member * 2, 2, 1)
    theirs = lax.dynamic_slice_in_dim(blocks, (1 - member) * 2, 2, 1)
    parts.append(
        (
            jnp.concatenate([over_rows(mine[:, i], gds) for i in range(2)], 0),
            jnp.concatenate([over_rows(theirs[:, i], gds) for i in range(2)], 0).astype(BF),
        )
    )
    sums = [kept + from_partner(sent, "pipe", 0).astype(F32) for kept, sent in parts]
    vec_mine = lax.dynamic_slice_in_dim(vecg, member * 8, 8, 0)
    vec_theirs = lax.dynamic_slice_in_dim(vecg, (1 - member) * 8, 8, 0)
    mine_small = jnp.concatenate([vec_mine, memg], 0)
    small = mine_small + from_partner(jnp.concatenate([vec_theirs, memg], 0), "pipe", 0)
    *grads, small = lax.psum((*sums, small), "items")
    qkv, out_proj, up, down = grads
    columns = [up[:, j * D : (j + 1) * D] for j in range(4)] + [out_proj]
    columns += [qkv[:, j * D : (j + 1) * D] for j in range(3)]
    return jnp.concatenate([down.reshape(4, SEG, D), jnp.stack(columns)], 0), small


def per_device(
    text_in,
    memory,
    w_qkv,
    w_o,
    w_in,
    w_out,
    gains,
    biases,
    counts,
    last_lengths,
    text_cot,
    memory_cot,
):
    member = lax.axis_index("pipe") % 2
    pad = ((0, 0), (0, SEG - TEXT), (0, 0))
    x_own = jnp.pad(text_in[0], pad)
    c_own = jnp.pad(text_cot[0], pad)
    mcot = memory_cot.astype(F32).transpose(1, 0, 2)
    vec_own = jnp.concatenate([gains, biases, jnp.zeros(2 * D, gains.dtype)]).reshape(8, D).astype(F32)
    xs, ctxs, hids, acts, own_top, gds, gus, gbs, gps, own_back, _, vecg, memg = relay(
        (x_own, c_own, memory, mcot, counts, last_lengths, w_qkv, w_o, w_in, w_out, vec_own)
    )
    sum_all = reduce_grads if lax.axis_size("items") == 8 else functools.partial(sum_grads, member)
    sums = sum_all((xs, ctxs, hids, acts, gps, gbs, gus, gds, vecg, memg))
    text, text_grad, last_memory, memory_grad, *grads, down, gains_grad, biases_grad = finish(
        (counts, last_lengths, own_top, own_back, *sums)
    )
    return (
        text.transpose(1, 0, 2)[None],
        last_memory.transpose(1, 0, 2),
        text_grad.transpose(1, 0, 2)[None],
        memory_grad,
        *grads,
        down.reshape(FF // 2, D),
        gains_grad,
        biases_grad,
    )


def solution(mesh):
    placed = (
        P(("items", "pipe"), None, None, None),
        P(None, "pipe"),
        P("pipe", None),
        P("pipe", None),
        P("pipe", None),
        P("pipe", None),
        P("pipe"),
        P("pipe"),
        P("items"),
        P("items"),
        P(("items", "pipe"), None, None, None),
        P(("items", "pipe"), None, None),
    )
    return jax.shard_map(
        per_device,
        mesh=mesh,
        in_specs=placed,
        out_specs=(
            P(("items", "pipe"), None, None, None),
            P(("items", "pipe"), None, None),
            P(("items", "pipe"), None, None, None),
            P(None, "pipe"),
            P("pipe", None),
            P("pipe", None),
            P("pipe", None),
            P("pipe", None),
            P("pipe"),
            P("pipe"),
        ),
        check_vma=False,
    )
```
